128 devices in a mesh: segment: 2 (over x_lo), dp: 32 (over z, y, core), mp: 2 (over x_hi).
Axes of the slice: x: 4 (x_hi: 2, x_lo: 2; x = x_hi * 2 + x_lo), y: 4, z: 4, core: 2. Of those that a mesh axis runs over, the one named last changes fastest.
Arguments:
- segment_inputs: bfloat16 [2, 16384, 4096], P('segment', 'dp', 'mp'), may hold values from -68 to 68
- cotangent: bfloat16 [16384, 4096], P('dp', 'mp'), may hold values from -6 to 6
- report_lengths: int32 [128], P('dp'), may hold values from 64 to 128
- norm_gain: float32 [2, 4096], P('segment', 'mp'), may hold values from 0.25 to 1.75
- attn_gate: float32 [2], P('segment'), may hold values from 0.3 to 1.5
- w_query: bfloat16 [2, 4096, 1024], P('segment', 'mp', 'dp'), may hold values from -0.09375 to 0.09375
- w_out: bfloat16 [2, 1024, 4096], P('segment', 'dp', 'mp'), may hold values from -0.1875 to 0.1875
- w_key: bfloat16 [2, 1536, 1024], P('segment', None, 'mp'), may hold values from -0.15625 to 0.15625
- w_value: bfloat16 [2, 1536, 1024], P('segment', None, 'mp'), may hold values from -0.15625 to 0.15625
- tiles: bfloat16 [128, 64, 1536], P('dp')
- tile_counts: int32 [32, 4], P('dp'), may hold values from 1 to 64, 160 in all within a row
- lat_query: bfloat16 [32, 1536], replicated
- request_source: int32 [128, 6, 1], replicated, may hold values from 0 to 31; in each aligned block of 24 rows (0 to 23, 24 to 47, ..., all dimensions but the last counted through in order) at most 2 rows name the same one
- request_slide: int32 [128, 6], replicated, may hold values from 0 to 3
- cross_pattern: int32 [128, 4, 6], P('dp'), may hold values from 0 to 1, as said below
Outputs:
- grad_inputs: bfloat16 [2, 16384, 4096], P('segment', 'dp', 'mp')
- latent_grad: float32 [128, 192, 1536], P('dp', ('segment', 'mp'))
The draws below stay inside these ranges and needn't reach their ends.
Inputs may be any that keep to these rules, and one draw needn't show every extreme that they name: `request_source`: among the 24 requests of one dp index's reports, no encoder shard is named more than 2 times, a bound that some block reaches. `cross_pattern`: every query block of every report attends to at least one slide.
All inputs are finite; a program needn't handle non-finite values.
Results may differ from the reference program's by a relative error of at most 0.022.
The reference program's roundings to bfloat16 on the way count: a program that leaves them out, or rounds other values in their place, can miss the bound.
Values may be sent and summed in bfloat16 or wider, within the bound.
No kernel may reach another device: no remote copies, remote signals or barrier semaphores. Data moves between devices by JAX's collectives and lax.ppermute only.
A program may use at most 192 MiB of HBM per device.

```python
import math
import jax
import jax.numpy as jnp
import numpy as np
from jax import lax

MODEL_WIDTH = 4096
E = 1536
HEAD = 128
INNER = 1024
LAT = 32
SPR = 6
MAXT = 64
SLIDE_DEV = 4
L = 128
QBLK = 32
REP_DEV = 4
NQB = 4
REPORTS = 128
TOKENS = 16384
SLIDES = 128
CAP = 2
N_SEGMENT = 2
N_DP = 32
N_MP = 2


def shared_queries(key):
    return jax.random.normal(jax.random.fold_in(key, 99), (LAT, E), jnp.float32)


def draw_segment_inputs(key, part):
    key = jax.random.fold_in(key, 13)
    first = jax.random.fold_in(key, 0)
    place = jnp.arange(MODEL_WIDTH).astype(jnp.float32) / (MODEL_WIDTH - 1)
    noise = jnp.clip(jax.random.normal(first, (N_SEGMENT, TOKENS, MODEL_WIDTH), jnp.float32), -6.0, 6.0)
    ramp = jnp.exp(1.791759 * place)
    return (noise * ramp[None, None, :]).astype(jnp.bfloat16)


def draw_lat_query(key, part):
    base = shared_queries(key)
    return base.astype(jnp.bfloat16)


def draw_tiles(key, part):
    key = jax.random.fold_in(key, 7)
    first = jax.random.fold_in(key, 0)
    noise = jax.random.normal(first, (SLIDES, MAXT, E), jnp.float32)
    return jnp.clip(noise, -6.0, 6.0).astype(jnp.bfloat16)


def draw_cross_pattern(key, part):
    key = jax.random.fold_in(key, 11)
    first, second = jax.random.split(key)
    chosen = jax.random.randint(first, (REPORTS, NQB, SPR), 0, 2)
    single = jax.random.randint(second, (REPORTS, NQB), 0, SPR)
    onehot = (jnp.arange(SPR)[None, None, :] == single[:, :, None]).astype(jnp.int32)
    return jnp.maximum(chosen, onehot).astype(jnp.int32)


def with_ends(entries, key, smallest, high):
    index_at = [jax.random.randint(jax.random.fold_in(key, axis), (), 0, length) for axis, length in enumerate(entries.shape)]
    widest = entries.shape.index(max(entries.shape))
    next_to = index_at[:widest] + [(index_at[widest] + 1) % entries.shape[widest]] + index_at[widest + 1:]
    return entries.at[tuple(index_at)].set(smallest).at[tuple(next_to)].set(high)


def level_of(stream_key, dims, cuts, smallest, top_value):
    level, own = 1.0, jax.random.fold_in(stream_key, 6)
    for dim, blocks in cuts:
        draws = jnp.exp(jax.random.uniform(jax.random.fold_in(own, dim), (blocks,), jnp.float32, smallest / len(cuts), top_value / len(cuts)))
        level = level * jnp.repeat(draws, dims[dim] // blocks).reshape([-1 if axis == dim else 1 for axis in range(len(dims))])
    return level


def profile(number_of, total, reach, lean):
    portions = [(1 << 20) // math.isqrt(grade ** lean) + 1 for grade in range(2, number_of + 1)]
    spare, given = total - reach - (number_of - 1), [1] * (number_of - 1)
    while spare > 0:
        free = [i for i in range(number_of - 1) if given[i] < reach]
        pool, remaining = sum([portions[i] for i in free]), spare
        for i in free:
            more = min(reach - given[i], max(1, remaining * portions[i] // pool), spare)
            given[i] = given[i] + more
            spare = spare - more
    return np.array([reach] + given)


def uneven_parts(key, number_of, total, bound, slope):
    if number_of == 2:
        one = jax.random.randint(key, (), max(1, total - bound), min(bound, total - 1) + 1)
        return jnp.stack([one, total - one])
    tallies = jnp.asarray(profile(number_of, total, bound, slope), jnp.int32)
    couples = (number_of - 1) // 2
    source_of, taker = tallies[1:1 + 2 * couples:2], tallies[2:2 + 2 * couples:2]
    room = jnp.minimum(source_of - 1, bound - taker)
    shifted = jax.random.randint(jax.random.fold_in(key, 1), (couples,), 0, 1 << 20) % (room + 1)
    tallies = tallies.at[1:1 + 2 * couples:2].set(source_of - shifted).at[2:2 + 2 * couples:2].set(taker + shifted)
    return tallies[jax.random.permutation(jax.random.fold_in(key, 2), number_of)]


def deal_out(own_key, own, number, rows, number_of, top, bound, lean):
    sequence = jax.random.permutation(own_key, number_of)
    crowded, common = portions_of(number_of, rows * top, bound, lean, True), portions_of(number_of, rows * top, bound, lean, False)
    places = jnp.arange(number_of)

    def named(lengths, rotation):
        used = int((lengths > 0).sum())
        fixed = max(1, used // 4)
        shifted = fixed + (places - fixed + rotation * (used - fixed)) % max(1, number_of - fixed)
        return jnp.zeros((number_of,), jnp.int32).at[sequence[jnp.where(places < fixed, places, shifted)]].set(jnp.asarray(lengths, jnp.int32))

    lengths = jnp.where(number % 4 == 0, named(crowded, number // 4), named(common, number - number // 4 - 1))
    mixed = jax.random.permutation(jax.random.fold_in(own, 3), number_of)
    donor, receiver = mixed[0:number_of // 2 * 2:2], mixed[1:number_of // 2 * 2:2]
    margin = jnp.minimum(lengths[donor] - 1, bound - lengths[receiver]) // 2
    margin = jnp.where((donor == sequence[0]) | (receiver == sequence[0]) | (lengths[receiver] == 0), 0, jnp.maximum(margin, 0))
    shifted = jax.random.randint(jax.random.fold_in(own, 4), (number_of // 2,), 0, 1 << 20) % (margin + 1)
    lengths = lengths.at[donor].add(-shifted).at[receiver].add(shifted)
    members = jnp.searchsorted(jnp.cumsum(lengths), jnp.arange(rows * top), side="right").astype(jnp.int32)
    grid = members.reshape(top, rows).T
    grid = grid[jax.random.permutation(jax.random.fold_in(own, 1), rows)]
    rotation = jax.random.randint(jax.random.fold_in(own, 2), (rows, 1), 0, top)
    return jnp.take_along_axis(grid, (jnp.arange(top)[None, :] + rotation) % top, axis=1)


def portions_of(count, total, most, lean, full):
    loads = [(1 << 20) // math.isqrt(rank ** lean) + 1 for rank in range(1, count + 1)]
    largest = most if full else min(most, max(-(-total // count), total * loads[0] // sum(loads)))
    least = 1 if total - largest >= count - 1 else 0
    given, rest = [largest] + [least] * (count - 1), total - largest - least * (count - 1)
    while rest > 0:
        movable = [i for i in range(1, count) if given[i] < largest] or [i for i in range(1, count) if given[i] < most]
        mass, remaining = sum([loads[i] for i in movable]), rest
        for i in movable:
            more = min(most - given[i], max(1, remaining * loads[i] // mass), rest)
            given[i] = given[i] + more
            rest = rest - more
    return np.array(given)


def gaussian(stream_key, shape, scale, bound, shards=(), held_as=jnp.bfloat16):
    level = level_of(stream_key, shape, shards, -0.22, 0.18) if shards else 1.0
    entries = jax.random.normal(stream_key, shape, jnp.float32) * scale * level
    return jnp.minimum(jnp.maximum(entries, -bound), bound).astype(held_as)


def setup_inputs(seed: int = 0) -> dict:
    key_list = jax.random.split(jax.random.key(seed), 16)
    segment_inputs = draw_segment_inputs(jax.random.fold_in(key_list[15], 71), 0)
    cotangent = gaussian(key_list[1], (TOKENS, MODEL_WIDTH), 1.0, 6.0, ((0, 32), (1, 2)))
    report_lengths = with_ends(jax.random.randint(key_list[2], (REPORTS,), L // 2, L + 1), jax.random.fold_in(key_list[2], 1), L // 2, L).astype(jnp.int32)
    norm_gain = jnp.clip(1.0 + 0.15 * jax.random.normal(key_list[3], (N_SEGMENT, MODEL_WIDTH), jnp.float32), 0.25, 1.75)
    attn_gate = jnp.clip(0.3 + 1.2 * jax.random.uniform(key_list[4], (N_SEGMENT,), jnp.float32) ** level_of(key_list[4], (N_SEGMENT,), ((0, 2),), -0.2, 0.2), 0.3, 1.5)
    w_query = gaussian(key_list[5], (N_SEGMENT, MODEL_WIDTH, INNER), MODEL_WIDTH ** -0.5, 0.09375, ((0, 2), (1, 2), (2, 32)))
    w_out = gaussian(key_list[6], (N_SEGMENT, INNER, MODEL_WIDTH), INNER ** -0.5, 0.1875, ((0, 2), (1, 32), (2, 2)))
    w_key = gaussian(key_list[7], (N_SEGMENT, E, INNER), E ** -0.5, 0.15625, ((0, 2), (2, 2)))
    w_value = gaussian(key_list[8], (N_SEGMENT, E, INNER), E ** -0.5, 0.15625, ((0, 2), (2, 2)))
    tiles = draw_tiles(jax.random.fold_in(key_list[15], 71), 0)
    tile_counts = jax.vmap(lambda own: uneven_parts(own, SLIDE_DEV, SLIDE_DEV * MAXT * 5 // 8, MAXT, 2))(jax.random.split(key_list[10], N_DP)).reshape((N_DP, SLIDE_DEV)).astype(jnp.int32)
    lat_query = draw_lat_query(jax.random.fold_in(key_list[15], 71), 0)
    request_source_keys = jax.random.split(jax.random.fold_in(key_list[12], 1), REPORTS * SPR // (REP_DEV * SPR))
    request_source_turns = jax.random.permutation(jax.random.fold_in(key_list[12], 3), REPORTS * SPR // (REP_DEV * SPR))
    request_source = jax.vmap(lambda own, number: deal_out(jax.random.fold_in(key_list[12], 2), own, number, REP_DEV * SPR, N_DP, 1, CAP, 1))(request_source_keys, request_source_turns).reshape((REPORTS, SPR, 1))
    request_slide = with_ends(jax.random.randint(key_list[13], (REPORTS, SPR), 0, SLIDE_DEV), jax.random.fold_in(key_list[13], 1), 0, SLIDE_DEV - 1).astype(jnp.int32)
    cross_pattern = draw_cross_pattern(jax.random.fold_in(key_list[15], 71), 0)
    return dict(segment_inputs=segment_inputs, cotangent=cotangent, report_lengths=report_lengths, norm_gain=norm_gain, attn_gate=attn_gate, w_query=w_query, w_out=w_out, w_key=w_key, w_value=w_value, tiles=tiles, tile_counts=tile_counts, lat_query=lat_query, request_source=request_source, request_slide=request_slide, cross_pattern=cross_pattern)


def round_keep(values):
    return lax.optimization_barrier(values.astype(jnp.bfloat16)).astype(jnp.float32)

def pool_slides(slides, counts, queries):
    heads = E // HEAD
    number = slides.shape[0]
    slots = slides.shape[1]
    keys = slides.astype(jnp.float32).reshape(number, slots, heads, HEAD)
    qry = queries.astype(jnp.float32).reshape(LAT, heads, HEAD)
    scores = jnp.einsum('lhd,nthd->nhlt', qry, keys) * HEAD ** (-0.5)
    live = jnp.arange(slots)[None, None, None, :] < counts[:, None, None, None]
    scores = jnp.where(live, scores, -1e+30)
    weights = round_keep(jax.nn.softmax(scores, axis=-1))
    pooled = jnp.einsum('nhlt,nthd->nlhd', weights, keys)
    return (queries.astype(jnp.float32)[None] + pooled.reshape(number, LAT, E)).astype(jnp.bfloat16)

def reference(segment_inputs, cotangent, report_lengths, norm_gain, attn_gate, w_query, w_out, w_key, w_value, tiles, tile_counts, lat_query, request_source, request_slide, cross_pattern):
    scale = HEAD ** (-0.5)
    heads = INNER // HEAD
    row_count = request_source[:, :, 0].reshape(-1) * SLIDE_DEV + request_slide.reshape(-1)
    chosen = tiles[row_count]
    counts = tile_counts.reshape(-1)[row_count]
    latents = pool_slides(chosen, counts, lat_query).reshape(REPORTS, SPR * LAT, E)
    position = jnp.arange(TOKENS)
    report = position // L
    qblock = position % L // QBLK
    pattern_tok = cross_pattern[report, qblock]
    key_slide = jnp.arange(SPR * LAT) // LAT
    allowed = (pattern_tok[:, key_slide] == 1).reshape(REPORTS, L, SPR * LAT)
    live_len = position % L < report_lengths[report]
    upstream = jnp.where(live_len[:, None], cotangent, jnp.zeros((), jnp.bfloat16)).astype(jnp.bfloat16)
    latent_grad = jnp.zeros((REPORTS, SPR * LAT, E), jnp.float32)
    results = []
    lat32 = latents.astype(jnp.float32)
    quarter = MODEL_WIDTH // N_MP
    for section in range(N_SEGMENT - 1, -1, -1):
        hidden_state = segment_inputs[section].astype(jnp.float32)
        inverse_root_mean = lax.rsqrt(lax.optimization_barrier(jnp.sum(hidden_state * hidden_state, axis=1)) / MODEL_WIDTH + 1e-05)
        normalized_input = hidden_state * inverse_root_mean[:, None]
        scale_factor = norm_gain[section]
        normalized_rows = (normalized_input * scale_factor).astype(jnp.bfloat16)
        queries = jnp.dot(normalized_rows, w_query[section], preferred_element_type=jnp.float32)
        queries_b = queries.astype(jnp.bfloat16)
        keys = jnp.einsum('rke,ej->rkj', lat32, w_key[section].astype(jnp.float32)).astype(jnp.bfloat16)
        vals = jnp.einsum('rke,ej->rkj', lat32, w_value[section].astype(jnp.float32)).astype(jnp.bfloat16)
        qh = queries_b.astype(jnp.float32).reshape(REPORTS, L, heads, HEAD)
        kh = keys.astype(jnp.float32).reshape(REPORTS, SPR * LAT, heads, HEAD)
        vh = vals.astype(jnp.float32).reshape(REPORTS, SPR * LAT, heads, HEAD)
        scores = jnp.einsum('rthd,rkhd->rhtk', qh, kh) * scale
        scores = jnp.where(allowed[:, None], scores, -1e+30)
        probs = jax.nn.softmax(scores, axis=-1)
        probs_b = round_keep(probs)
        wout = w_out[section].astype(jnp.float32).reshape(INNER, N_MP, quarter)
        upper = upstream.astype(jnp.float32).reshape(TOKENS, N_MP, quarter)
        parts = jnp.einsum('tmd,imd->mti', upper, wout)
        out_sum = lax.optimization_barrier(jnp.sum(round_keep(parts), axis=0))
        out_grad = (jnp.tanh(attn_gate[section]) * out_sum).astype(jnp.bfloat16)
        og = out_grad.astype(jnp.float32).reshape(REPORTS, L, heads, HEAD)
        dprob = jnp.einsum('rthd,rkhd->rhtk', og, vh)
        rowdot = lax.optimization_barrier(jnp.sum(probs * dprob, axis=-1, keepdims=True))
        dscore = round_keep(probs * (dprob - rowdot))
        dquery = (jnp.einsum('rhtk,rkhd->rthd', dscore, kh) * scale).astype(jnp.bfloat16).reshape(TOKENS, INNER)
        dkey = (jnp.einsum('rhtk,rthd->rkhd', dscore, qh) * scale).reshape(REPORTS, SPR * LAT, INNER).astype(jnp.bfloat16)
        dval = jnp.einsum('rhtk,rthd->rkhd', probs_b, og).reshape(REPORTS, SPR * LAT, INNER).astype(jnp.bfloat16)
        norm_statistic = lax.optimization_barrier(jnp.sum(queries * dquery.astype(jnp.float32), axis=1))
        normalized_gradient = jnp.dot(dquery, w_query[section].T, preferred_element_type=jnp.float32)
        input_gradient = inverse_root_mean[:, None] * (scale_factor * normalized_gradient - normalized_input * (norm_statistic / MODEL_WIDTH)[:, None])
        grad = (upstream.astype(jnp.float32) + input_gradient).astype(jnp.bfloat16)
        results.append(grad)
        latent_grad = latent_grad + jnp.einsum('rkj,ej->rke', dkey.astype(jnp.float32), w_key[section].astype(jnp.float32))
        latent_grad = latent_grad + jnp.einsum('rkj,ej->rke', dval.astype(jnp.float32), w_value[section].astype(jnp.float32))
        upstream = grad
    grad_inputs = jnp.stack(results[::-1], axis=0)
    return (grad_inputs, latent_grad)
```

```python
import functools

import jax
import jax.numpy as jnp
from jax import lax
from jax.experimental import pallas as pl
from jax.experimental.pallas import tpu as pltpu
from jax.sharding import Mesh
from jax.sharding import PartitionSpec as P

MODEL_WIDTH = 4096
E = 1536
HEAD = 128
LAT = 32
SPR = 6
L = 128
QBLK = 32
MAXT = 64
QUARTER = E // 4
SCALE = HEAD ** (-0.5)
DP = ("z", "y", "core")
X = ("segment", "mp")
BF = jnp.bfloat16
F32 = jnp.float32
LIMIT = 48 * 1024 * 1024
NT = (((1,), (1,)), ((), ()))
NN = (((1,), (0,)), ((), ()))
TN = (((0,), (0,)), ((), ()))

SWAP_MP = [(0, 1), (1, 0), (2, 3), (3, 2)]
LAST_TO_SAME = [(2, 0), (3, 1)]
LAST_TO_CROSS = [(2, 1), (3, 0)]
LAST_SWAP = [(2, 3), (3, 2)]
FIRST_TO_SAME = [(0, 2), (1, 3)]
FIRST_TO_CROSS = [(0, 3), (1, 2)]
FIRST_SWAP = [(0, 1), (1, 0)]
AT_X = (0, 2, 1, 3)


def x_perm(k):
    return [(AT_X[x], AT_X[(x + k) % 4]) for x in range(4)]


def yz_perm(stage, k):
    pairs = []
    for z in range(4):
        for y in range(4):
            for core in range(2):
                along_y = (core == 0) == (stage == 1)
                to_z = z if along_y else (z + k) % 4
                to_y = (y + k) % 4 if along_y else y
                pairs.append(((z * 4 + y) * 2 + core, (to_z * 4 + to_y) * 2 + core))
    return pairs


def dot(a, b, dims):
    return lax.dot_general(a, b, dims, preferred_element_type=F32)


def params(**kwargs):
    return pltpu.CompilerParams(vmem_limit_bytes=LIMIT, **kwargs)


def whole(shape):
    return pl.BlockSpec(shape, lambda *_: (0,) * len(shape))


SMEM = pl.BlockSpec(memory_space=pltpu.SMEM)
ANY = pl.BlockSpec(memory_space=pl.ANY)


def pool_kernel(which, counts, tiles, queries, out):
    for slide in range(4):
        live = lax.broadcasted_iota(jnp.int32, (LAT, MAXT), 1) < counts[slide]
        for head in range(QUARTER // HEAD):
            cols = slice(head * HEAD, (head + 1) * HEAD)
            tile = tiles[slide, :, cols]
            query = queries[:, cols]
            scores = dot(query, tile, NT) * SCALE
            scores = jnp.where(live, scores, -1e30)
            exps = jnp.exp(scores - jnp.max(scores, axis=1, keepdims=True))
            weights = (exps / jnp.sum(exps, axis=1, keepdims=True)).astype(BF)
            pooled = dot(weights, tile, NN)
            out[slide * LAT : (slide + 1) * LAT, cols] = (query.astype(F32) + pooled).astype(BF)


def pool(which, counts, tiles, queries):
    return pl.pallas_call(
        pool_kernel,
        grid_spec=pltpu.PrefetchScalarGridSpec(
            num_scalar_prefetch=2,
            grid=(1,),
            in_specs=[
                pl.BlockSpec((4, MAXT, QUARTER), lambda i, which, counts: (0, 0, which[0])),
                pl.BlockSpec((LAT, QUARTER), lambda i, which, counts: (0, which[0])),
            ],
            out_specs=pl.BlockSpec((4 * LAT, QUARTER), lambda i, which, counts: (0, 0)),
        ),
        out_shape=jax.ShapeDtypeStruct((4 * LAT, QUARTER), BF),
        compiler_params=params(),
    )(which, counts, tiles, queries)


def gather_dp(block):
    parts = [block] + [lax.ppermute(block, DP, yz_perm(1, k)) for k in (1, 2, 3)]
    bundle = jnp.stack(parts)
    mine = [bundle] + [lax.ppermute(bundle, DP, yz_perm(2, k)) for k in (1, 2, 3)]
    others = [lax.ppermute(b, "core", [(0, 1), (1, 0)]) for b in mine]
    return mine + others


def places():
    z, y, core = (lax.axis_index(name) for name in DP)
    table = []
    for a in range(8):
        c = core if a < 4 else 1 - core
        for k in range(4):
            j = a % 4
            at_z = lax.rem(z - jnp.where(c == 0, j, k) + 4, 4)
            at_y = lax.rem(y - jnp.where(c == 0, k, j) + 4, 4)
            table.append((at_z * 4 + at_y) * 2 + c)
    return jnp.stack(table).astype(jnp.int32)


def assemble_kernel(kinds, rows, *refs):
    ins, outs, sems = refs[:8], refs[8 : 8 + kinds], refs[8 + kinds]
    copies = []
    for a in range(8):
        for k in range(4):
            at = pl.multiple_of(rows[a * 4 + k], 32)
            for kind in range(kinds):
                copies.append(
                    pltpu.make_async_copy(
                        ins[a].at[k, pl.ds(kind * 32, 32)],
                        outs[kind].at[pl.ds(at, 32)],
                        sems.at[(a * 4 + k) * kinds + kind],
                    )
                )
    for copy in copies:
        copy.start()
    for copy in copies:
        copy.wait()


def assemble(rows, blocks, kinds):
    width = blocks[0].shape[2]
    out = jax.ShapeDtypeStruct((1024, width), BF)
    return pl.pallas_call(
        functools.partial(assemble_kernel, kinds),
        in_specs=[SMEM] + [ANY] * 8,
        out_specs=[ANY] * kinds,
        out_shape=[out] * kinds,
        scratch_shapes=[pltpu.SemaphoreType.DMA((32 * kinds,))],
        compiler_params=params(),
    )(rows, *blocks)


def select_kernel(wanted, array, block, slide, *refs):
    ins, out, sems = refs[:8], refs[8], refs[9]
    for i in range(wanted):
        for a in range(8):

            @pl.when(array[i] == a)
            def _():
                pltpu.make_async_copy(
                    ins[a].at[block[i], pl.ds(pl.multiple_of(slide[i] * LAT, LAT), LAT)],
                    out.at[pl.ds(i * LAT, LAT)],
                    sems.at[i],
                ).start()

    for i in range(wanted):
        pltpu.make_async_copy(
            ins[0].at[0, pl.ds(0, LAT)], out.at[pl.ds(i * LAT, LAT)], sems.at[i]
        ).wait()


def select(array, block, slide, blocks):
    wanted = array.shape[0]
    return pl.pallas_call(
        functools.partial(select_kernel, wanted),
        in_specs=[SMEM] * 3 + [ANY] * 8,
        out_specs=ANY,
        out_shape=jax.ShapeDtypeStruct((wanted * LAT, QUARTER), BF),
        scratch_shapes=[pltpu.SemaphoreType.DMA((wanted,))],
        compiler_params=params(),
    )(array, block, slide, *blocks)


def front_kernel(h, rinv, gain, cot, live, wq, wo, q_own, q_send, o_own, o_send, q_acc, o_acc):
    step = pl.program_id(0)
    normed = (h[...].astype(F32) * rinv[...] * gain[...]).astype(BF)
    upstream = jnp.where(live[...] > 0, cot[...], jnp.zeros((), BF))
    q_term = dot(normed, wq[...], NT)
    o_term = dot(upstream, wo[...], NT)

    @pl.when(step == 0)
    def _():
        q_acc[...] = q_term
        o_acc[...] = o_term

    @pl.when(step > 0)
    def _():
        q_acc[...] += q_term
        o_acc[...] += o_term

    @pl.when(step == pl.num_programs(0) - 1)
    def _():
        half = q_own.shape[1]
        q_own[...] = q_acc[:, :half]
        q_send[...] = q_acc[:, half:].astype(BF)
        o_own[...] = o_acc[:, :half].astype(BF)
        o_send[...] = o_acc[:, half:].astype(BF)


TILE = 512


def front(h, rinv, gain, cot, live, wq, wo):
    tokens, width = h.shape
    inner = wq.shape[0]
    half = inner // 2
    act = pl.BlockSpec((tokens, TILE), lambda i: (0, i))
    weight = pl.BlockSpec((inner, TILE), lambda i: (0, i))
    column = whole((tokens, 1))
    result = whole((tokens, half))
    return pl.pallas_call(
        front_kernel,
        grid=(width // TILE,),
        in_specs=[act, column, pl.BlockSpec((1, TILE), lambda i: (0, i)), act, column, weight, weight],
        out_specs=[result] * 4,
        out_shape=[jax.ShapeDtypeStruct((tokens, half), t) for t in (F32, BF, BF, BF)],
        scratch_shapes=[pltpu.VMEM((tokens, inner), F32)] * 2,
        compiler_params=params(),
        cost_estimate=pl.CostEstimate(
            flops=4 * tokens * width * inner, bytes_accessed=14 << 20, transcendentals=0
        ),
    )(h, rinv, gain, cot, live, wq, wo)


def attend_kernel(slot, gate, q_own, q_got, o_own, o_got, keys, vals, allowed, dq_out, dkv_out):
    report = pl.program_id(0)
    rows = pl.ds(pl.multiple_of(report * L, L), L)
    local = q_own.shape[1]
    mask = allowed[...] > 0
    stat = jnp.zeros((L, HEAD), F32)
    for head in range(local // HEAD):
        cols = slice(head * HEAD, (head + 1) * HEAD)
        q = q_own[:, cols] + q_got[:, cols].astype(F32)
        qb = q.astype(BF)
        og = (gate[0] * (o_own[:, cols].astype(F32) + o_got[:, cols].astype(F32))).astype(BF)
        key = keys[:, cols]
        val = vals[:, cols]
        scores = jnp.where(mask, dot(qb, key, NT) * SCALE, -1e30)
        exps = jnp.exp(scores - jnp.max(scores, axis=1, keepdims=True))
        probs = exps / jnp.sum(exps, axis=1, keepdims=True)
        dprob = dot(og, val, NT)
        rowdot = jnp.sum(probs * dprob, axis=1, keepdims=True)
        dscore = (probs * (dprob - rowdot)).astype(BF)
        dq = (dot(dscore, key, NN) * SCALE).astype(BF)
        dkey = (dot(dscore, qb, TN) * SCALE).astype(BF)
        dval = dot(probs.astype(BF), og, TN).astype(BF)
        dq_out[rows, cols] = dq
        stat += q * dq.astype(F32)
        for part in range(4):
            into = pl.ds(pl.multiple_of(report * 48, 16), 48)
            dkv_out[slot[part], into, cols] = dkey[part * 48 : (part + 1) * 48]
            dkv_out[slot[part], into, slice(local + head * HEAD, local + (head + 1) * HEAD)] = dval[
                part * 48 : (part + 1) * 48
            ]
    total = jnp.sum(stat.T, axis=0, keepdims=True)
    high = total.astype(BF)
    rest = total - high.astype(F32)
    low = rest.astype(BF)
    lower = (rest - low.astype(F32)).astype(BF)
    zero = jnp.zeros((13, L), F32)
    extra = jnp.concatenate([high.astype(F32), low.astype(F32), lower.astype(F32), zero], axis=0)
    tokens = q_own.shape[0] * pl.num_programs(0)
    dq_out[4 * L : 4 * L + 16, rows] = extra.astype(BF)


def attend(slot, gate, q_own, q_got, o_own, o_got, keys, vals, allowed):
    tokens, local = q_own.shape
    reports = tokens // L
    span = keys.shape[0] // reports
    token = pl.BlockSpec((L, local), lambda i: (i, 0))
    latent = pl.BlockSpec((span, local), lambda i: (i, 0))
    return pl.pallas_call(
        attend_kernel,
        grid=(reports,),
        in_specs=[SMEM, SMEM, token, token, token, token, latent, latent]
        + [pl.BlockSpec((L, span), lambda i: (i, 0))],
        out_specs=[whole((tokens + 16, local)), whole((4, reports * 48, 2 * local))],
        out_shape=[
            jax.ShapeDtypeStruct((tokens + 16, local), BF),
            jax.ShapeDtypeStruct((4, reports * 48, 2 * local), BF),
        ],
        compiler_params=params(),
        cost_estimate=pl.CostEstimate(
            flops=10 * tokens * span * local, bytes_accessed=6 << 20, transcendentals=tokens * span * 4
        ),
    )(slot, gate, q_own, q_got, o_own, o_got, keys, vals, allowed)


def back_kernel(following, dq_own, dq_got, stat, up, live, h, rinv, gain, wq, *refs):
    half = dq_own.shape[1]
    if following:
        wo, grad, o_own, o_send, o_acc = refs
    else:
        (grad,) = refs
    step = pl.program_id(0)
    dnormed = dot(dq_own[...], wq[:half], NN) + dot(dq_got[...], wq[half:], NN)
    upstream = jnp.where(live[...] > 0, up[...].astype(F32), 0.0)
    xhat = h[...].astype(F32) * rinv[...]
    value = upstream + rinv[...] * (gain[...] * dnormed - xhat * (stat[...] / MODEL_WIDTH))
    value = value.astype(BF)
    grad[...] = value
    if not following:
        return
    o_term = dot(value, wo[...], NT)

    @pl.when(step == 0)
    def _():
        o_acc[...] = o_term

    @pl.when(step > 0)
    def _():
        o_acc[...] += o_term

    @pl.when(step == pl.num_programs(0) - 1)
    def _():
        o_own[...] = o_acc[:, :half].astype(BF)
        o_send[...] = o_acc[:, half:].astype(BF)


def back(dq_own, dq_got, stat, up, live, h, rinv, gain, wq, wo=None):
    tokens, width = h.shape
    inner = wq.shape[0]
    half = inner // 2
    act = pl.BlockSpec((tokens, TILE), lambda i: (0, i))
    weight = pl.BlockSpec((inner, TILE), lambda i: (0, i))
    column = whole((tokens, 1))
    inputs = [dq_own, dq_got, stat, up, live, h, rinv, gain, wq]
    specs = [whole((tokens, half))] * 2 + [column, act, column, act, column]
    specs += [pl.BlockSpec((1, TILE), lambda i: (0, i)), weight]
    out_specs = [act]
    out_shape = [jax.ShapeDtypeStruct((tokens, width), BF)]
    scratch = []
    if wo is not None:
        inputs.append(wo)
        specs.append(weight)
        out_specs += [whole((tokens, half))] * 2
        out_shape += [jax.ShapeDtypeStruct((tokens, half), BF)] * 2
        scratch = [pltpu.VMEM((tokens, inner), F32)]
    return pl.pallas_call(
        functools.partial(back_kernel, wo is not None),
        grid=(width // TILE,),
        in_specs=specs,
        out_specs=out_specs,
        out_shape=out_shape,
        scratch_shapes=scratch,
        compiler_params=params(),
        cost_estimate=pl.CostEstimate(
            flops=(4 if wo is not None else 2) * tokens * width * inner,
            bytes_accessed=14 << 20,
            transcendentals=0,
        ),
    )(*inputs)


def per_device(
    segment_inputs,
    cotangent,
    report_lengths,
    norm_gain,
    attn_gate,
    w_query,
    w_out,
    w_key,
    w_value,
    tiles,
    tile_counts,
    lat_query,
    request_source,
    request_slide,
    cross_pattern,
):
    z, y, core = (lax.axis_index(name) for name in DP)
    me_dp = (z * 4 + y) * 2 + core
    me_mp = lax.axis_index("mp")
    seg = lax.axis_index("segment")
    me_x = me_mp * 2 + seg
    last = seg == 1
    reports = cross_pattern.shape[0]
    wanted = reports * SPR

    pooled = pool(
        me_x.reshape(1).astype(jnp.int32), tile_counts.reshape(4), tiles, lat_query
    )
    lat_blocks = gather_dp(pooled)

    wq_t = w_query[0].T
    w_blocks = gather_dp(jnp.concatenate([w_out[0], wq_t], axis=0))

    place = places()
    rows = lax.rem(place * 32 - me_mp * 512 + 1024, 1024).astype(jnp.int32)
    where_is = jnp.zeros((32,), jnp.int32).at[place].set(jnp.arange(32, dtype=jnp.int32))
    source = lax.dynamic_index_in_dim(
        request_source.reshape(32, wanted), me_dp, 0, keepdims=False
    )
    slide = lax.dynamic_index_in_dim(request_slide.reshape(32, wanted), me_dp, 0, keepdims=False)
    found = where_is[source]
    chosen = select(found // 4, found % 4, slide, lat_blocks)
    lat_parts = [chosen] + [lax.ppermute(chosen, X, x_perm(k)) for k in (1, 2, 3)]
    latents = jnp.concatenate(lat_parts, axis=1)
    w_kv = jnp.concatenate([w_key[0], w_value[0]], axis=1)
    w_kv_x = jnp.concatenate(
        [
            lax.dynamic_slice_in_dim(w_kv, lax.rem(me_x - k + 4, 4) * QUARTER, QUARTER, 0)
            for k in range(4)
        ],
        axis=0,
    )
    kv = dot(latents, w_kv_x, NN).astype(BF)
    local = w_key.shape[2]
    keys, vals = kv[:, :local], kv[:, local:]

    h = segment_inputs[0]
    h32 = h.astype(F32)
    squares = lax.psum(jnp.sum(h32 * h32, axis=1), "mp")
    both = lax.all_gather(jnp.concatenate([squares, norm_gain[0]]), "segment")
    tokens, width = h.shape
    squares1, gain1 = both[1, :tokens], both[1, tokens:]
    rinv = lax.rsqrt(squares / MODEL_WIDTH + 1e-05)[:, None]
    rinv1 = lax.rsqrt(squares1 / MODEL_WIDTH + 1e-05)[:, None]
    gain = norm_gain[0][None, :]
    gain1 = gain1[None, :]
    h1 = jnp.where(last, h, lax.ppermute(h, "segment", [(1, 0)]))
    wq1_t = jnp.where(last, wq_t, lax.ppermute(wq_t, "segment", [(1, 0)]))
    live = (jnp.arange(tokens) % L < jnp.repeat(report_lengths, L)).astype(F32)[:, None]
    allowed = jnp.broadcast_to(
        cross_pattern[:, :, None, :, None], (reports, cross_pattern.shape[1], QBLK, SPR, LAT)
    ).reshape(tokens, SPR * LAT).astype(F32)
    gate = jnp.tanh(attn_gate)
    slot = []
    for part in range(4):
        same_seg, same_mp = seg == part // 2, me_mp == part % 2
        slot.append(jnp.where(same_seg, jnp.where(same_mp, 0, 3), jnp.where(same_mp, 1, 2)))
    slot = jnp.stack(slot).astype(jnp.int32)

    wo, wq = assemble(rows, w_blocks, 2)
    (wq1,) = assemble(rows, gather_dp(wq1_t), 1)

    q_own, q_send, o_own, o_send = front(h, rinv, gain, cotangent, live, wq, wo)
    q_got = lax.ppermute(q_send, X, SWAP_MP)
    o_got = lax.ppermute(o_send, X, LAST_SWAP)
    dq, dkv = attend(slot, gate, q_own, q_got, o_own, o_got, keys, vals, allowed)
    dq_same = jnp.where(last, dq, lax.ppermute(dq, X, LAST_TO_SAME))
    dq_cross = lax.ppermute(dq, X, LAST_TO_CROSS) + lax.ppermute(dq, X, LAST_SWAP)

    def split(own, got):
        stat = jnp.sum(
            own[tokens : tokens + 3].astype(F32) + got[tokens : tokens + 3].astype(F32), axis=0
        )
        return own[:tokens], got[:tokens], stat[:, None]

    def latent_terms(dkv):
        own = dot(dkv[0], w_kv, NT)
        return own, [dot(dkv[k], w_kv, NT).astype(BF) for k in (1, 2, 3)]

    own1, terms = latent_terms(dkv)
    got = [
        lax.ppermute(t, X, p)
        for t, p in zip(terms, (LAST_TO_SAME, LAST_TO_CROSS, LAST_SWAP))
    ]
    grad1, o_own, o_send = back(
        *split(dq_same, dq_cross), cotangent, live, h1, rinv1, gain1, wq1, wo
    )

    o_got = lax.ppermute(o_send, X, FIRST_SWAP)
    dq, dkv = attend(slot, gate, q_own, q_got, o_own, o_got, keys, vals, allowed)
    dq_got = lax.ppermute(dq, X, FIRST_SWAP)
    own0, terms = latent_terms(dkv)
    got += [
        lax.ppermute(t, X, p)
        for t, p in zip(terms, (FIRST_TO_SAME, FIRST_TO_CROSS, FIRST_SWAP))
    ]
    (grad0,) = back(*split(dq, dq_got), grad1, jnp.ones_like(live), h, rinv, gain, wq)

    grads = jnp.where(last, grad1, grad0)
    latent_grad = jnp.where(last, own1, own0)
    for term in got:
        latent_grad = latent_grad + term.astype(F32)
    return grads[None], latent_grad.reshape(reports, 48, E)


def solution(mesh):
    fine = Mesh(mesh.devices.reshape(2, 4, 4, 2, 2), ("segment", "z", "y", "core", "mp"))
    return jax.shard_map(
        per_device,
        mesh=fine,
        in_specs=(
            P("segment", DP, "mp"),
            P(DP, "mp"),
            P(DP),
            P("segment", "mp"),
            P("segment"),
            P("segment", "mp", DP),
            P("segment", DP, "mp"),
            P("segment", None, "mp"),
            P("segment", None, "mp"),
            P(DP, None, None),
            P(DP, None),
            P(),
            P(),
            P(),
            P(DP, None, None),
        ),
        out_specs=(P("segment", DP, "mp"), P(DP, X, None)),
        check_vma=False,
    )
```

```python
import functools

import jax
import jax.numpy as jnp
from jax import lax
from jax.experimental import pallas as pl
from jax.experimental.pallas import tpu as pltpu
from jax.sharding import Mesh
from jax.sharding import PartitionSpec as P

MODEL_WIDTH = 4096
E = 1536
HEAD = 128
LAT = 32
SPR = 6
L = 128
QBLK = 32
MAXT = 64
QUARTER = E // 4
SCALE = HEAD ** (-0.5)
DP = ("z", "y", "core")
X = ("segment", "mp")
BF = jnp.bfloat16
F32 = jnp.float32
LIMIT = 60 * 1024 * 1024
NT = (((1,), (1,)), ((), ()))
NN = (((1,), (0,)), ((), ()))
TN = (((0,), (0,)), ((), ()))

SWAP_MP = [(0, 1), (1, 0), (2, 3), (3, 2)]
LAST_TO_SAME = [(2, 0), (3, 1)]
LAST_TO_CROSS = [(2, 1), (3, 0)]
LAST_SWAP = [(2, 3), (3, 2)]
FIRST_TO_SAME = [(0, 2), (1, 3)]
FIRST_TO_CROSS = [(0, 3), (1, 2)]
FIRST_SWAP = [(0, 1), (1, 0)]
AT_X = (0, 2, 1, 3)


def x_perm(k):
    return [(AT_X[x], AT_X[(x + k) % 4]) for x in range(4)]


def yz_perm(stage, k):
    pairs = []
    for z in range(4):
        for y in range(4):
            for core in range(2):
                along_y = (core == 0) == (stage == 1)
                to_z = z if along_y else (z + k) % 4
                to_y = (y + k) % 4 if along_y else y
                pairs.append(((z * 4 + y) * 2 + core, (to_z * 4 + to_y) * 2 + core))
    return pairs


def dot(a, b, dims):
    return lax.dot_general(a, b, dims, preferred_element_type=F32)


def params(**kwargs):
    return pltpu.CompilerParams(vmem_limit_bytes=LIMIT, **kwargs)


def whole(shape):
    return pl.BlockSpec(shape, lambda *_: (0,) * len(shape))


SMEM = pl.BlockSpec(memory_space=pltpu.SMEM)
ANY = pl.BlockSpec(memory_space=pl.ANY)
VMEM = pl.BlockSpec(memory_space=pltpu.VMEM)
TILE = 512


def pool_kernel(which, counts, tiles, queries, out):
    for slide in range(4):
        live = lax.broadcasted_iota(jnp.int32, (LAT, MAXT), 1) < counts[slide]
        for head in range(QUARTER // HEAD):
            cols = slice(head * HEAD, (head + 1) * HEAD)
            tile = tiles[slide, :, cols]
            query = queries[:, cols]
            scores = dot(query, tile, NT) * SCALE
            scores = jnp.where(live, scores, -1e30)
            exps = jnp.exp(scores - jnp.max(scores, axis=1, keepdims=True))
            weights = (exps / jnp.sum(exps, axis=1, keepdims=True)).astype(BF)
            pooled = dot(weights, tile, NN)
            out[slide * LAT : (slide + 1) * LAT, cols] = (query.astype(F32) + pooled).astype(BF)


def pool(which, counts, tiles, queries):
    return pl.pallas_call(
        pool_kernel,
        grid_spec=pltpu.PrefetchScalarGridSpec(
            num_scalar_prefetch=2,
            grid=(1,),
            in_specs=[
                pl.BlockSpec((4, MAXT, QUARTER), lambda i, which, counts: (0, 0, which[0])),
                pl.BlockSpec((LAT, QUARTER), lambda i, which, counts: (0, which[0])),
            ],
            out_specs=pl.BlockSpec((4 * LAT, QUARTER), lambda i, which, counts: (0, 0)),
        ),
        out_shape=jax.ShapeDtypeStruct((4 * LAT, QUARTER), BF),
        compiler_params=params(),
    )(which, counts, tiles, queries)


def gather_chips(block):
    parts = [block] + [lax.ppermute(block, DP, yz_perm(1, k)) for k in (1, 2, 3)]
    bundle = jnp.stack(parts)
    return [bundle] + [lax.ppermute(bundle, DP, yz_perm(2, k)) for k in (1, 2, 3)]


def places(z, y, core):
    table = []
    for a in range(8):
        c = core if a < 4 else 1 - core
        for k in range(4):
            j = a % 4
            at_z = lax.rem(z - jnp.where(c == 0, j, k) + 4, 4)
            at_y = lax.rem(y - jnp.where(c == 0, k, j) + 4, 4)
            table.append((at_z * 4 + at_y) * 2 + c)
    return jnp.stack(table).astype(jnp.int32)


def select_kernel(wanted, array, block, slide, *refs):
    ins, outs, sems = refs[:4], refs[4:6], refs[6]

    def copy(a, which, i):
        at = which * wanted + i
        return pltpu.make_async_copy(
            ins[a].at[block[at], pl.ds(pl.multiple_of(slide[at] * LAT, LAT), LAT)],
            outs[which].at[pl.ds(i * LAT, LAT)],
            sems.at[at],
        )

    for act in ("start", "wait"):
        for which in range(2):
            for i in range(wanted):
                for a in range(4):

                    @pl.when(array[which * wanted + i] == a)
                    def _():
                        getattr(copy(a, which, i), act)()


def select(array, block, slide, blocks):
    wanted = array.shape[0] // 2
    out = jax.ShapeDtypeStruct((wanted * LAT, QUARTER), BF)
    return pl.pallas_call(
        functools.partial(select_kernel, wanted),
        in_specs=[SMEM] * 3 + [ANY] * 4,
        out_specs=[VMEM, VMEM],
        out_shape=[out, out],
        scratch_shapes=[pltpu.SemaphoreType.DMA((2 * wanted,))],
        compiler_params=params(),
    )(array, block, slide, *blocks)


def column(row):
    return jnp.broadcast_to(row, (HEAD, row.shape[1])).T[:, :1]


def live_tokens(lengths, tokens):
    index = lax.broadcasted_iota(jnp.int32, (tokens, 1), 0)
    parts = [index[r * L : (r + 1) * L] < r * L + lengths[r] for r in range(tokens // L)]
    return jnp.concatenate([p.astype(F32) for p in parts], axis=0) > 0


def project_kernel(kind, rows, lengths, rinv, gain, x, *refs):
    ins, (send, weight, left), (w_v, x_v, sems) = refs[:8], refs[8:11], refs[11:]
    load = pltpu.make_async_copy(x, x_v, sems.at[2])
    load.start()
    half = w_v.shape[0] // 2
    for part in (1, 0):
        for a in range(8):
            for k in range(4):
                at = pl.multiple_of(rows[a * 4 + k], 32)
                group = (at >= half).astype(jnp.int32)

                @pl.when(group == part)
                def _():
                    pltpu.make_async_copy(
                        ins[a].at[k, pl.ds(kind * 32, 32)], w_v.at[pl.ds(at, 32)], sems.at[part]
                    ).start()

    load.wait()
    if kind == 0:
        live = live_tokens(lengths, x_v.shape[0])
        x_v[...] = jnp.where(live, x_v[...].astype(F32), 0.0).astype(BF)
    else:
        x_v[...] = (x_v[...].astype(F32) * column(rinv[...]) * gain[...]).astype(BF)
    store_x = pltpu.make_async_copy(x_v, left, sems.at[2])
    store_x.start()

    def group(part):
        return w_v.at[pl.ds(part * half, half)]

    pltpu.make_async_copy(group(1), group(1), sems.at[1]).wait()
    store1 = pltpu.make_async_copy(group(1), weight.at[pl.ds(half, half)], sems.at[1])
    store1.start()
    send[...] = dot(x_v[...], w_v[half:], NT).astype(BF)
    pltpu.make_async_copy(group(0), group(0), sems.at[0]).wait()
    store0 = pltpu.make_async_copy(group(0), weight.at[pl.ds(0, half)], sems.at[0])
    store0.start()
    store_x.wait()
    store1.wait()
    store0.wait()


def project(kind, rows, lengths, rinv, gain, x, blocks):
    tokens, width = x.shape
    inner = 32 * 32
    return pl.pallas_call(
        functools.partial(project_kernel, kind),
        in_specs=[SMEM, SMEM, VMEM, VMEM, ANY] + [ANY] * 8,
        out_specs=[VMEM, ANY, ANY],
        out_shape=[
            jax.ShapeDtypeStruct((tokens, inner // 2), BF),
            jax.ShapeDtypeStruct((inner, width), BF),
            jax.ShapeDtypeStruct((tokens, width), BF),
        ],
        scratch_shapes=[
            pltpu.VMEM((inner, width), BF),
            pltpu.VMEM((tokens, width), BF),
            pltpu.SemaphoreType.DMA((3,)),
        ],
        compiler_params=params(),
        cost_estimate=pl.CostEstimate(
            flops=tokens * width * inner, bytes_accessed=12 << 20, transcendentals=0
        ),
    )(rows, lengths, rinv, gain, x, *blocks)


def forward_kernel(pattern, q_own, q_got, keys, probs):
    report = pl.program_id(0)
    span = keys.shape[0]
    slide = lax.broadcasted_iota(jnp.int32, (QBLK, span), 1) // LAT
    masks = []
    for block in range(L // QBLK):
        seen = jnp.zeros((QBLK, span), jnp.int32)
        for j in range(SPR):
            seen = jnp.where(slide == j, pattern[(report * (L // QBLK) + block) * SPR + j], seen)
        masks.append(seen)
    mask = jnp.concatenate(masks, axis=0) == 1
    for head in range(probs.shape[0]):
        cols = slice(head * HEAD, (head + 1) * HEAD)
        qb = (q_own[:, cols] + q_got[:, cols].astype(F32)).astype(BF)
        scores = jnp.where(mask, dot(qb, keys[:, cols], NT) * SCALE, -1e30)
        exps = jnp.exp(scores - jnp.max(scores, axis=1, keepdims=True))
        probs[head] = exps / jnp.sum(exps, axis=1, keepdims=True)


def forward(pattern, q_own, q_got, kv):
    tokens, local = q_own.shape
    reports = tokens // L
    span = kv.shape[0] // reports
    heads = local // HEAD
    token = pl.BlockSpec((L, local), lambda i: (i, 0))
    return pl.pallas_call(
        forward_kernel,
        grid=(reports,),
        in_specs=[SMEM, token, token, pl.BlockSpec((span, local), lambda i: (i, 0))],
        out_specs=pl.BlockSpec((heads, L, span), lambda i: (0, i, 0)),
        out_shape=jax.ShapeDtypeStruct((heads, tokens, span), F32),
        compiler_params=params(),
        cost_estimate=pl.CostEstimate(
            flops=2 * tokens * span * local, bytes_accessed=6 << 20, transcendentals=tokens * span * 4
        ),
    )(pattern, q_own, q_got, kv)


def backward_kernel(slot, gate, q_own, q_got, o_own, o_got, keys, vals, probs, dq_out, dkv_out):
    report = pl.program_id(0)
    rows = pl.ds(pl.multiple_of(report * L, L), L)
    local = q_own.shape[1]
    stat = jnp.zeros((L, HEAD), F32)
    for head in range(local // HEAD):
        cols = slice(head * HEAD, (head + 1) * HEAD)
        q = q_own[:, cols] + q_got[:, cols].astype(F32)
        qb = q.astype(BF)
        og = (gate[0] * (o_own[:, cols].astype(F32) + o_got[:, cols].astype(F32))).astype(BF)
        key = keys[:, cols]
        prob = probs[head]
        dprob = dot(og, vals[:, cols], NT)
        rowdot = jnp.sum(prob * dprob, axis=1, keepdims=True)
        dscore = (prob * (dprob - rowdot)).astype(BF)
        dq = (dot(dscore, key, NN) * SCALE).astype(BF)
        dkey = (dot(dscore, qb, TN) * SCALE).astype(BF)
        dval = dot(prob.astype(BF), og, TN).astype(BF)
        dq_out[rows, cols] = dq
        stat += q * dq.astype(F32)
        for part in range(4):
            into = pl.ds(pl.multiple_of(report * 48, 16), 48)
            piece = slice(part * 48, (part + 1) * 48)
            dkv_out[slot[part], into, cols] = dkey[piece]
            dkv_out[slot[part], into, local + head * HEAD : local + (head + 1) * HEAD] = dval[piece]
    total = jnp.sum(stat.T, axis=0, keepdims=True)
    high = total.astype(BF)
    rest = total - high.astype(F32)
    low = rest.astype(BF)
    lower = (rest - low.astype(F32)).astype(BF)
    zero = jnp.zeros((13, L), F32)
    extra = jnp.concatenate([high.astype(F32), low.astype(F32), lower.astype(F32), zero], axis=0)
    dq_out[4 * L : 4 * L + 16, rows] = extra.astype(BF)


def backward(slot, gate, q_own, q_got, o_own, o_got, kv, probs):
    tokens, local = q_own.shape
    reports = tokens // L
    heads, _, span = probs.shape
    token = pl.BlockSpec((L, local), lambda i: (i, 0))
    return pl.pallas_call(
        backward_kernel,
        grid=(reports,),
        in_specs=[SMEM, SMEM, token, token, token, token]
        + [
            pl.BlockSpec((span, local), lambda i: (i, 0)),
            pl.BlockSpec((span, local), lambda i: (i, 1)),
            pl.BlockSpec((heads, L, span), lambda i: (0, i, 0)),
        ],
        out_specs=[whole((tokens + 16, local)), whole((4, reports * 48, 2 * local))],
        out_shape=[
            jax.ShapeDtypeStruct((tokens + 16, local), BF),
            jax.ShapeDtypeStruct((4, reports * 48, 2 * local), BF),
        ],
        compiler_params=params(),
        cost_estimate=pl.CostEstimate(
            flops=8 * tokens * span * local, bytes_accessed=8 << 20, transcendentals=0
        ),
    )(slot, gate, q_own, q_got, o_own, o_got, kv, kv, probs)


def back_kernel(following, info, lengths, dq_own, dq_got, rinv, gain, up, h, wq, *refs):
    if following:
        wo, grad, o_send, wq_v, up_v, h_v, wo_v, sems = refs
    else:
        grad, wq_v, up_v, h_v, sems = refs
    inner, width = wq_v.shape
    half = inner // 2
    tokens = up_v.shape[0]
    tiles = width // TILE

    def copies(tile):
        cols = slice(tile * TILE, (tile + 1) * TILE)
        out = []
        for part in range(2):
            at = pl.multiple_of(info[1 + part], half)
            into = slice(part * half, (part + 1) * half)
            out.append((wq.at[pl.ds(at, half), cols], wq_v.at[into, cols]))
        out.append((up.at[:, cols], up_v.at[:, cols]))
        out.append((h.at[:, cols], h_v.at[:, cols]))
        return [
            pltpu.make_async_copy(a, b, sems.at[tile * 4 + i]) for i, (a, b) in enumerate(out)
        ]

    for tile in range(tiles):
        for copy in copies(tile):
            copy.start()
    if following:
        load = pltpu.make_async_copy(wo.at[pl.ds(half, half)], wo_v, sems.at[tiles * 4])
        load.start()
    stat = column(
        jnp.sum(dq_own[tokens:].astype(F32) + dq_got[tokens:].astype(F32), axis=0, keepdims=True)
    )
    scale = column(rinv[...])
    share = scale * scale * stat / MODEL_WIDTH
    if following:
        live = live_tokens(lengths, tokens)
    stores = []
    for tile in range(tiles):
        for copy in copies(tile):
            copy.wait()
        cols = slice(tile * TILE, (tile + 1) * TILE)
        dnormed = dot(dq_own[:tokens], wq_v[:half, cols], NN)
        dnormed += dot(dq_got[:tokens], wq_v[half:, cols], NN)
        upstream = up_v[:, cols].astype(F32)
        if following:
            upstream = jnp.where(live, upstream, 0.0)
        value = upstream + (scale * (gain[:, cols] * dnormed) - h_v[:, cols].astype(F32) * share)
        if following:
            value = jnp.where(info[0] == 1, upstream, value)
        up_v[:, cols] = value.astype(BF)
        store = pltpu.make_async_copy(up_v.at[:, cols], grad.at[:, cols], sems.at[tile * 4])
        store.start()
        stores.append(store)
    if following:
        load.wait()
        o_send[...] = dot(up_v[...], wo_v[...], NT).astype(BF)
    for store in stores:
        store.wait()


def back(info, lengths, dq_own, dq_got, rinv, gain, up, h, wq, wo=None):
    tokens, width = h.shape
    inner = wq.shape[0]
    half = inner // 2
    inputs = [info, lengths, dq_own, dq_got, rinv, gain, up, h, wq]
    in_specs = [SMEM, SMEM, VMEM, VMEM, VMEM, VMEM, ANY, ANY, ANY]
    out_specs = [ANY]
    out_shape = [jax.ShapeDtypeStruct((tokens, width), BF)]
    scratch = [pltpu.VMEM((inner, width), BF)] + [pltpu.VMEM((tokens, width), BF)] * 2
    if wo is not None:
        inputs.append(wo)
        in_specs.append(ANY)
        out_specs.append(VMEM)
        out_shape.append(jax.ShapeDtypeStruct((tokens, half), BF))
        scratch.append(pltpu.VMEM((half, width), BF))
    return pl.pallas_call(
        functools.partial(back_kernel, wo is not None),
        in_specs=in_specs,
        out_specs=out_specs,
        out_shape=out_shape,
        scratch_shapes=scratch + [pltpu.SemaphoreType.DMA((width // TILE * 4 + 1,))],
        compiler_params=params(),
        cost_estimate=pl.CostEstimate(
            flops=(3 if wo is not None else 2) * tokens * width * inner,
            bytes_accessed=12 << 20,
            transcendentals=0,
        ),
    )(*inputs)


def term_kernel(dkv, w_kv, own, *terms):
    for k in range(4):
        value = dot(dkv[k], w_kv[...], NT)
        if k == 0:
            own[...] = value
        else:
            terms[k - 1][...] = value.astype(BF)


def latent_terms(dkv, w_kv):
    rows, inner = dkv.shape[1:]
    features = w_kv.shape[0]
    tile = features // 3
    result = pl.BlockSpec((rows, tile), lambda i: (0, i))
    return pl.pallas_call(
        term_kernel,
        grid=(features // tile,),
        in_specs=[whole(dkv.shape), pl.BlockSpec((tile, inner), lambda i: (i, 0))],
        out_specs=[result] * 4,
        out_shape=[jax.ShapeDtypeStruct((rows, features), t) for t in (F32, BF, BF, BF)],
        compiler_params=params(),
        cost_estimate=pl.CostEstimate(
            flops=8 * rows * inner * features, bytes_accessed=8 << 20, transcendentals=0
        ),
    )(dkv, w_kv)


def per_device(
    segment_inputs,
    cotangent,
    report_lengths,
    norm_gain,
    attn_gate,
    w_query,
    w_out,
    w_key,
    w_value,
    tiles,
    tile_counts,
    lat_query,
    request_source,
    request_slide,
    cross_pattern,
):
    z, y, core = (lax.axis_index(name) for name in DP)
    me_dp = (z * 4 + y) * 2 + core
    me_mp = lax.axis_index("mp")
    seg = lax.axis_index("segment")
    me_x = me_mp * 2 + seg
    last = seg == 1
    reports = cross_pattern.shape[0]
    wanted = reports * SPR
    h = segment_inputs[0]
    tokens, width = h.shape
    half = 512

    wq_t = w_query[0].T
    h1 = lax.ppermute(h, "segment", [(1, 0)])
    wq1 = lax.all_gather(lax.ppermute(wq_t, "segment", [(1, 0)]), DP, axis=0, tiled=True)

    pooled = pool(me_x.reshape(1).astype(jnp.int32), tile_counts.reshape(4), tiles, lat_query)
    lat_blocks = gather_chips(pooled)
    pair = me_dp - core
    sources = request_source.reshape(32, wanted)
    slides = request_slide.reshape(32, wanted)
    order = jnp.stack([me_dp, me_dp + 1 - 2 * core])
    source = sources[order]
    slide = slides[order].reshape(-1)
    source_core = source % 2
    far_z = lax.rem(z - source // 8 + 4, 4)
    far_y = lax.rem(y - source // 2 % 4 + 4, 4)
    first = jnp.where(core == 0, far_y, far_z)
    second = jnp.where(core == 0, far_z, far_y)
    array = jnp.where(source_core == core, second, 4)
    near, across = select(array.reshape(-1), first.reshape(-1), slide, lat_blocks)
    crossed = lax.ppermute(across, "core", [(0, 1), (1, 0)])
    is_near = jnp.repeat(source_core[0] == core, LAT)[:, None]
    chosen = jnp.where(is_near, near, crossed)
    latents = jnp.concatenate(
        [chosen] + [lax.ppermute(chosen, X, x_perm(k)) for k in (1, 2, 3)], axis=1
    )
    w_kv = jnp.concatenate([w_key[0], w_value[0]], axis=1)
    w_kv_x = jnp.concatenate(
        [
            lax.dynamic_slice_in_dim(w_kv, lax.rem(me_x - k + 4, 4) * QUARTER, QUARTER, 0)
            for k in range(4)
        ],
        axis=0,
    )
    kv = dot(latents, w_kv_x, NN).astype(BF)

    blocks = gather_chips(jnp.concatenate([w_out[0], wq_t], axis=0))
    blocks = blocks + [lax.ppermute(b, "core", [(0, 1), (1, 0)]) for b in blocks]
    rows = lax.rem(places(z, y, core) * 32 - me_mp * half + 2 * half, 2 * half)

    h32 = h.astype(F32)
    message = jnp.concatenate([jnp.sum(h32 * h32, axis=1), norm_gain[0]])
    messages = lax.all_gather(message, X)
    squares = messages[:, :tokens].reshape(2, 2, tokens).sum(axis=1)
    rinvs = lax.rsqrt(squares / MODEL_WIDTH + 1e-05)
    rinv = lax.dynamic_index_in_dim(rinvs, seg, 0)
    rinv1 = rinvs[1:]
    gain = norm_gain
    gain1 = lax.dynamic_index_in_dim(messages[2:, tokens:], me_mp, 0)
    gate = jnp.tanh(attn_gate)
    slot = []
    for part in range(4):
        same_seg, same_mp = seg == part // 2, me_mp == part % 2
        slot.append(jnp.where(same_seg, jnp.where(same_mp, 0, 3), jnp.where(same_mp, 1, 2)))
    slot = jnp.stack(slot).astype(jnp.int32)
    pattern = cross_pattern.reshape(-1)

    q_send, wq, normed = project(1, rows, report_lengths, rinv, gain, h, blocks)
    q_got = lax.ppermute(q_send, X, SWAP_MP)
    o_send, wo, up1 = project(0, rows, report_lengths, rinv, gain, cotangent, blocks)
    o_got = lax.ppermute(o_send, X, LAST_SWAP)
    q_own = dot(normed, wq[:half], NT)
    o_own = dot(up1, wo[:half], NT).astype(BF)
    probs = forward(pattern, q_own, q_got, kv)
    dq1, dkv1 = backward(slot, gate, q_own, q_got, o_own, o_got, kv, probs)
    dq_same = lax.ppermute(dq1, X, LAST_TO_SAME)
    dq_cross = lax.ppermute(dq1, X, LAST_TO_CROSS)
    info1 = jnp.stack([seg, me_mp * half, (1 - me_mp) * half]).astype(jnp.int32)
    up, o_send = back(
        info1, report_lengths, dq_same, dq_cross, rinv1, gain1, cotangent, h1, wq1, wo
    )
    o_got = lax.ppermute(o_send, X, FIRST_SWAP)
    o_own = dot(up, wo[:half], NT).astype(BF)
    dq1, dkv1, _ = lax.optimization_barrier((dq1, dkv1, o_send))
    dq1_got = lax.ppermute(dq1, X, LAST_SWAP)
    own1, *terms = latent_terms(dkv1, w_kv)
    moves = (LAST_TO_SAME, LAST_TO_CROSS, LAST_SWAP)
    got = [lax.ppermute(t, X, p) for t, p in zip(terms, moves)]

    dq0, dkv0 = backward(slot, gate, q_own, q_got, o_own, o_got, kv, probs)
    dq0_got = lax.ppermute(dq0, X, FIRST_SWAP)
    own0, *terms = latent_terms(dkv0, w_kv)
    moves = (FIRST_TO_SAME, FIRST_TO_CROSS, FIRST_SWAP)
    got += [lax.ppermute(t, X, p) for t, p in zip(terms, moves)]
    dq = jnp.where(last, dq1, dq0)
    dq_got = jnp.where(last, dq1_got, dq0_got)
    info = jnp.array([0, 0, half], jnp.int32)
    (grads,) = back(info, report_lengths, dq, dq_got, rinv, gain, up, h, wq)

    latent_grad = jnp.where(last, own1, own0)
    for term in got:
        latent_grad = latent_grad + term.astype(F32)
    return grads[None], latent_grad.reshape(reports, 48, E)


def solution(mesh):
    fine = Mesh(mesh.devices.reshape(2, 4, 4, 2, 2), ("segment", "z", "y", "core", "mp"))
    return jax.shard_map(
        per_device,
        mesh=fine,
        in_specs=(
            P("segment", DP, "mp"),
            P(DP, "mp"),
            P(DP),
            P("segment", "mp"),
            P("segment"),
            P("segment", "mp", DP),
            P("segment", DP, "mp"),
            P("segment", None, "mp"),
            P("segment", None, "mp"),
            P(DP, None, None),
            P(DP, None),
            P(),
            P(),
            P(),
            P(DP, None, None),
        ),
        out_specs=(P("segment", DP, "mp"), P(DP, X, None)),
        check_vma=False,
    )
```

```python
import functools

import jax
import jax.numpy as jnp
from jax import lax
from jax.experimental import pallas as pl
from jax.experimental.pallas import tpu as pltpu
from jax.sharding import Mesh
from jax.sharding import PartitionSpec as P

MODEL_WIDTH = 4096
E = 1536
HEAD = 128
LAT = 32
SPR = 6
L = 128
QBLK = 32
MAXT = 64
QUARTER = E // 4
SCALE = HEAD ** (-0.5)
DP = ("z", "y", "core")
X = ("segment", "mp")
BF = jnp.bfloat16
F32 = jnp.float32
LIMIT = 60 * 1024 * 1024
NT = (((1,), (1,)), ((), ()))
NN = (((1,), (0,)), ((), ()))
TN = (((0,), (0,)), ((), ()))

SWAP_MP = [(0, 1), (1, 0), (2, 3), (3, 2)]
LAST_TO_SAME = [(2, 0), (3, 1)]
LAST_TO_CROSS = [(2, 1), (3, 0)]
LAST_SWAP = [(2, 3), (3, 2)]
FIRST_TO_SAME = [(0, 2), (1, 3)]
FIRST_TO_CROSS = [(0, 3), (1, 2)]
FIRST_SWAP = [(0, 1), (1, 0)]
AT_X = (0, 2, 1, 3)


def x_perm(k):
    return [(AT_X[x], AT_X[(x + k) % 4]) for x in range(4)]


def yz_perm(stage, k):
    pairs = []
    for z in range(4):
        for y in range(4):
            for core in range(2):
                along_y = (core == 0) == (stage == 1)
                to_z = z if along_y else (z + k) % 4
                to_y = (y + k) % 4 if along_y else y
                pairs.append(((z * 4 + y) * 2 + core, (to_z * 4 + to_y) * 2 + core))
    return pairs


def dot(a, b, dims):
    return lax.dot_general(a, b, dims, preferred_element_type=F32)


def params(**kwargs):
    return pltpu.CompilerParams(vmem_limit_bytes=LIMIT, **kwargs)


def whole(shape):
    return pl.BlockSpec(shape, lambda *_: (0,) * len(shape))


SMEM = pl.BlockSpec(memory_space=pltpu.SMEM)
ANY = pl.BlockSpec(memory_space=pl.ANY)
VMEM = pl.BlockSpec(memory_space=pltpu.VMEM)
TILE = 512
ROWS, SLOT, INFO, LENGTHS, PATTERN = 0, 32, 36, 39, 43


def pool_kernel(which, counts, tiles, queries, out):
    for slide in range(4):
        live = lax.broadcasted_iota(jnp.int32, (LAT, MAXT), 1) < counts[slide]
        for head in range(QUARTER // HEAD):
            cols = slice(head * HEAD, (head + 1) * HEAD)
            tile = tiles[slide, :, cols]
            query = queries[:, cols]
            scores = dot(query, tile, NT) * SCALE
            scores = jnp.where(live, scores, -1e30)
            exps = jnp.exp(scores - jnp.max(scores, axis=1, keepdims=True))
            weights = (exps / jnp.sum(exps, axis=1, keepdims=True)).astype(BF)
            pooled = dot(weights, tile, NN)
            out[slide * LAT : (slide + 1) * LAT, cols] = (query.astype(F32) + pooled).astype(BF)


def pool(which, counts, tiles, queries):
    return pl.pallas_call(
        pool_kernel,
        grid_spec=pltpu.PrefetchScalarGridSpec(
            num_scalar_prefetch=2,
            grid=(1,),
            in_specs=[
                pl.BlockSpec((4, MAXT, QUARTER), lambda i, which, counts: (0, 0, which[0])),
                pl.BlockSpec((LAT, QUARTER), lambda i, which, counts: (0, which[0])),
            ],
            out_specs=pl.BlockSpec((4 * LAT, QUARTER), lambda i, which, counts: (0, 0)),
        ),
        out_shape=jax.ShapeDtypeStruct((4 * LAT, QUARTER), BF),
        compiler_params=params(),
    )(which, counts, tiles, queries)


def gather_chips(block):
    parts = [block] + [lax.ppermute(block, DP, yz_perm(1, k)) for k in (1, 2, 3)]
    bundle = jnp.stack(parts)
    return [bundle] + [lax.ppermute(bundle, DP, yz_perm(2, k)) for k in (1, 2, 3)]


def places(z, y, core):
    table = []
    for a in range(8):
        c = core if a < 4 else 1 - core
        for k in range(4):
            j = a % 4
            at_z = lax.rem(z - jnp.where(c == 0, j, k) + 4, 4)
            at_y = lax.rem(y - jnp.where(c == 0, k, j) + 4, 4)
            table.append((at_z * 4 + at_y) * 2 + c)
    return jnp.stack(table).astype(jnp.int32)


def select_kernel(wanted, picks, *refs):
    ins, outs, sems = refs[:4], refs[4:6], refs[6]

    def copy(a, which, i):
        at = which * wanted + i
        slide = pl.multiple_of(picks[4 * wanted + at] * LAT, LAT)
        return pltpu.make_async_copy(
            ins[a].at[picks[2 * wanted + at], pl.ds(slide, LAT)],
            outs[which].at[pl.ds(i * LAT, LAT)],
            sems.at[at],
        )

    for act in ("start", "wait"):
        for which in range(2):
            for i in range(wanted):
                for a in range(4):

                    @pl.when(picks[which * wanted + i] == a)
                    def _():
                        getattr(copy(a, which, i), act)()


def select(picks, blocks):
    wanted = picks.shape[0] // 6
    out = jax.ShapeDtypeStruct((wanted * LAT, QUARTER), BF)
    return pl.pallas_call(
        functools.partial(select_kernel, wanted),
        in_specs=[SMEM] + [ANY] * 4,
        out_specs=[VMEM, VMEM],
        out_shape=[out, out],
        scratch_shapes=[pltpu.SemaphoreType.DMA((2 * wanted,))],
        compiler_params=params(),
    )(picks, *blocks)


def column(row):
    return jnp.broadcast_to(row, (HEAD, row.shape[1])).T[:, :1]


def live_tokens(meta, tokens):
    index = lax.broadcasted_iota(jnp.int32, (tokens, 1), 0)
    parts = [index[r * L : (r + 1) * L] < r * L + meta[LENGTHS + r] for r in range(tokens // L)]
    return jnp.concatenate([p.astype(F32) for p in parts], axis=0) > 0


def project_kernel(kind, meta, x, *refs):
    ins, (send, weight), (w_v, x_v, sems) = refs[:8], refs[8:10], refs[10:]
    load = pltpu.make_async_copy(x, x_v, sems.at[2])
    load.start()
    half = w_v.shape[0] // 2
    for part in (1, 0):
        for a in range(8):
            for k in range(4):
                at = pl.multiple_of(meta[ROWS + a * 4 + k], 32)

                @pl.when((at >= half) == (part == 1))
                def _():
                    pltpu.make_async_copy(
                        ins[a].at[k, pl.ds(kind * 32, 32)], w_v.at[pl.ds(at, 32)], sems.at[part]
                    ).start()

    def group(part):
        return w_v.at[pl.ds(part * half, half)]

    load.wait()
    pltpu.make_async_copy(group(1), group(1), sems.at[1]).wait()
    store1 = pltpu.make_async_copy(group(1), weight.at[pl.ds(half, half)], sems.at[1])
    store1.start()
    send[...] = dot(x_v[...], w_v[half:], NT).astype(BF)
    pltpu.make_async_copy(group(0), group(0), sems.at[0]).wait()
    store0 = pltpu.make_async_copy(group(0), weight.at[pl.ds(0, half)], sems.at[0])
    store0.start()
    store1.wait()
    store0.wait()


def project(kind, meta, x, blocks):
    tokens, width = x.shape
    inner = 32 * 32
    return pl.pallas_call(
        functools.partial(project_kernel, kind),
        in_specs=[SMEM, ANY] + [ANY] * 8,
        out_specs=[VMEM, ANY],
        out_shape=[
            jax.ShapeDtypeStruct((tokens, inner // 2), BF),
            jax.ShapeDtypeStruct((inner, width), BF),
        ],
        scratch_shapes=[
            pltpu.VMEM((inner, width), BF),
            pltpu.VMEM((tokens, width), BF),
            pltpu.SemaphoreType.DMA((3,)),
        ],
        compiler_params=params(),
        cost_estimate=pl.CostEstimate(
            flops=tokens * width * inner, bytes_accessed=12 << 20, transcendentals=0
        ),
    )(meta, x, *blocks)


def forward_kernel(meta, q_own, q_got, keys, probs):
    report = pl.program_id(0)
    span = keys.shape[0]
    slide = lax.broadcasted_iota(jnp.int32, (QBLK, span), 1) // LAT
    masks = []
    for block in range(L // QBLK):
        seen = jnp.zeros((QBLK, span), jnp.int32)
        for j in range(SPR):
            at = PATTERN + (report * (L // QBLK) + block) * SPR + j
            seen = jnp.where(slide == j, meta[at], seen)
        masks.append(seen)
    mask = jnp.concatenate(masks, axis=0) == 1
    heads = [slice(head * HEAD, (head + 1) * HEAD) for head in range(probs.shape[0])]
    qb = [(q_own[:, c] + q_got[:, c].astype(F32)).astype(BF) for c in heads]
    scores = [dot(q, keys[:, c], NT) * SCALE for q, c in zip(qb, heads)]
    scores = [jnp.where(mask, s, -1e30) for s in scores]
    exps = [jnp.exp(s - jnp.max(s, axis=1, keepdims=True)) for s in scores]
    totals = [jnp.sum(e, axis=1, keepdims=True) for e in exps]
    for head, (e, total) in enumerate(zip(exps, totals)):
        probs[head] = e / total


def forward(meta, q_own, q_got, kv):
    tokens, local = q_own.shape
    reports = tokens // L
    span = kv.shape[0] // reports
    heads = local // HEAD
    token = pl.BlockSpec((L, local), lambda i: (i, 0))
    return pl.pallas_call(
        forward_kernel,
        grid=(reports,),
        in_specs=[SMEM, token, token, pl.BlockSpec((span, local), lambda i: (i, 0))],
        out_specs=pl.BlockSpec((heads, L, span), lambda i: (0, i, 0)),
        out_shape=jax.ShapeDtypeStruct((heads, tokens, span), F32),
        compiler_params=params(),
        cost_estimate=pl.CostEstimate(
            flops=2 * tokens * span * local, bytes_accessed=6 << 20, transcendentals=tokens * span * 4
        ),
    )(meta, q_own, q_got, kv)


def backward_kernel(meta, gate, q_own, q_got, o_own, o_got, keys, vals, probs, dq_out, dkv_out):
    report = pl.program_id(0)
    rows = pl.ds(pl.multiple_of(report * L, L), L)
    local = q_own.shape[1]
    heads = [slice(head * HEAD, (head + 1) * HEAD) for head in range(local // HEAD)]
    og = [
        (gate[0] * (o_own[:, c].astype(F32) + o_got[:, c].astype(F32))).astype(BF) for c in heads
    ]
    dprob = [dot(g, vals[:, c], NT) for g, c in zip(og, heads)]
    prob = [probs[head] for head in range(len(heads))]
    rowdot = [jnp.sum(p * d, axis=1, keepdims=True) for p, d in zip(prob, dprob)]
    dscore = [(p * (d - r)).astype(BF) for p, d, r in zip(prob, dprob, rowdot)]
    dq = [(dot(d, keys[:, c], NN) * SCALE).astype(BF) for d, c in zip(dscore, heads)]
    q = [q_own[:, c] + q_got[:, c].astype(F32) for c in heads]
    dkey = [(dot(d, x.astype(BF), TN) * SCALE).astype(BF) for d, x in zip(dscore, q)]
    dval = [dot(p.astype(BF), g, TN).astype(BF) for p, g in zip(prob, og)]
    stat = jnp.zeros((L, HEAD), F32)
    for c, d, x in zip(heads, dq, q):
        dq_out[rows, c] = d
        stat += x * d.astype(F32)
    into = pl.ds(pl.multiple_of(report * 48, 16), 48)
    both = jnp.concatenate(dkey + dval, axis=1)
    for part in range(4):
        dkv_out[meta[SLOT + part], into, :] = both[part * 48 : (part + 1) * 48]
    total = jnp.sum(stat.T, axis=0, keepdims=True)
    high = total.astype(BF)
    rest = total - high.astype(F32)
    low = rest.astype(BF)
    lower = (rest - low.astype(F32)).astype(BF)
    zero = jnp.zeros((13, L), F32)
    extra = jnp.concatenate([high.astype(F32), low.astype(F32), lower.astype(F32), zero], axis=0)
    dq_out[4 * L : 4 * L + 16, rows] = extra.astype(BF)


def backward(meta, gate, q_own, q_got, o_own, o_got, kv, probs):
    tokens, local = q_own.shape
    reports = tokens // L
    heads, _, span = probs.shape
    token = pl.BlockSpec((L, local), lambda i: (i, 0))
    return pl.pallas_call(
        backward_kernel,
        grid=(reports,),
        in_specs=[SMEM, SMEM, token, token, token, token]
        + [
            pl.BlockSpec((span, local), lambda i: (i, 0)),
            pl.BlockSpec((span, local), lambda i: (i, 1)),
            pl.BlockSpec((heads, L, span), lambda i: (0, i, 0)),
        ],
        out_specs=[whole((tokens + 16, local)), whole((4, reports * 48, 2 * local))],
        out_shape=[
            jax.ShapeDtypeStruct((tokens + 16, local), BF),
            jax.ShapeDtypeStruct((4, reports * 48, 2 * local), BF),
        ],
        compiler_params=params(),
        cost_estimate=pl.CostEstimate(
            flops=8 * tokens * span * local, bytes_accessed=8 << 20, transcendentals=0
        ),
    )(meta, gate, q_own, q_got, o_own, o_got, kv, kv, probs)


def back_kernel(following, meta, rinv, gain, *refs):
    if following:
        dq_own, dq_got, up, h, wq, wo, grad, o_send, wq_v, up_v, h_v, wo_v, sems = refs
        left, right = dq_own[...], dq_got[...]
    else:
        dq1, dq0, got1, got0, up, h, wq, grad, wq_v, up_v, h_v, sems = refs
        left = jnp.where(meta[INFO] == 1, dq1[...].astype(F32), dq0[...].astype(F32)).astype(BF)
        right = (got1[...].astype(F32) + got0[...].astype(F32)).astype(BF)
    if len(h.shape) == 3:
        h = h.at[1]
    inner, width = wq_v.shape
    half = inner // 2
    tokens = up_v.shape[0]
    tiles = width // TILE

    def copies(tile):
        cols = slice(tile * TILE, (tile + 1) * TILE)
        out = []
        for part in range(2):
            at = pl.multiple_of(meta[INFO + 1 + part], half) if following else part * half
            into = slice(part * half, (part + 1) * half)
            out.append((wq.at[pl.ds(at, half), cols], wq_v.at[into, cols]))
        out.append((up.at[:, cols], up_v.at[:, cols]))
        out.append((h.at[:, cols], h_v.at[:, cols]))
        return [
            pltpu.make_async_copy(a, b, sems.at[tile * 4 + i]) for i, (a, b) in enumerate(out)
        ]

    for tile in range(tiles):
        for copy in copies(tile):
            copy.start()
    if following:
        load = pltpu.make_async_copy(wo.at[pl.ds(half, half)], wo_v, sems.at[tiles * 4])
        load.start()
    stat = column(
        jnp.sum(left[tokens:].astype(F32) + right[tokens:].astype(F32), axis=0, keepdims=True)
    )
    left, right = left[:tokens], right[:tokens]
    scale = column(rinv[...])
    share = scale * scale * stat / MODEL_WIDTH
    if following:
        live = live_tokens(meta, tokens)
    stores = []
    for tile in range(tiles):
        for copy in copies(tile):
            copy.wait()
        cols = slice(tile * TILE, (tile + 1) * TILE)
        dnormed = dot(left, wq_v[:half, cols], NN) + dot(right, wq_v[half:, cols], NN)
        upstream = up_v[:, cols].astype(F32)
        if following:
            upstream = jnp.where(live, upstream, 0.0)
        value = upstream + (scale * (gain[:, cols] * dnormed) - h_v[:, cols].astype(F32) * share)
        if following:
            value = jnp.where(meta[INFO] == 1, upstream, value)
        up_v[:, cols] = value.astype(BF)
        store = pltpu.make_async_copy(up_v.at[:, cols], grad.at[:, cols], sems.at[tile * 4])
        store.start()
        stores.append(store)
    if following:
        load.wait()
        o_send[...] = dot(up_v[...], wo_v[...], NT).astype(BF)
    for store in stores:
        store.wait()


def back(meta, rinv, gain, dqs, up, h, wq, wo=None):
    tokens, width = up.shape
    inner = wq.shape[0]
    half = inner // 2
    inputs = [meta, rinv, gain, *dqs, up, h, wq]
    in_specs = [SMEM] + [VMEM] * (2 + len(dqs)) + [ANY] * 3
    out_specs = [ANY]
    out_shape = [jax.ShapeDtypeStruct((tokens, width), BF)]
    scratch = [pltpu.VMEM((inner, width), BF)] + [pltpu.VMEM((tokens, width), BF)] * 2
    if wo is not None:
        inputs.append(wo)
        in_specs.append(ANY)
        out_specs.append(VMEM)
        out_shape.append(jax.ShapeDtypeStruct((tokens, half), BF))
        scratch.append(pltpu.VMEM((half, width), BF))
    return pl.pallas_call(
        functools.partial(back_kernel, wo is not None),
        in_specs=in_specs,
        out_specs=out_specs,
        out_shape=out_shape,
        scratch_shapes=scratch + [pltpu.SemaphoreType.DMA((width // TILE * 4 + 1,))],
        compiler_params=params(),
        cost_estimate=pl.CostEstimate(
            flops=(3 if wo is not None else 2) * tokens * width * inner,
            bytes_accessed=12 << 20,
            transcendentals=0,
        ),
    )(*inputs)


def term_kernel(dkv, w_kv, own, *terms):
    for k in range(4):
        value = dot(dkv[k], w_kv[...], NT)
        if k == 0:
            own[...] = value
        else:
            terms[k - 1][...] = value.astype(BF)


def latent_terms(dkv, w_kv):
    rows, inner = dkv.shape[1:]
    features = w_kv.shape[0]
    tile = features // 3
    result = pl.BlockSpec((rows, tile), lambda i: (0, i))
    return pl.pallas_call(
        term_kernel,
        grid=(features // tile,),
        in_specs=[whole(dkv.shape), pl.BlockSpec((tile, inner), lambda i: (i, 0))],
        out_specs=[result] * 4,
        out_shape=[jax.ShapeDtypeStruct((rows, features), t) for t in (F32, BF, BF, BF)],
        compiler_params=params(),
        cost_estimate=pl.CostEstimate(
            flops=8 * rows * inner * features, bytes_accessed=8 << 20, transcendentals=0
        ),
    )(dkv, w_kv)


def per_device(
    segment_inputs,
    cotangent,
    report_lengths,
    norm_gain,
    attn_gate,
    w_query,
    w_out,
    w_key,
    w_value,
    tiles,
    tile_counts,
    lat_query,
    request_source,
    request_slide,
    cross_pattern,
):
    z, y, core = (lax.axis_index(name) for name in DP)
    me_dp = (z * 4 + y) * 2 + core
    me_mp = lax.axis_index("mp")
    seg = lax.axis_index("segment")
    me_x = me_mp * 2 + seg
    last = seg == 1
    reports = cross_pattern.shape[0]
    wanted = reports * SPR
    h = segment_inputs[0]
    tokens, width = h.shape
    half = 512

    slot = []
    for part in range(4):
        same_seg, same_mp = seg == part // 2, me_mp == part % 2
        slot.append(jnp.where(same_seg, jnp.where(same_mp, 0, 3), jnp.where(same_mp, 1, 2)))
    rows = lax.rem(places(z, y, core) * 32 - me_mp * half + 2 * half, 2 * half)
    info = [seg, me_mp * half, (1 - me_mp) * half]
    meta = jnp.concatenate(
        [rows, jnp.stack(slot + info).astype(jnp.int32), report_lengths, cross_pattern.reshape(-1)]
    )
    order = jnp.stack([me_dp, me_dp + 1 - 2 * core])
    source = request_source.reshape(32, wanted)[order]
    slide = request_slide.reshape(32, wanted)[order]
    source_core = source % 2
    far_z = lax.rem(z - source // 8 + 4, 4)
    far_y = lax.rem(y - source // 2 % 4 + 4, 4)
    first = jnp.where(core == 0, far_y, far_z)
    second = jnp.where(core == 0, far_z, far_y)
    array = jnp.where(source_core == core, second, 4)
    picks = jnp.concatenate([array.reshape(-1), first.reshape(-1), slide.reshape(-1)])

    h_all = lax.all_gather(h, "segment")

    wq_t = w_query[0].T
    block = jnp.concatenate([w_out[0], wq_t], axis=0)
    blocks = gather_chips(block)

    pooled = pool(me_x.reshape(1).astype(jnp.int32), tile_counts.reshape(4), tiles, lat_query)
    lat_blocks = gather_chips(pooled)
    lat_blocks[3], blocks[1], blocks[3] = lax.optimization_barrier(
        (lat_blocks[3], blocks[1], blocks[3])
    )
    near, across = select(picks, lat_blocks)
    crossed = lax.ppermute(across, "core", [(0, 1), (1, 0)])
    is_near = jnp.repeat(source_core[0] == core, LAT)[:, None]
    chosen = jnp.where(is_near, near, crossed)
    latents = jnp.concatenate(
        [chosen] + [lax.ppermute(chosen, X, x_perm(k)) for k in (1, 2, 3)], axis=1
    )
    w_kv = jnp.concatenate([w_key[0], w_value[0]], axis=1)
    w_kv_x = jnp.concatenate(
        [
            lax.dynamic_slice_in_dim(w_kv, lax.rem(me_x - k + 4, 4) * QUARTER, QUARTER, 0)
            for k in range(4)
        ],
        axis=0,
    )
    kv = dot(latents, w_kv_x, NN).astype(BF)
    blocks = blocks + [lax.ppermute(b, "core", [(0, 1), (1, 0)]) for b in blocks]

    wq_t, _ = lax.optimization_barrier((wq_t, lat_blocks[0]))
    wq1 = lax.all_gather(lax.ppermute(wq_t, "segment", [(1, 0)]), DP, axis=0, tiled=True)

    h32 = h.astype(F32)
    partial = jnp.sum(h32 * h32, axis=1)
    squares = partial + lax.ppermute(partial, "mp", [(0, 1), (1, 0)])
    rinv = lax.rsqrt(squares / MODEL_WIDTH + 1e-05)
    gain = norm_gain
    message = lax.ppermute(jnp.concatenate([rinv, gain[0]]), "segment", [(1, 0)])[None]
    rinv1, gain1 = message[:, :tokens], message[:, tokens:]
    normed = (h32 * rinv[:, None] * gain).astype(BF)
    position = jnp.arange(tokens)
    live = position % L < jnp.repeat(report_lengths, L)
    up1 = jnp.where(live[:, None], cotangent, jnp.zeros((), BF))
    rinv = rinv[None]
    gate = jnp.tanh(attn_gate)

    q_send, wq = project(1, meta, normed, blocks)
    q_got = lax.ppermute(q_send, X, SWAP_MP)
    o_send, wo = project(0, meta, up1, blocks)
    o_got = lax.ppermute(o_send, X, LAST_SWAP)
    q_own = dot(normed, wq[:half], NT)
    o_own = dot(up1, wo[:half], NT).astype(BF)
    probs = forward(meta, q_own, q_got, kv)
    dq1, dkv1 = backward(meta, gate, q_own, q_got, o_own, o_got, kv, probs)
    dqs = [lax.ppermute(dq1, X, LAST_TO_SAME), lax.ppermute(dq1, X, LAST_TO_CROSS)]
    up, o_send = back(meta, rinv1, gain1, dqs, cotangent, h_all, wq1, wo)
    o_got = lax.ppermute(o_send, X, FIRST_SWAP)
    o_own = dot(up, wo[:half], NT).astype(BF)
    dq1, dkv1, _ = lax.optimization_barrier((dq1, dkv1, o_send))
    got1 = lax.ppermute(dq1, X, LAST_SWAP)
    own1, *terms = latent_terms(dkv1, w_kv)
    moves = (LAST_TO_SAME, LAST_TO_CROSS, LAST_SWAP)
    got = [lax.ppermute(t, X, p) for t, p in zip(terms, moves)]

    dq0, dkv0 = backward(meta, gate, q_own, q_got, o_own, o_got, kv, probs)
    got0 = lax.ppermute(dq0, X, FIRST_SWAP)
    own0, *terms = latent_terms(dkv0, w_kv)
    moves = (FIRST_TO_SAME, FIRST_TO_CROSS, FIRST_SWAP)
    got += [lax.ppermute(t, X, p) for t, p in zip(terms, moves)]
    (grads,) = back(meta, rinv, gain, [dq1, dq0, got1, got0], up, h, wq)

    latent_grad = jnp.where(last, own1, own0)
    for term in got:
        latent_grad = latent_grad + term.astype(F32)
    return grads[None], latent_grad.reshape(reports, 48, E)


def solution(mesh):
    fine = Mesh(mesh.devices.reshape(2, 4, 4, 2, 2), ("segment", "z", "y", "core", "mp"))
    return jax.shard_map(
        per_device,
        mesh=fine,
        in_specs=(
            P("segment", DP, "mp"),
            P(DP, "mp"),
            P(DP),
            P("segment", "mp"),
            P("segment"),
            P("segment", "mp", DP),
            P("segment", DP, "mp"),
            P("segment", None, "mp"),
            P("segment", None, "mp"),
            P(DP, None, None),
            P(DP, None),
            P(),
            P(),
            P(),
            P(DP, None, None),
        ),
        out_specs=(P("segment", DP, "mp"), P(DP, X, None)),
        check_vma=False,
    )
```

```python
import functools

import jax
import jax.numpy as jnp
from jax import lax
from jax.experimental import pallas as pl
from jax.experimental.pallas import tpu as pltpu
from jax.sharding import Mesh
from jax.sharding import PartitionSpec as P

MODEL_WIDTH = 4096
E = 1536
HEAD = 128
LAT = 32
SPR = 6
L = 128
QBLK = 32
MAXT = 64
QUARTER = E // 4
SCALE = HEAD ** (-0.5)
DP = ("z", "y", "core")
X = ("segment", "mp")
BF = jnp.bfloat16
F32 = jnp.float32
LIMIT = 60 * 1024 * 1024
NT = (((1,), (1,)), ((), ()))
NN = (((1,), (0,)), ((), ()))
TN = (((0,), (0,)), ((), ()))

SWAP_MP = [(0, 1), (1, 0), (2, 3), (3, 2)]
LAST_TO_SAME = [(2, 0), (3, 1)]
LAST_TO_CROSS = [(2, 1), (3, 0)]
LAST_SWAP = [(2, 3), (3, 2)]
FIRST_TO_SAME = [(0, 2), (1, 3)]
FIRST_TO_CROSS = [(0, 3), (1, 2)]
FIRST_SWAP = [(0, 1), (1, 0)]
AT_X = (0, 2, 1, 3)


def x_perm(k):
    return [(AT_X[x], AT_X[(x + k) % 4]) for x in range(4)]


def yz_perm(stage, k):
    pairs = []
    for z in range(4):
        for y in range(4):
            for core in range(2):
                along_y = (core == 0) == (stage == 1)
                to_z = z if along_y else (z + k) % 4
                to_y = (y + k) % 4 if along_y else y
                pairs.append(((z * 4 + y) * 2 + core, (to_z * 4 + to_y) * 2 + core))
    return pairs


def dot(a, b, dims):
    return lax.dot_general(a, b, dims, preferred_element_type=F32)


def params(**kwargs):
    return pltpu.CompilerParams(vmem_limit_bytes=LIMIT, **kwargs)


def whole(shape):
    return pl.BlockSpec(shape, lambda *_: (0,) * len(shape))


SMEM = pl.BlockSpec(memory_space=pltpu.SMEM)
ANY = pl.BlockSpec(memory_space=pl.ANY)
VMEM = pl.BlockSpec(memory_space=pltpu.VMEM)
TILE = 512
ROWS, SLOT, INFO, LENGTHS, PATTERN = 0, 32, 36, 39, 43


def pool_kernel(which, counts, tiles, queries, out):
    heads = [slice(head * HEAD, (head + 1) * HEAD) for head in range(QUARTER // HEAD)]
    pairs = [(slide, cols) for slide in range(4) for cols in heads]
    slot = lax.broadcasted_iota(jnp.int32, (LAT, MAXT), 1)
    tile = [tiles[slide, :, cols] for slide, cols in pairs]
    query = [queries[:, cols] for _, cols in pairs]
    scores = [dot(q, t, NT) * SCALE for q, t in zip(query, tile)]
    scores = [jnp.where(slot < counts[s], x, -1e30) for x, (s, _) in zip(scores, pairs)]
    exps = [jnp.exp(s - jnp.max(s, axis=1, keepdims=True)) for s in scores]
    weights = [(e / jnp.sum(e, axis=1, keepdims=True)).astype(BF) for e in exps]
    pooled = [dot(w, t, NN) for w, t in zip(weights, tile)]
    for (slide, cols), q, p in zip(pairs, query, pooled):
        out[slide * LAT : (slide + 1) * LAT, cols] = (q.astype(F32) + p).astype(BF)


def pool(which, counts, tiles, queries):
    return pl.pallas_call(
        pool_kernel,
        grid_spec=pltpu.PrefetchScalarGridSpec(
            num_scalar_prefetch=2,
            grid=(1,),
            in_specs=[
                pl.BlockSpec((4, MAXT, QUARTER), lambda i, which, counts: (0, 0, which[0])),
                pl.BlockSpec((LAT, QUARTER), lambda i, which, counts: (0, which[0])),
            ],
            out_specs=pl.BlockSpec((4 * LAT, QUARTER), lambda i, which, counts: (0, 0)),
        ),
        out_shape=jax.ShapeDtypeStruct((4 * LAT, QUARTER), BF),
        compiler_params=params(),
    )(which, counts, tiles, queries)


def gather_chips(blocks):
    first = [[lax.ppermute(b, DP, yz_perm(1, k)) for k in (1, 2, 3)] for b in blocks]
    first = lax.optimization_barrier(first)
    bundles = [jnp.stack([b, *parts]) for b, parts in zip(blocks, first)]
    bundles = lax.optimization_barrier(bundles)
    return [[b] + [lax.ppermute(b, DP, yz_perm(2, k)) for k in (1, 2, 3)] for b in bundles]


def places(z, y, core):
    table = []
    for a in range(8):
        c = core if a < 4 else 1 - core
        for k in range(4):
            j = a % 4
            at_z = lax.rem(z - jnp.where(c == 0, j, k) + 4, 4)
            at_y = lax.rem(y - jnp.where(c == 0, k, j) + 4, 4)
            table.append((at_z * 4 + at_y) * 2 + c)
    return jnp.stack(table).astype(jnp.int32)


def select_kernel(wanted, picks, *refs):
    ins, outs, sems = refs[:4], refs[4:6], refs[6]

    def copy(a, which, i):
        at = which * wanted + i
        slide = pl.multiple_of(picks[4 * wanted + at] * LAT, LAT)
        return pltpu.make_async_copy(
            ins[a].at[picks[2 * wanted + at], pl.ds(slide, LAT)],
            outs[which].at[pl.ds(i * LAT, LAT)],
            sems.at[at],
        )

    for act in ("start", "wait"):
        for which in range(2):
            for i in range(wanted):
                for a in range(4):

                    @pl.when(picks[which * wanted + i] == a)
                    def _():
                        getattr(copy(a, which, i), act)()


def select(picks, blocks):
    wanted = picks.shape[0] // 6
    out = jax.ShapeDtypeStruct((wanted * LAT, QUARTER), BF)
    return pl.pallas_call(
        functools.partial(select_kernel, wanted),
        in_specs=[SMEM] + [ANY] * 4,
        out_specs=[VMEM, VMEM],
        out_shape=[out, out],
        scratch_shapes=[pltpu.SemaphoreType.DMA((2 * wanted,))],
        compiler_params=params(),
    )(picks, *blocks)


def column(row):
    return jnp.broadcast_to(row, (HEAD, row.shape[1])).T[:, :1]


def live_tokens(meta, tokens):
    index = lax.broadcasted_iota(jnp.int32, (tokens, 1), 0)
    parts = [index[r * L : (r + 1) * L] < r * L + meta[LENGTHS + r] for r in range(tokens // L)]
    return jnp.concatenate([p.astype(F32) for p in parts], axis=0) > 0


def project_kernel(kind, meta, x, *refs):
    ins, (send, weight), (w_v, x_v, sems) = refs[:8], refs[8:10], refs[10:]
    load = pltpu.make_async_copy(x, x_v, sems.at[2])
    load.start()
    half = w_v.shape[0] // 2
    for a in range(8):
        for k in range(4):
            at = pl.multiple_of(meta[ROWS + a * 4 + k], 32)
            pltpu.make_async_copy(
                ins[a].at[k, pl.ds(kind * 32, 32)], w_v.at[pl.ds(at, 32)], sems.at[at // half]
            ).start()

    def group(part):
        return w_v.at[pl.ds(part * half, half)]

    load.wait()
    pltpu.make_async_copy(group(1), group(1), sems.at[1]).wait()
    store1 = pltpu.make_async_copy(group(1), weight.at[pl.ds(half, half)], sems.at[1])
    store1.start()
    send[...] = dot(x_v[...], w_v[half:], NT).astype(BF)
    pltpu.make_async_copy(group(0), group(0), sems.at[0]).wait()
    store0 = pltpu.make_async_copy(group(0), weight.at[pl.ds(0, half)], sems.at[0])
    store0.start()
    store1.wait()
    store0.wait()


def project(kind, meta, x, blocks):
    tokens, width = x.shape
    inner = 32 * 32
    return pl.pallas_call(
        functools.partial(project_kernel, kind),
        in_specs=[SMEM, ANY] + [ANY] * 8,
        out_specs=[VMEM, ANY],
        out_shape=[
            jax.ShapeDtypeStruct((tokens, inner // 2), BF),
            jax.ShapeDtypeStruct((inner, width), BF),
        ],
        scratch_shapes=[
            pltpu.VMEM((inner, width), BF),
            pltpu.VMEM((tokens, width), BF),
            pltpu.SemaphoreType.DMA((3,)),
        ],
        compiler_params=params(),
        cost_estimate=pl.CostEstimate(
            flops=tokens * width * inner, bytes_accessed=12 << 20, transcendentals=0
        ),
    )(meta, x, *blocks)


def forward_kernel(meta, q_own, q_got, keys, probs):
    report = pl.program_id(0)
    span = keys.shape[0]
    slide = lax.broadcasted_iota(jnp.int32, (QBLK, span), 1) // LAT
    masks = []
    for block in range(L // QBLK):
        seen = jnp.zeros((QBLK, span), jnp.int32)
        for j in range(SPR):
            at = PATTERN + (report * (L // QBLK) + block) * SPR + j
            seen = jnp.where(slide == j, meta[at], seen)
        masks.append(seen)
    mask = jnp.concatenate(masks, axis=0) == 1
    heads = [slice(head * HEAD, (head + 1) * HEAD) for head in range(probs.shape[0])]
    qb = [(q_own[:, c] + q_got[:, c].astype(F32)).astype(BF) for c in heads]
    scores = [dot(q, keys[:, c], NT) * SCALE for q, c in zip(qb, heads)]
    scores = [jnp.where(mask, s, -1e30) for s in scores]
    exps = [jnp.exp(s - jnp.max(s, axis=1, keepdims=True)) for s in scores]
    totals = [jnp.sum(e, axis=1, keepdims=True) for e in exps]
    for head, (e, total) in enumerate(zip(exps, totals)):
        probs[head] = e / total


def forward(meta, q_own, q_got, kv):
    tokens, local = q_own.shape
    reports = tokens // L
    span = kv.shape[0] // reports
    heads = local // HEAD
    token = pl.BlockSpec((L, local), lambda i: (i, 0))
    return pl.pallas_call(
        forward_kernel,
        grid=(reports,),
        in_specs=[SMEM, token, token, pl.BlockSpec((span, local), lambda i: (i, 0))],
        out_specs=pl.BlockSpec((heads, L, span), lambda i: (0, i, 0)),
        out_shape=jax.ShapeDtypeStruct((heads, tokens, span), F32),
        compiler_params=params(),
        cost_estimate=pl.CostEstimate(
            flops=2 * tokens * span * local, bytes_accessed=6 << 20, transcendentals=tokens * span * 4
        ),
    )(meta, q_own, q_got, kv)


def backward_kernel(meta, gate, q_own, q_got, o_own, o_got, keys, vals, probs, dq_out, dkv_out):
    report = pl.program_id(0)
    rows = pl.ds(pl.multiple_of(report * L, L), L)
    local = q_own.shape[1]
    heads = [slice(head * HEAD, (head + 1) * HEAD) for head in range(local // HEAD)]
    og = [
        (gate[0] * (o_own[:, c].astype(F32) + o_got[:, c].astype(F32))).astype(BF) for c in heads
    ]
    dprob = [dot(g, vals[:, c], NT) for g, c in zip(og, heads)]
    prob = [probs[head] for head in range(len(heads))]
    rowdot = [jnp.sum(p * d, axis=1, keepdims=True) for p, d in zip(prob, dprob)]
    dscore = [(p * (d - r)).astype(BF) for p, d, r in zip(prob, dprob, rowdot)]
    dq = [(dot(d, keys[:, c], NN) * SCALE).astype(BF) for d, c in zip(dscore, heads)]
    q = [q_own[:, c] + q_got[:, c].astype(F32) for c in heads]
    dkey = [(dot(d, x.astype(BF), TN) * SCALE).astype(BF) for d, x in zip(dscore, q)]
    dval = [dot(p.astype(BF), g, TN).astype(BF) for p, g in zip(prob, og)]
    stat = jnp.zeros((L, HEAD), F32)
    for c, d, x in zip(heads, dq, q):
        dq_out[rows, c] = d
        stat += x * d.astype(F32)
    into = pl.ds(pl.multiple_of(report * 48, 16), 48)
    both = jnp.concatenate(dkey + dval, axis=1)
    for part in range(4):
        dkv_out[meta[SLOT + part], into, :] = both[part * 48 : (part + 1) * 48]
    total = jnp.sum(stat.T, axis=0, keepdims=True)
    high = total.astype(BF)
    rest = total - high.astype(F32)
    low = rest.astype(BF)
    lower = (rest - low.astype(F32)).astype(BF)
    zero = jnp.zeros((13, L), F32)
    extra = jnp.concatenate([high.astype(F32), low.astype(F32), lower.astype(F32), zero], axis=0)
    dq_out[4 * L : 4 * L + 16, rows] = extra.astype(BF)


def backward(meta, gate, q_own, q_got, o_own, o_got, kv, probs):
    tokens, local = q_own.shape
    reports = tokens // L
    heads, _, span = probs.shape
    token = pl.BlockSpec((L, local), lambda i: (i, 0))
    return pl.pallas_call(
        backward_kernel,
        grid=(reports,),
        in_specs=[SMEM, SMEM, token, token, token, token]
        + [
            pl.BlockSpec((span, local), lambda i: (i, 0)),
            pl.BlockSpec((span, local), lambda i: (i, 1)),
            pl.BlockSpec((heads, L, span), lambda i: (0, i, 0)),
        ],
        out_specs=[whole((tokens + 16, local)), whole((4, reports * 48, 2 * local))],
        out_shape=[
            jax.ShapeDtypeStruct((tokens + 16, local), BF),
            jax.ShapeDtypeStruct((4, reports * 48, 2 * local), BF),
        ],
        compiler_params=params(),
        cost_estimate=pl.CostEstimate(
            flops=8 * tokens * span * local, bytes_accessed=8 << 20, transcendentals=0
        ),
    )(meta, gate, q_own, q_got, o_own, o_got, kv, kv, probs)


def back_kernel(following, meta, rinv, gain, *refs):
    if following:
        dq_own, dq_got, up, h, wq, wo, grad, o_send, wq_v, up_v, h_v, wo_v, sems = refs
        left, right = dq_own[...], dq_got[...]
    else:
        dq1, dq0, got1, got0, up, h, wq, grad, wq_v, up_v, h_v, sems = refs
        left = jnp.where(meta[INFO] == 1, dq1[...].astype(F32), dq0[...].astype(F32)).astype(BF)
        right = (got1[...].astype(F32) + got0[...].astype(F32)).astype(BF)
    if len(h.shape) == 3:
        h = h.at[1]
    inner, width = wq_v.shape
    half = inner // 2
    tokens = up_v.shape[0]
    tiles = width // TILE

    def copies(tile):
        cols = slice(tile * TILE, (tile + 1) * TILE)
        out = []
        for part in range(2):
            at = pl.multiple_of(meta[INFO + 1 + part], half) if following else part * half
            into = slice(part * half, (part + 1) * half)
            out.append((wq.at[pl.ds(at, half), cols], wq_v.at[into, cols]))
        out.append((up.at[:, cols], up_v.at[:, cols]))
        out.append((h.at[:, cols], h_v.at[:, cols]))
        return [
            pltpu.make_async_copy(a, b, sems.at[tile * 4 + i]) for i, (a, b) in enumerate(out)
        ]

    for tile in range(tiles):
        for copy in copies(tile):
            copy.start()
    if following:
        load = pltpu.make_async_copy(wo.at[pl.ds(half, half)], wo_v, sems.at[tiles * 4])
        load.start()
    stat = column(
        jnp.sum(left[tokens:].astype(F32) + right[tokens:].astype(F32), axis=0, keepdims=True)
    )
    dq = jnp.concatenate([left[:tokens], right[:tokens]], axis=1)
    scale = column(rinv[...])
    share = scale * scale * stat / MODEL_WIDTH
    if following:
        live = live_tokens(meta, tokens)
    stores = []
    for tile in range(tiles):
        for copy in copies(tile):
            copy.wait()
        cols = slice(tile * TILE, (tile + 1) * TILE)
        dnormed = dot(dq, wq_v[:, cols], NN)
        upstream = up_v[:, cols].astype(F32)
        if following:
            upstream = jnp.where(live, upstream, 0.0)
        value = upstream + (scale * (gain[:, cols] * dnormed) - h_v[:, cols].astype(F32) * share)
        if following:
            value = jnp.where(meta[INFO] == 1, upstream, value)
        up_v[:, cols] = value.astype(BF)
        store = pltpu.make_async_copy(up_v.at[:, cols], grad.at[:, cols], sems.at[tile * 4])
        store.start()
        stores.append(store)
    if following:
        load.wait()
        o_send[...] = dot(up_v[...], wo_v[...], NT).astype(BF)
    for store in stores:
        store.wait()


def back(meta, rinv, gain, dqs, up, h, wq, wo=None):
    tokens, width = up.shape
    inner = wq.shape[0]
    half = inner // 2
    inputs = [meta, rinv, gain, *dqs, up, h, wq]
    in_specs = [SMEM] + [VMEM] * (2 + len(dqs)) + [ANY] * 3
    out_specs = [ANY]
    out_shape = [jax.ShapeDtypeStruct((tokens, width), BF)]
    scratch = [pltpu.VMEM((inner, width), BF)] + [pltpu.VMEM((tokens, width), BF)] * 2
    if wo is not None:
        inputs.append(wo)
        in_specs.append(ANY)
        out_specs.append(VMEM)
        out_shape.append(jax.ShapeDtypeStruct((tokens, half), BF))
        scratch.append(pltpu.VMEM((half, width), BF))
    return pl.pallas_call(
        functools.partial(back_kernel, wo is not None),
        in_specs=in_specs,
        out_specs=out_specs,
        out_shape=out_shape,
        scratch_shapes=scratch + [pltpu.SemaphoreType.DMA((width // TILE * 4 + 1,))],
        compiler_params=params(),
        cost_estimate=pl.CostEstimate(
            flops=(3 if wo is not None else 2) * tokens * width * inner,
            bytes_accessed=12 << 20,
            transcendentals=0,
        ),
    )(*inputs)


def term_kernel(dkv, w_kv, own, *terms):
    rows = own.shape[0]
    value = dot(dkv[...].reshape(4 * rows, dkv.shape[2]), w_kv[...], NT)
    own[...] = value[:rows]
    for k, term in enumerate(terms, 1):
        term[...] = value[k * rows : (k + 1) * rows].astype(BF)


def latent_terms(dkv, w_kv):
    rows, inner = dkv.shape[1:]
    features = w_kv.shape[0]
    tile = features // 3
    result = pl.BlockSpec((rows, tile), lambda i: (0, i))
    return pl.pallas_call(
        term_kernel,
        grid=(features // tile,),
        in_specs=[whole(dkv.shape), pl.BlockSpec((tile, inner), lambda i: (i, 0))],
        out_specs=[result] * 4,
        out_shape=[jax.ShapeDtypeStruct((rows, features), t) for t in (F32, BF, BF, BF)],
        compiler_params=params(),
        cost_estimate=pl.CostEstimate(
            flops=8 * rows * inner * features, bytes_accessed=8 << 20, transcendentals=0
        ),
    )(dkv, w_kv)


def per_device(
    segment_inputs,
    cotangent,
    report_lengths,
    norm_gain,
    attn_gate,
    w_query,
    w_out,
    w_key,
    w_value,
    tiles,
    tile_counts,
    lat_query,
    request_source,
    request_slide,
    cross_pattern,
):
    z, y, core = (lax.axis_index(name) for name in DP)
    me_dp = (z * 4 + y) * 2 + core
    me_mp = lax.axis_index("mp")
    seg = lax.axis_index("segment")
    me_x = me_mp * 2 + seg
    last = seg == 1
    reports = cross_pattern.shape[0]
    wanted = reports * SPR
    h = segment_inputs[0]
    tokens, width = h.shape
    half = 512

    slot = []
    for part in range(4):
        same_seg, same_mp = seg == part // 2, me_mp == part % 2
        slot.append(jnp.where(same_seg, jnp.where(same_mp, 0, 3), jnp.where(same_mp, 1, 2)))
    rows = lax.rem(places(z, y, core) * 32 - me_mp * half + 2 * half, 2 * half)
    info = [seg, me_mp * half, (1 - me_mp) * half]
    meta = jnp.concatenate(
        [rows, jnp.stack(slot + info).astype(jnp.int32), report_lengths, cross_pattern.reshape(-1)]
    )
    order = jnp.stack([me_dp, me_dp + 1 - 2 * core])
    source = request_source.reshape(32, wanted)[order]
    slide = request_slide.reshape(32, wanted)[order]
    source_core = source % 2
    far_z = lax.rem(z - source // 8 + 4, 4)
    far_y = lax.rem(y - source // 2 % 4 + 4, 4)
    first = jnp.where(core == 0, far_y, far_z)
    second = jnp.where(core == 0, far_z, far_y)
    array = jnp.where(source_core == core, second, 4)
    picks = jnp.concatenate([array.reshape(-1), first.reshape(-1), slide.reshape(-1)])

    h_all = lax.all_gather(h, "segment")

    wq_t = w_query[0].T
    pooled = pool(me_x.reshape(1).astype(jnp.int32), tile_counts.reshape(4), tiles, lat_query)
    lat_blocks, blocks = gather_chips([pooled, jnp.concatenate([w_out[0], wq_t], axis=0)])

    h32 = h.astype(F32)
    partial = jnp.sum(h32 * h32, axis=1)
    squares = partial + lax.ppermute(partial, "mp", [(0, 1), (1, 0)])
    rinv = lax.rsqrt(squares / MODEL_WIDTH + 1e-05)
    gain = norm_gain
    message = lax.ppermute(jnp.concatenate([rinv, gain[0]]), "segment", [(1, 0)])[None]
    rinv1, gain1 = message[:, :tokens], message[:, tokens:]
    normed = (h32 * rinv[:, None] * gain).astype(BF)
    position = jnp.arange(tokens)
    live = position % L < jnp.repeat(report_lengths, L)
    up1 = jnp.where(live[:, None], cotangent, jnp.zeros((), BF))
    rinv = rinv[None]
    gate = jnp.tanh(attn_gate)
    w_kv = jnp.concatenate([w_key[0], w_value[0]], axis=1)
    w_kv_x = jnp.concatenate(
        [
            lax.dynamic_slice_in_dim(w_kv, lax.rem(me_x - k + 4, 4) * QUARTER, QUARTER, 0)
            for k in range(4)
        ],
        axis=0,
    )

    wq_t, _ = lax.optimization_barrier((wq_t, blocks[0]))
    lat_blocks[0], wq1 = lax.optimization_barrier(
        (lat_blocks[0], lax.ppermute(wq_t, "segment", [(1, 0)]))
    )
    wq1 = lax.all_gather(wq1, DP, axis=0, tiled=True)

    near, across = select(picks, lat_blocks)
    near, across, blocks[1], blocks[3] = lax.optimization_barrier(
        (near, across, blocks[1], blocks[3])
    )
    crossed = lax.ppermute(across, "core", [(0, 1), (1, 0)])
    is_near = jnp.repeat(source_core[0] == core, LAT)[:, None]
    chosen = jnp.where(is_near, near, crossed)
    chosen, blocks[2], normed, up1, meta, w_kv, w_kv_x = lax.optimization_barrier(
        (chosen, blocks[2], normed, up1, meta, w_kv, w_kv_x)
    )
    latents = [chosen] + [lax.ppermute(chosen, X, x_perm(k)) for k in (1, 2, 3)]
    blocks = blocks + [lax.ppermute(b, "core", [(0, 1), (1, 0)]) for b in blocks]


    q_send, wq = project(1, meta, normed, blocks)
    q_got = lax.ppermute(q_send, X, SWAP_MP)
    o_send, wo = project(0, meta, up1, blocks)
    o_got = lax.ppermute(o_send, X, LAST_SWAP)
    q_own = dot(normed, wq[:half], NT)
    q_own, rinv1, gain1 = lax.optimization_barrier((q_own, rinv1, gain1))
    o_own = dot(up1, wo[:half], NT).astype(BF)
    latents, o_send = lax.optimization_barrier((latents, o_send))
    kv = dot(jnp.concatenate(latents, axis=1), w_kv_x, NN).astype(BF)
    probs = forward(meta, q_own, q_got, kv)
    dq1, dkv1 = backward(meta, gate, q_own, q_got, o_own, o_got, kv, probs)
    dqs = [lax.ppermute(dq1, X, LAST_TO_SAME), lax.ppermute(dq1, X, LAST_TO_CROSS)]
    up, o_send = back(meta, rinv1, gain1, dqs, cotangent, h_all, wq1, wo)
    o_got = lax.ppermute(o_send, X, FIRST_SWAP)
    o_own = dot(up, wo[:half], NT).astype(BF)
    dq1, dkv1, _ = lax.optimization_barrier((dq1, dkv1, o_send))
    got1 = lax.ppermute(dq1, X, LAST_SWAP)
    own1, *terms = latent_terms(dkv1, w_kv)
    moves = (LAST_TO_SAME, LAST_TO_CROSS, LAST_SWAP)
    got = [lax.ppermute(t, X, p) for t, p in zip(terms, moves)]
    received = jnp.where(last, own1, 0.0)
    for term in got:
        received = received + term.astype(F32)

    dq0, dkv0 = backward(meta, gate, q_own, q_got, o_own, o_got, kv, probs)
    got0 = lax.ppermute(dq0, X, FIRST_SWAP)
    own0, *terms = latent_terms(dkv0, w_kv)
    terms, received = lax.optimization_barrier((terms, received))
    moves = (FIRST_TO_SAME, FIRST_TO_CROSS, FIRST_SWAP)
    got = [lax.ppermute(t, X, p) for t, p in zip(terms, moves)]
    (grads,) = back(meta, rinv, gain, [dq1, dq0, got1, got0], up, h, wq)

    latent_grad = received + jnp.where(last, 0.0, own0)
    for term in got:
        latent_grad = latent_grad + term.astype(F32)
    return grads[None], latent_grad.reshape(reports, 48, E)


def solution(mesh):
    fine = Mesh(mesh.devices.reshape(2, 4, 4, 2, 2), ("segment", "z", "y", "core", "mp"))
    return jax.shard_map(
        per_device,
        mesh=fine,
        in_specs=(
            P("segment", DP, "mp"),
            P(DP, "mp"),
            P(DP),
            P("segment", "mp"),
            P("segment"),
            P("segment", "mp", DP),
            P("segment", DP, "mp"),
            P("segment", None, "mp"),
            P("segment", None, "mp"),
            P(DP, None, None),
            P(DP, None),
            P(),
            P(),
            P(),
            P(DP, None, None),
        ),
        out_specs=(P("segment", DP, "mp"), P(DP, X, None)),
        check_vma=False,
    )
```

```python
import functools

import jax
import jax.numpy as jnp
from jax import lax
from jax.experimental import pallas as pl
from jax.experimental.pallas import tpu as pltpu
from jax.sharding import Mesh
from jax.sharding import PartitionSpec as P

MODEL_WIDTH = 4096
E = 1536
HEAD = 128
LAT = 32
SPR = 6
L = 128
QBLK = 32
MAXT = 64
SCALE = HEAD ** (-0.5)
DP = ("z", "y", "core")
X = ("segment", "mp")
BF = jnp.bfloat16
F32 = jnp.float32
LIMIT = 60 * 1024 * 1024
NT = (((1,), (1,)), ((), ()))
NN = (((1,), (0,)), ((), ()))
TN = (((0,), (0,)), ((), ()))

SWAP_MP = [(0, 1), (1, 0), (2, 3), (3, 2)]
LAST_TO_SAME = [(2, 0), (3, 1)]
LAST_TO_CROSS = [(2, 1), (3, 0)]
LAST_SWAP = [(2, 3), (3, 2)]
FIRST_TO_SAME = [(0, 2), (1, 3)]
FIRST_TO_CROSS = [(0, 3), (1, 2)]
FIRST_SWAP = [(0, 1), (1, 0)]


def yz_perm(stage, k):
    pairs = []
    for z in range(4):
        for y in range(4):
            for core in range(2):
                along_y = (core == 0) == (stage == 1)
                to_z = z if along_y else (z + k) % 4
                to_y = (y + k) % 4 if along_y else y
                pairs.append(((z * 4 + y) * 2 + core, (to_z * 4 + to_y) * 2 + core))
    return pairs


def dot(a, b, dims):
    return lax.dot_general(a, b, dims, preferred_element_type=F32)


def params(**kwargs):
    return pltpu.CompilerParams(vmem_limit_bytes=LIMIT, **kwargs)


def whole(shape):
    return pl.BlockSpec(shape, lambda *_: (0,) * len(shape))


SMEM = pl.BlockSpec(memory_space=pltpu.SMEM)
ANY = pl.BlockSpec(memory_space=pl.ANY)
VMEM = pl.BlockSpec(memory_space=pltpu.VMEM)
TILE = 512
ROWS, SLOT, INFO, LENGTHS, PATTERN, PICKS = 0, 32, 36, 39, 43, 139
ARRAYS = ((0, (0, 1, 2, 3)), (1, (0, 1, 2, 3)), (3, (0, 1, 2, 3)), (2, (0, 1)), (2, (2, 3)))


def block_kernel(counts, tiles, queries, w_out, w_query, w_key, w_value, out, w_v, latents, sems):
    loads = [
        pltpu.make_async_copy(w, w_v.at[i], sems.at[i]) for i, w in enumerate((w_key, w_value))
    ]
    for load in loads:
        load.start()
    out[:32] = w_out[...]
    out[32:64] = w_query[...]
    heads = [slice(head * HEAD, (head + 1) * HEAD) for head in range(E // HEAD)]
    slot = lax.broadcasted_iota(jnp.int32, (LAT, MAXT), 1)
    for slide in range(tiles.shape[0]):
        tile = [tiles[slide, :, cols] for cols in heads]
        query = [queries[:, cols] for cols in heads]
        scores = [dot(q, t, NT) * SCALE for q, t in zip(query, tile)]
        scores = [jnp.where(slot < counts[slide], x, -1e30) for x in scores]
        exps = [jnp.exp(s - jnp.max(s, axis=1, keepdims=True)) for s in scores]
        weights = [(e / jnp.sum(e, axis=1, keepdims=True)).astype(BF) for e in exps]
        pooled = [dot(w, t, NN) for w, t in zip(weights, tile)]
        for cols, q, p in zip(heads, query, pooled):
            latents[slide * LAT : (slide + 1) * LAT, cols] = (q.astype(F32) + p).astype(BF)
    for i, load in enumerate(loads):
        load.wait()
        value = dot(latents[...], w_v[i], NN).astype(BF)
        half = value.shape[1]
        for slide in range(tiles.shape[0]):
            at = 64 + slide // 2 * LAT
            col = (slide % 2 * 2 + i) * half
            out[at : at + LAT, col : col + half] = value[slide * LAT : (slide + 1) * LAT]


def make_block(counts, tiles, queries, w_out, w_query, w_key, w_value):
    slides = tiles.shape[0]
    return pl.pallas_call(
        block_kernel,
        in_specs=[SMEM] + [VMEM] * 4 + [ANY] * 2,
        out_specs=VMEM,
        out_shape=jax.ShapeDtypeStruct((64 + slides // 2 * LAT, w_out.shape[1]), BF),
        scratch_shapes=[
            pltpu.VMEM((2,) + w_key.shape, BF),
            pltpu.VMEM((slides * LAT, E), BF),
            pltpu.SemaphoreType.DMA((2,)),
        ],
        compiler_params=params(),
    )(counts, tiles, queries, w_out, w_query, w_key, w_value)


def gather_chips(block):
    first = [lax.ppermute(block, DP, yz_perm(1, k)) for k in (1, 2, 3)]
    bundle = jnp.stack([block, *first])
    one = lax.ppermute(bundle, DP, yz_perm(2, 1))
    three = lax.ppermute(bundle, DP, yz_perm(2, 3))
    two = lax.ppermute(one[:2], DP, yz_perm(2, 1)), lax.ppermute(three[2:], DP, yz_perm(2, 3))
    return [bundle, one, three, *two]


def places(z, y, core):
    table = []
    for c in (core, 1 - core):
        for j, blocks in ARRAYS:
            for k in blocks:
                at_z = lax.rem(z - jnp.where(c == 0, j, k) + 4, 4)
                at_y = lax.rem(y - jnp.where(c == 0, k, j) + 4, 4)
                table.append((at_z * 4 + at_y) * 2 + c)
    return jnp.stack(table).astype(jnp.int32)


def column(row):
    return jnp.broadcast_to(row, (HEAD, row.shape[1])).T[:, :1]


def live_tokens(meta, tokens):
    index = lax.broadcasted_iota(jnp.int32, (tokens, 1), 0)
    parts = [index[r * L : (r + 1) * L] < r * L + meta[LENGTHS + r] for r in range(tokens // L)]
    return jnp.concatenate([p.astype(F32) for p in parts], axis=0) > 0


def project_kernel(kind, part, meta, x, *refs):
    ins, (out, weight), (w_v, x_v, sems) = refs[:10], refs[10:12], refs[12:]
    load = pltpu.make_async_copy(x, x_v, sems.at[1])
    load.start()
    half = w_v.shape[0]
    index = 0
    for a in range(10):
        for k in range(len(ARRAYS[a % 5][1])):
            at = pl.multiple_of(meta[ROWS + index] - part * half, 32)
            index += 1

            @pl.when((at >= 0) & (at < half))
            def _():
                pltpu.make_async_copy(
                    ins[a].at[k, pl.ds(kind * 32, 32)], w_v.at[pl.ds(at, 32)], sems.at[0]
                ).start()

    load.wait()
    pltpu.make_async_copy(w_v, w_v, sems.at[0]).wait()
    store = pltpu.make_async_copy(w_v, weight, sems.at[0])
    store.start()
    out[...] = dot(x_v[...], w_v[...], NT).astype(out.dtype)
    store.wait()


def project(kind, part, dtype, meta, x, blocks):
    tokens, width = x.shape
    half = 512
    return pl.pallas_call(
        functools.partial(project_kernel, kind, part),
        in_specs=[SMEM, ANY] + [ANY] * 10,
        out_specs=[VMEM, ANY],
        out_shape=[
            jax.ShapeDtypeStruct((tokens, half), dtype),
            jax.ShapeDtypeStruct((half, width), BF),
        ],
        scratch_shapes=[
            pltpu.VMEM((half, width), BF),
            pltpu.VMEM((tokens, width), BF),
            pltpu.SemaphoreType.DMA((2,)),
        ],
        compiler_params=params(),
        cost_estimate=pl.CostEstimate(
            flops=2 * tokens * width * half, bytes_accessed=7 << 20, transcendentals=0
        ),
    )(meta, x, *blocks)


def select_kernel(wanted, meta, *refs):
    ins, out, sems = refs[:10], refs[10], refs[11]
    width = out.shape[1]
    for i in range(wanted):
        block = meta[PICKS + wanted + i]
        slide = meta[PICKS + 2 * wanted + i]
        rows = pl.ds(pl.multiple_of(64 + slide // 2 * LAT, LAT), LAT)
        cols = pl.ds(pl.multiple_of(slide % 2 * width, width), width)
        for a in range(10):

            @pl.when(meta[PICKS + i] == a)
            def _():
                pltpu.make_async_copy(
                    ins[a].at[block, rows, cols], out.at[pl.ds(i * LAT, LAT)], sems.at[0]
                ).start()

    pltpu.make_async_copy(out, out, sems.at[0]).wait()


def select(wanted, meta, blocks):
    return pl.pallas_call(
        functools.partial(select_kernel, wanted),
        in_specs=[SMEM] + [ANY] * 10,
        out_specs=VMEM,
        out_shape=jax.ShapeDtypeStruct((wanted * LAT, 1024), BF),
        scratch_shapes=[pltpu.SemaphoreType.DMA((1,))],
        compiler_params=params(),
        cost_estimate=pl.CostEstimate(flops=0, bytes_accessed=3 << 20, transcendentals=0),
    )(meta, *blocks)


def forward_kernel(meta, q_own, q_got, keys, probs):
    report = pl.program_id(0)
    span = keys.shape[0]
    slide = lax.broadcasted_iota(jnp.int32, (QBLK, span), 1) // LAT
    masks = []
    for block in range(L // QBLK):
        seen = jnp.zeros((QBLK, span), jnp.int32)
        for j in range(SPR):
            at = PATTERN + (report * (L // QBLK) + block) * SPR + j
            seen = jnp.where(slide == j, meta[at], seen)
        masks.append(seen)
    mask = jnp.concatenate(masks, axis=0) == 1
    heads = [slice(head * HEAD, (head + 1) * HEAD) for head in range(probs.shape[0])]
    qb = [(q_own[:, c] + q_got[:, c].astype(F32)).astype(BF) for c in heads]
    scores = [dot(q, keys[:, c], NT) * SCALE for q, c in zip(qb, heads)]
    scores = [jnp.where(mask, s, -1e30) for s in scores]
    exps = [jnp.exp(s - jnp.max(s, axis=1, keepdims=True)) for s in scores]
    totals = [jnp.sum(e, axis=1, keepdims=True) for e in exps]
    for head, (e, total) in enumerate(zip(exps, totals)):
        probs[head] = e / total


def forward(meta, q_own, q_got, kv):
    tokens, local = q_own.shape
    reports = tokens // L
    span = kv.shape[0] // reports
    heads = local // HEAD
    token = pl.BlockSpec((L, local), lambda i: (i, 0))
    return pl.pallas_call(
        forward_kernel,
        grid=(reports,),
        in_specs=[SMEM, token, token, pl.BlockSpec((span, local), lambda i: (i, 0))],
        out_specs=pl.BlockSpec((heads, L, span), lambda i: (0, i, 0)),
        out_shape=jax.ShapeDtypeStruct((heads, tokens, span), F32),
        compiler_params=params(),
        cost_estimate=pl.CostEstimate(
            flops=2 * tokens * span * local, bytes_accessed=6 << 20, transcendentals=tokens * span * 4
        ),
    )(meta, q_own, q_got, kv)


def backward_kernel(meta, gate, q_own, q_got, o_own, o_got, keys, vals, probs, dq_out, dkv_out):
    report = pl.program_id(0)
    rows = pl.ds(pl.multiple_of(report * L, L), L)
    local = q_own.shape[1]
    heads = [slice(head * HEAD, (head + 1) * HEAD) for head in range(local // HEAD)]
    og = [
        (gate[0] * (o_own[:, c].astype(F32) + o_got[:, c].astype(F32))).astype(BF) for c in heads
    ]
    dprob = [dot(g, vals[:, c], NT) for g, c in zip(og, heads)]
    prob = [probs[head] for head in range(len(heads))]
    rowdot = [jnp.sum(p * d, axis=1, keepdims=True) for p, d in zip(prob, dprob)]
    dscore = [(p * (d - r)).astype(BF) for p, d, r in zip(prob, dprob, rowdot)]
    dq = [(dot(d, keys[:, c], NN) * SCALE).astype(BF) for d, c in zip(dscore, heads)]
    q = [q_own[:, c] + q_got[:, c].astype(F32) for c in heads]
    dkey = [(dot(d, x.astype(BF), TN) * SCALE).astype(BF) for d, x in zip(dscore, q)]
    dval = [dot(p.astype(BF), g, TN).astype(BF) for p, g in zip(prob, og)]
    stat = jnp.zeros((L, HEAD), F32)
    for c, d, x in zip(heads, dq, q):
        dq_out[rows, c] = d
        stat += x * d.astype(F32)
    into = pl.ds(pl.multiple_of(report * 48, 16), 48)
    both = jnp.concatenate(dkey + dval, axis=1)
    for part in range(4):
        dkv_out[meta[SLOT + part], into, :] = both[part * 48 : (part + 1) * 48]
    total = jnp.sum(stat.T, axis=0, keepdims=True)
    high = total.astype(BF)
    rest = total - high.astype(F32)
    low = rest.astype(BF)
    lower = (rest - low.astype(F32)).astype(BF)
    zero = jnp.zeros((13, L), F32)
    extra = jnp.concatenate([high.astype(F32), low.astype(F32), lower.astype(F32), zero], axis=0)
    dq_out[4 * L : 4 * L + 16, rows] = extra.astype(BF)


def backward(meta, gate, q_own, q_got, o_own, o_got, kv, probs):
    tokens, local = q_own.shape
    reports = tokens // L
    heads, _, span = probs.shape
    token = pl.BlockSpec((L, local), lambda i: (i, 0))
    return pl.pallas_call(
        backward_kernel,
        grid=(reports,),
        in_specs=[SMEM, SMEM, token, token, token, token]
        + [
            pl.BlockSpec((span, local), lambda i: (i, 0)),
            pl.BlockSpec((span, local), lambda i: (i, 1)),
            pl.BlockSpec((heads, L, span), lambda i: (0, i, 0)),
        ],
        out_specs=[whole((tokens + 16, local)), whole((4, reports * 48, 2 * local))],
        out_shape=[
            jax.ShapeDtypeStruct((tokens + 16, local), BF),
            jax.ShapeDtypeStruct((4, reports * 48, 2 * local), BF),
        ],
        compiler_params=params(),
        cost_estimate=pl.CostEstimate(
            flops=8 * tokens * span * local, bytes_accessed=8 << 20, transcendentals=0
        ),
    )(meta, gate, q_own, q_got, o_own, o_got, kv, kv, probs)


def back_kernel(following, meta, rinv, gain, *refs):
    if following:
        dq_own, dq_got, up, h, wq, wo, grad, o_send, wq_v, up_v, h_v, wo_v, sems = refs
        left, right = dq_own[...], dq_got[...]
    else:
        dq1, dq0, got1, got0, up, h, wq_own, wq_got, grad, wq_v, up_v, h_v, sems = refs
        left = jnp.where(meta[INFO] == 1, dq1[...].astype(F32), dq0[...].astype(F32)).astype(BF)
        right = (got1[...].astype(F32) + got0[...].astype(F32)).astype(BF)
    if len(h.shape) == 3:
        h = h.at[1]
    inner, width = wq_v.shape
    half = inner // 2
    tokens = up_v.shape[0]
    tiles = width // TILE

    def copies(tile):
        cols = slice(tile * TILE, (tile + 1) * TILE)
        out = []
        for part in range(2):
            into = wq_v.at[part * half : (part + 1) * half, cols]
            if following:
                at = pl.multiple_of(meta[INFO + 1 + part], half)
                out.append((wq.at[pl.ds(at, half), cols], into))
            else:
                out.append(((wq_own, wq_got)[part].at[:, cols], into))
        out.append((up.at[:, cols], up_v.at[:, cols]))
        out.append((h.at[:, cols], h_v.at[:, cols]))
        return [
            pltpu.make_async_copy(a, b, sems.at[tile * 4 + i]) for i, (a, b) in enumerate(out)
        ]

    for tile in range(2):
        for copy in copies(tile):
            copy.start()
    if following:
        load = pltpu.make_async_copy(wo, wo_v, sems.at[tiles * 4])
    stat = column(
        jnp.sum(left[tokens:].astype(F32) + right[tokens:].astype(F32), axis=0, keepdims=True)
    )
    dq = jnp.concatenate([left[:tokens], right[:tokens]], axis=1)
    scale = column(rinv[...])
    share = scale * scale * stat / MODEL_WIDTH
    if following:
        live = live_tokens(meta, tokens)
    stores = []
    for tile in range(tiles):
        for copy in copies(tile):
            copy.wait()
        if tile + 2 < tiles:
            for copy in copies(tile + 2):
                copy.start()
        elif following and tile + 2 == tiles:
            load.start()
        cols = slice(tile * TILE, (tile + 1) * TILE)
        dnormed = dot(dq, wq_v[:, cols], NN)
        upstream = up_v[:, cols].astype(F32)
        if following:
            upstream = jnp.where(live, upstream, 0.0)
        value = upstream + (scale * (gain[:, cols] * dnormed) - h_v[:, cols].astype(F32) * share)
        if following:
            value = jnp.where(meta[INFO] == 1, upstream, value)
        up_v[:, cols] = value.astype(BF)
        store = pltpu.make_async_copy(up_v.at[:, cols], grad.at[:, cols], sems.at[tile * 4])
        store.start()
        stores.append(store)
    if following:
        load.wait()
        o_send[...] = dot(up_v[...], wo_v[...], NT).astype(BF)
    for store in stores:
        store.wait()


def back(meta, rinv, gain, dqs, up, h, weights, wo=None):
    tokens, width = up.shape
    half = dqs[0].shape[1]
    inner = 2 * half
    inputs = [meta, rinv, gain, *dqs, up, h, *weights]
    in_specs = [SMEM] + [VMEM] * (2 + len(dqs)) + [ANY] * (2 + len(weights))
    out_specs = [ANY]
    out_shape = [jax.ShapeDtypeStruct((tokens, width), BF)]
    scratch = [pltpu.VMEM((inner, width), BF)] + [pltpu.VMEM((tokens, width), BF)] * 2
    if wo is not None:
        inputs.append(wo)
        in_specs.append(ANY)
        out_specs.append(VMEM)
        out_shape.append(jax.ShapeDtypeStruct((tokens, half), BF))
        scratch.append(pltpu.VMEM((half, width), BF))
    return pl.pallas_call(
        functools.partial(back_kernel, wo is not None),
        in_specs=in_specs,
        out_specs=out_specs,
        out_shape=out_shape,
        scratch_shapes=scratch + [pltpu.SemaphoreType.DMA((width // TILE * 4 + 1,))],
        compiler_params=params(),
        cost_estimate=pl.CostEstimate(
            flops=(3 if wo is not None else 2) * tokens * width * inner,
            bytes_accessed=12 << 20,
            transcendentals=0,
        ),
    )(*inputs)


def term_kernel(dkv, w_kv, own, *terms):
    rows = own.shape[0]
    value = dot(dkv[...].reshape(4 * rows, dkv.shape[2]), w_kv[...], NT)
    own[...] = value[:rows]
    for k, term in enumerate(terms, 1):
        term[...] = value[k * rows : (k + 1) * rows].astype(BF)


def latent_terms(dkv, w_kv):
    rows, inner = dkv.shape[1:]
    features = w_kv.shape[0]
    tile = features // 6
    result = pl.BlockSpec((rows, tile), lambda i: (0, i))
    return pl.pallas_call(
        term_kernel,
        grid=(features // tile,),
        in_specs=[whole(dkv.shape), pl.BlockSpec((tile, inner), lambda i: (i, 0))],
        out_specs=[result] * 4,
        out_shape=[jax.ShapeDtypeStruct((rows, features), t) for t in (F32, BF, BF, BF)],
        compiler_params=params(),
        cost_estimate=pl.CostEstimate(
            flops=8 * rows * inner * features, bytes_accessed=8 << 20, transcendentals=0
        ),
    )(dkv, w_kv)


def per_device(
    segment_inputs,
    cotangent,
    report_lengths,
    norm_gain,
    attn_gate,
    w_query,
    w_out,
    w_key,
    w_value,
    tiles,
    tile_counts,
    lat_query,
    request_source,
    request_slide,
    cross_pattern,
):
    z, y, core = (lax.axis_index(name) for name in DP)
    me_dp = (z * 4 + y) * 2 + core
    me_mp = lax.axis_index("mp")
    seg = lax.axis_index("segment")
    last = seg == 1
    reports = cross_pattern.shape[0]
    wanted = reports * SPR
    h = segment_inputs[0]
    tokens, width = h.shape
    half = 512

    slot = []
    for part in range(4):
        same_seg, same_mp = seg == part // 2, me_mp == part % 2
        slot.append(jnp.where(same_seg, jnp.where(same_mp, 0, 3), jnp.where(same_mp, 1, 2)))
    rows = lax.rem(places(z, y, core) * 32 - me_mp * half + 2 * half, 2 * half)
    info = [seg, me_mp * half, (1 - me_mp) * half]
    source = lax.dynamic_index_in_dim(
        request_source.reshape(32, wanted), me_dp, 0, keepdims=False
    )
    slide = lax.dynamic_index_in_dim(request_slide.reshape(32, wanted), me_dp, 0, keepdims=False)
    source_core = source % 2
    far_z = lax.rem(z - source // 8 + 4, 4)
    far_y = lax.rem(y - source // 2 % 4 + 4, 4)
    first = jnp.where(source_core == 0, far_y, far_z)
    second = jnp.where(source_core == 0, far_z, far_y)
    array = jnp.where(second < 2, second, jnp.where(second == 3, 2, jnp.where(first < 2, 3, 4)))
    array = array + jnp.where(source_core == core, 0, 5)
    block = jnp.where(second == 2, first % 2, first)
    meta = jnp.concatenate(
        [rows, jnp.stack(slot + info).astype(jnp.int32), report_lengths]
        + [cross_pattern.reshape(-1), array, block, slide]
    )

    h_all = lax.all_gather(h, "segment")

    wq_t = w_query[0].T
    blocks = gather_chips(
        make_block(
            tile_counts.reshape(4), tiles, lat_query, w_out[0], wq_t, w_key[0], w_value[0]
        )
    )

    h32 = h.astype(F32)
    partial = jnp.sum(h32 * h32, axis=1)
    squares = partial + lax.ppermute(partial, "mp", [(0, 1), (1, 0)])
    rinv = lax.rsqrt(squares / MODEL_WIDTH + 1e-05)
    gain = norm_gain
    message = lax.ppermute(jnp.concatenate([rinv, gain[0]]), "segment", [(1, 0)])[None]
    rinv1, gain1 = message[:, :tokens], message[:, tokens:]
    normed = (h32 * rinv[:, None] * gain).astype(BF)
    position = jnp.arange(tokens)
    live = position % L < jnp.repeat(report_lengths, L)
    up1 = jnp.where(live[:, None], cotangent, jnp.zeros((), BF))
    rinv = rinv[None]
    gate = jnp.tanh(attn_gate)
    w_kv = jnp.concatenate([w_key[0], w_value[0]], axis=1)
    wq_t, _ = lax.optimization_barrier((wq_t, squares))
    wq1 = lax.ppermute(wq_t, "segment", [(1, 0)])
    swap = [(0, 1), (1, 0)]
    others = [lax.ppermute(b, "core", swap) for b in blocks[:3]]
    blocks, others, normed, up1, rinv1, gain1, meta, w_kv, wq1 = lax.optimization_barrier(
        (blocks, others, normed, up1, rinv1, gain1, meta, w_kv, wq1)
    )
    wq1 = lax.all_gather(wq1, DP, axis=0, tiled=True)
    blocks = blocks + others + [lax.ppermute(b, "core", swap) for b in blocks[3:]]

    q_send, wq_got = project(1, 1, BF, meta, normed, blocks)
    q_got = lax.ppermute(q_send, X, SWAP_MP)
    o_send, wo_got = project(0, 1, BF, meta, up1, blocks)
    o_got = lax.ppermute(o_send, X, LAST_SWAP)
    q_own, wq_own = project(1, 0, F32, meta, normed, blocks)
    o_own, wo_own = project(0, 0, BF, meta, up1, blocks)
    kv = select(wanted, meta, blocks)
    probs = forward(meta, q_own, q_got, kv)
    dq1, dkv1 = backward(meta, gate, q_own, q_got, o_own, o_got, kv, probs)
    dqs = [lax.ppermute(dq1, X, LAST_TO_SAME), lax.ppermute(dq1, X, LAST_TO_CROSS)]
    own1, *terms = latent_terms(dkv1, w_kv)
    dqs, terms = lax.optimization_barrier((dqs, terms))
    up, o_send = back(meta, rinv1, gain1, dqs, cotangent, h_all, [wq1], wo_got)
    o_got = lax.ppermute(o_send, X, FIRST_SWAP)
    o_own = dot(up, wo_own, NT).astype(BF)
    dq1, terms, _ = lax.optimization_barrier((dq1, terms, o_send))
    got1 = lax.ppermute(dq1, X, LAST_SWAP)
    moves = (LAST_TO_SAME, LAST_TO_CROSS, LAST_SWAP)
    got = [lax.ppermute(t, X, p) for t, p in zip(terms, moves)]

    dq0, dkv0 = backward(meta, gate, q_own, q_got, o_own, o_got, kv, probs)
    own0, *terms = latent_terms(dkv0, w_kv)
    got0 = lax.ppermute(dq0, X, FIRST_SWAP)
    terms, got = lax.optimization_barrier((terms, got))
    moves = (FIRST_TO_SAME, FIRST_TO_CROSS, FIRST_SWAP)
    late = [lax.ppermute(t, X, p) for t, p in zip(terms, moves)]
    got, got0 = lax.optimization_barrier((got, got0))
    received = jnp.where(last, own1, own0)
    for term in got:
        received = received + term.astype(F32)
    (grads,) = back(meta, rinv, gain, [dq1, dq0, got1, got0], up, h, [wq_own, wq_got])
    latent_grad, late = lax.optimization_barrier((received, late))
    for term in late:
        latent_grad = latent_grad + term.astype(F32)
    return grads[None], latent_grad.reshape(reports, 48, E)


def solution(mesh):
    fine = Mesh(mesh.devices.reshape(2, 4, 4, 2, 2), ("segment", "z", "y", "core", "mp"))
    return jax.shard_map(
        per_device,
        mesh=fine,
        in_specs=(
            P("segment", DP, "mp"),
            P(DP, "mp"),
            P(DP),
            P("segment", "mp"),
            P("segment"),
            P("segment", "mp", DP),
            P("segment", DP, "mp"),
            P("segment", None, "mp"),
            P("segment", None, "mp"),
            P(DP, None, None),
            P(DP, None),
            P(),
            P(),
            P(),
            P(DP, None, None),
        ),
        out_specs=(P("segment", DP, "mp"), P(DP, X, None)),
        check_vma=False,
    )
```

```python
import functools

import jax
import jax.numpy as jnp
from jax import lax
from jax.experimental import pallas as pl
from jax.experimental.pallas import tpu as pltpu
from jax.sharding import Mesh
from jax.sharding import PartitionSpec as P

MODEL_WIDTH = 4096
E = 1536
HEAD = 128
LAT = 32
SPR = 6
L = 128
QBLK = 32
MAXT = 64
SCALE = HEAD ** (-0.5)
DP = ("z", "y", "core")
X = ("segment", "mp")
BF = jnp.bfloat16
F32 = jnp.float32
LIMIT = 60 * 1024 * 1024
NT = (((1,), (1,)), ((), ()))
NN = (((1,), (0,)), ((), ()))
TN = (((0,), (0,)), ((), ()))

SWAP_MP = [(0, 1), (1, 0), (2, 3), (3, 2)]
LAST_TO_SAME = [(2, 0), (3, 1)]
LAST_TO_CROSS = [(2, 1), (3, 0)]
LAST_SWAP = [(2, 3), (3, 2)]
FIRST_TO_SAME = [(0, 2), (1, 3)]
FIRST_TO_CROSS = [(0, 3), (1, 2)]
FIRST_SWAP = [(0, 1), (1, 0)]


def yz_perm(stage, k):
    pairs = []
    for z in range(4):
        for y in range(4):
            for core in range(2):
                along_y = (core == 0) == (stage == 1)
                to_z = z if along_y else (z + k) % 4
                to_y = (y + k) % 4 if along_y else y
                pairs.append(((z * 4 + y) * 2 + core, (to_z * 4 + to_y) * 2 + core))
    return pairs


def dot(a, b, dims):
    return lax.dot_general(a, b, dims, preferred_element_type=F32)


def params(**kwargs):
    return pltpu.CompilerParams(vmem_limit_bytes=LIMIT, **kwargs)


def whole(shape):
    return pl.BlockSpec(shape, lambda *_: (0,) * len(shape))


SMEM = pl.BlockSpec(memory_space=pltpu.SMEM)
ANY = pl.BlockSpec(memory_space=pl.ANY)
VMEM = pl.BlockSpec(memory_space=pltpu.VMEM)
TILE = 512
ROWS, SLOT, INFO, LENGTHS, PATTERN, PICKS = 0, 32, 36, 39, 43, 139
ARRAYS = ((0, (0, 1, 2, 3)), (1, (0, 1, 2, 3)), (3, (0, 1, 2, 3)), (2, (0, 1)), (2, (2, 3)))


def kv_kernel(counts, tiles, queries, w_key, w_value, out, w_v, latents, sems):
    loads = [
        pltpu.make_async_copy(w, w_v.at[i], sems.at[i]) for i, w in enumerate((w_key, w_value))
    ]
    for load in loads:
        load.start()
    heads = [slice(head * HEAD, (head + 1) * HEAD) for head in range(E // HEAD)]
    slot = lax.broadcasted_iota(jnp.int32, (LAT, MAXT), 1)
    for slide in range(tiles.shape[0]):
        tile = [tiles[slide, :, cols] for cols in heads]
        query = [queries[:, cols] for cols in heads]
        scores = [dot(q, t, NT) * SCALE for q, t in zip(query, tile)]
        scores = [jnp.where(slot < counts[slide], x, -1e30) for x in scores]
        exps = [jnp.exp(s - jnp.max(s, axis=1, keepdims=True)) for s in scores]
        weights = [(e / jnp.sum(e, axis=1, keepdims=True)).astype(BF) for e in exps]
        pooled = [dot(w, t, NN) for w, t in zip(weights, tile)]
        for cols, q, p in zip(heads, query, pooled):
            latents[slide * LAT : (slide + 1) * LAT, cols] = (q.astype(F32) + p).astype(BF)
    for i, load in enumerate(loads):
        load.wait()
        value = dot(latents[...], w_v[i], NN).astype(BF)
        half = value.shape[1]
        for slide in range(tiles.shape[0]):
            at = slide // 2 * LAT
            col = (slide % 2 * 2 + i) * half
            out[at : at + LAT, col : col + half] = value[slide * LAT : (slide + 1) * LAT]


def make_kv(counts, tiles, queries, w_key, w_value):
    slides = tiles.shape[0]
    return pl.pallas_call(
        kv_kernel,
        in_specs=[SMEM] + [VMEM] * 2 + [ANY] * 2,
        out_specs=VMEM,
        out_shape=jax.ShapeDtypeStruct((slides // 2 * LAT, 4 * w_key.shape[1]), BF),
        scratch_shapes=[
            pltpu.VMEM((2,) + w_key.shape, BF),
            pltpu.VMEM((slides * LAT, E), BF),
            pltpu.SemaphoreType.DMA((2,)),
        ],
        compiler_params=params(),
    )(counts, tiles, queries, w_key, w_value)


def over_dp(array, stage, k):
    return lax.ppermute(array, DP, yz_perm(stage, k))


def over_core(arrays):
    return [lax.ppermute(a, "core", [(0, 1), (1, 0)]) for a in arrays]


def places(z, y, core):
    table = []
    for c in (core, 1 - core):
        for j, blocks in ARRAYS:
            for k in blocks:
                at_z = lax.rem(z - jnp.where(c == 0, j, k) + 4, 4)
                at_y = lax.rem(y - jnp.where(c == 0, k, j) + 4, 4)
                table.append((at_z * 4 + at_y) * 2 + c)
    return jnp.stack(table).astype(jnp.int32)


def column(row):
    return jnp.broadcast_to(row, (HEAD, row.shape[1])).T[:, :1]


def live_tokens(meta, tokens):
    index = lax.broadcasted_iota(jnp.int32, (tokens, 1), 0)
    parts = [index[r * L : (r + 1) * L] < r * L + meta[LENGTHS + r] for r in range(tokens // L)]
    return jnp.concatenate([p.astype(F32) for p in parts], axis=0) > 0


def project_kernel(kind, part, meta, x, *refs):
    ins, (out, weight), (w_v, x_v, sems) = refs[:10], refs[10:12], refs[12:]
    load = pltpu.make_async_copy(x, x_v, sems.at[1])
    load.start()
    half = w_v.shape[0]
    index = 0
    for a in range(10):
        for k in range(len(ARRAYS[a % 5][1])):
            at = pl.multiple_of(meta[ROWS + index] - part * half, 32)
            index += 1

            @pl.when((at >= 0) & (at < half))
            def _():
                pltpu.make_async_copy(
                    ins[a].at[k, pl.ds(kind * 32, 32)], w_v.at[pl.ds(at, 32)], sems.at[0]
                ).start()

    load.wait()
    pltpu.make_async_copy(w_v, w_v, sems.at[0]).wait()
    store = pltpu.make_async_copy(w_v, weight, sems.at[0])
    store.start()
    out[...] = dot(x_v[...], w_v[...], NT).astype(out.dtype)
    store.wait()


def project(kind, part, dtype, meta, x, blocks):
    tokens, width = x.shape
    half = 512
    return pl.pallas_call(
        functools.partial(project_kernel, kind, part),
        in_specs=[SMEM, ANY] + [ANY] * 10,
        out_specs=[VMEM, ANY],
        out_shape=[
            jax.ShapeDtypeStruct((tokens, half), dtype),
            jax.ShapeDtypeStruct((half, width), BF),
        ],
        scratch_shapes=[
            pltpu.VMEM((half, width), BF),
            pltpu.VMEM((tokens, width), BF),
            pltpu.SemaphoreType.DMA((2,)),
        ],
        compiler_params=params(),
        cost_estimate=pl.CostEstimate(
            flops=2 * tokens * width * half, bytes_accessed=7 << 20, transcendentals=0
        ),
    )(meta, x, *blocks)


def select_kernel(wanted, meta, *refs):
    ins, out, sems = refs[:10], refs[10], refs[11]
    width = out.shape[1]
    for i in range(wanted):
        block = meta[PICKS + wanted + i]
        slide = meta[PICKS + 2 * wanted + i]
        rows = pl.ds(pl.multiple_of(slide // 2 * LAT, LAT), LAT)
        cols = pl.ds(pl.multiple_of(slide % 2 * width, width), width)
        for a in range(10):

            @pl.when(meta[PICKS + i] == a)
            def _():
                pltpu.make_async_copy(
                    ins[a].at[block, rows, cols], out.at[pl.ds(i * LAT, LAT)], sems.at[0]
                ).start()

    pltpu.make_async_copy(out, out, sems.at[0]).wait()


def select(wanted, meta, blocks):
    return pl.pallas_call(
        functools.partial(select_kernel, wanted),
        in_specs=[SMEM] + [ANY] * 10,
        out_specs=VMEM,
        out_shape=jax.ShapeDtypeStruct((wanted * LAT, 1024), BF),
        scratch_shapes=[pltpu.SemaphoreType.DMA((1,))],
        compiler_params=params(),
        cost_estimate=pl.CostEstimate(flops=0, bytes_accessed=3 << 20, transcendentals=0),
    )(meta, *blocks)


def forward_kernel(meta, q_own, q_got, keys, probs):
    report = pl.program_id(0)
    span = keys.shape[0]
    slide = lax.broadcasted_iota(jnp.int32, (QBLK, span), 1) // LAT
    masks = []
    for block in range(L // QBLK):
        seen = jnp.zeros((QBLK, span), jnp.int32)
        for j in range(SPR):
            at = PATTERN + (report * (L // QBLK) + block) * SPR + j
            seen = jnp.where(slide == j, meta[at], seen)
        masks.append(seen)
    mask = jnp.concatenate(masks, axis=0) == 1
    heads = [slice(head * HEAD, (head + 1) * HEAD) for head in range(probs.shape[0])]
    qb = [(q_own[:, c] + q_got[:, c].astype(F32)).astype(BF) for c in heads]
    scores = [dot(q, keys[:, c], NT) * SCALE for q, c in zip(qb, heads)]
    scores = [jnp.where(mask, s, -1e30) for s in scores]
    exps = [jnp.exp(s - jnp.max(s, axis=1, keepdims=True)) for s in scores]
    totals = [jnp.sum(e, axis=1, keepdims=True) for e in exps]
    for head, (e, total) in enumerate(zip(exps, totals)):
        probs[head] = e / total


def forward(meta, q_own, q_got, kv):
    tokens, local = q_own.shape
    reports = tokens // L
    span = kv.shape[0] // reports
    heads = local // HEAD
    token = pl.BlockSpec((L, local), lambda i: (i, 0))
    return pl.pallas_call(
        forward_kernel,
        grid=(reports,),
        in_specs=[SMEM, token, token, pl.BlockSpec((span, local), lambda i: (i, 0))],
        out_specs=pl.BlockSpec((heads, L, span), lambda i: (0, i, 0)),
        out_shape=jax.ShapeDtypeStruct((heads, tokens, span), F32),
        compiler_params=params(),
        cost_estimate=pl.CostEstimate(
            flops=2 * tokens * span * local, bytes_accessed=6 << 20, transcendentals=tokens * span * 4
        ),
    )(meta, q_own, q_got, kv)


def backward_kernel(meta, gate, q_own, q_got, o_own, o_got, keys, vals, probs, dq_out, dkv_out):
    report = pl.program_id(0)
    rows = pl.ds(pl.multiple_of(report * L, L), L)
    local = q_own.shape[1]
    heads = [slice(head * HEAD, (head + 1) * HEAD) for head in range(local // HEAD)]
    og = [
        (gate[0] * (o_own[:, c].astype(F32) + o_got[:, c].astype(F32))).astype(BF) for c in heads
    ]
    dprob = [dot(g, vals[:, c], NT) for g, c in zip(og, heads)]
    prob = [probs[head] for head in range(len(heads))]
    rowdot = [jnp.sum(p * d, axis=1, keepdims=True) for p, d in zip(prob, dprob)]
    dscore = [(p * (d - r)).astype(BF) for p, d, r in zip(prob, dprob, rowdot)]
    dq = [(dot(d, keys[:, c], NN) * SCALE).astype(BF) for d, c in zip(dscore, heads)]
    q = [q_own[:, c] + q_got[:, c].astype(F32) for c in heads]
    dkey = [(dot(d, x.astype(BF), TN) * SCALE).astype(BF) for d, x in zip(dscore, q)]
    dval = [dot(p.astype(BF), g, TN).astype(BF) for p, g in zip(prob, og)]
    stat = jnp.zeros((L, HEAD), F32)
    for c, d, x in zip(heads, dq, q):
        dq_out[rows, c] = d
        stat += x * d.astype(F32)
    into = pl.ds(pl.multiple_of(report * 48, 16), 48)
    both = jnp.concatenate(dkey + dval, axis=1)
    for part in range(4):
        dkv_out[meta[SLOT + part], into, :] = both[part * 48 : (part + 1) * 48]
    total = jnp.sum(stat.T, axis=0, keepdims=True)
    high = total.astype(BF)
    rest = total - high.astype(F32)
    low = rest.astype(BF)
    lower = (rest - low.astype(F32)).astype(BF)
    zero = jnp.zeros((13, L), F32)
    extra = jnp.concatenate([high.astype(F32), low.astype(F32), lower.astype(F32), zero], axis=0)
    dq_out[4 * L : 4 * L + 16, rows] = extra.astype(BF)


def backward(meta, gate, q_own, q_got, o_own, o_got, kv, probs):
    tokens, local = q_own.shape
    reports = tokens // L
    heads, _, span = probs.shape
    token = pl.BlockSpec((L, local), lambda i: (i, 0))
    return pl.pallas_call(
        backward_kernel,
        grid=(reports,),
        in_specs=[SMEM, SMEM, token, token, token, token]
        + [
            pl.BlockSpec((span, local), lambda i: (i, 0)),
            pl.BlockSpec((span, local), lambda i: (i, 1)),
            pl.BlockSpec((heads, L, span), lambda i: (0, i, 0)),
        ],
        out_specs=[whole((tokens + 16, local)), whole((4, reports * 48, 2 * local))],
        out_shape=[
            jax.ShapeDtypeStruct((tokens + 16, local), BF),
            jax.ShapeDtypeStruct((4, reports * 48, 2 * local), BF),
        ],
        compiler_params=params(),
        cost_estimate=pl.CostEstimate(
            flops=8 * tokens * span * local, bytes_accessed=8 << 20, transcendentals=0
        ),
    )(meta, gate, q_own, q_got, o_own, o_got, kv, kv, probs)


def back_kernel(following, meta, rinv, gain, *refs):
    if following:
        dq_own, dq_got, up, h, wq, wo, grad, o_send, wq_v, up_v, h_v, wo_v, sems = refs
        left, right = dq_own[...], dq_got[...]
    else:
        dq1, dq0, got1, got0, up, h, wq_own, wq_got, grad, wq_v, up_v, h_v, sems = refs
        left = jnp.where(meta[INFO] == 1, dq1[...].astype(F32), dq0[...].astype(F32)).astype(BF)
        right = (got1[...].astype(F32) + got0[...].astype(F32)).astype(BF)
    if len(h.shape) == 3:
        h = h.at[1]
    inner, width = wq_v.shape
    half = inner // 2
    tokens = up_v.shape[0]
    tiles = width // TILE

    def copies(tile):
        cols = slice(tile * TILE, (tile + 1) * TILE)
        out = []
        for part in range(2):
            into = wq_v.at[part * half : (part + 1) * half, cols]
            if following:
                at = pl.multiple_of(meta[INFO + 1 + part], half)
                out.append((wq.at[pl.ds(at, half), cols], into))
            else:
                out.append(((wq_own, wq_got)[part].at[:, cols], into))
        out.append((up.at[:, cols], up_v.at[:, cols]))
        out.append((h.at[:, cols], h_v.at[:, cols]))
        return [
            pltpu.make_async_copy(a, b, sems.at[tile * 4 + i]) for i, (a, b) in enumerate(out)
        ]

    for tile in range(2):
        for copy in copies(tile):
            copy.start()
    if following:
        load = pltpu.make_async_copy(wo, wo_v, sems.at[tiles * 4])
    stat = column(
        jnp.sum(left[tokens:].astype(F32) + right[tokens:].astype(F32), axis=0, keepdims=True)
    )
    dq = jnp.concatenate([left[:tokens], right[:tokens]], axis=1)
    scale = column(rinv[...])
    share = scale * scale * stat / MODEL_WIDTH
    if following:
        live = live_tokens(meta, tokens)
    stores = []
    for tile in range(tiles):
        for copy in copies(tile):
            copy.wait()
        if tile + 2 < tiles:
            for copy in copies(tile + 2):
                copy.start()
        elif following and tile + 2 == tiles:
            load.start()
        cols = slice(tile * TILE, (tile + 1) * TILE)
        dnormed = dot(dq, wq_v[:, cols], NN)
        upstream = up_v[:, cols].astype(F32)
        if following:
            upstream = jnp.where(live, upstream, 0.0)
        value = upstream + (scale * (gain[:, cols] * dnormed) - h_v[:, cols].astype(F32) * share)
        if following:
            value = jnp.where(meta[INFO] == 1, upstream, value)
        up_v[:, cols] = value.astype(BF)
        store = pltpu.make_async_copy(up_v.at[:, cols], grad.at[:, cols], sems.at[tile * 4])
        store.start()
        stores.append(store)
    if following:
        load.wait()
        o_send[...] = dot(up_v[...], wo_v[...], NT).astype(BF)
    for store in stores:
        store.wait()


def back(meta, rinv, gain, dqs, up, h, weights, wo=None):
    tokens, width = up.shape
    half = dqs[0].shape[1]
    inner = 2 * half
    inputs = [meta, rinv, gain, *dqs, up, h, *weights]
    in_specs = [SMEM] + [VMEM] * (2 + len(dqs)) + [ANY] * (2 + len(weights))
    out_specs = [ANY]
    out_shape = [jax.ShapeDtypeStruct((tokens, width), BF)]
    scratch = [pltpu.VMEM((inner, width), BF)] + [pltpu.VMEM((tokens, width), BF)] * 2
    if wo is not None:
        inputs.append(wo)
        in_specs.append(ANY)
        out_specs.append(VMEM)
        out_shape.append(jax.ShapeDtypeStruct((tokens, half), BF))
        scratch.append(pltpu.VMEM((half, width), BF))
    return pl.pallas_call(
        functools.partial(back_kernel, wo is not None),
        in_specs=in_specs,
        out_specs=out_specs,
        out_shape=out_shape,
        scratch_shapes=scratch + [pltpu.SemaphoreType.DMA((width // TILE * 4 + 1,))],
        compiler_params=params(),
        cost_estimate=pl.CostEstimate(
            flops=(3 if wo is not None else 2) * tokens * width * inner,
            bytes_accessed=12 << 20,
            transcendentals=0,
        ),
    )(*inputs)


def term_kernel(dkv, w_key, w_value, own, *terms):
    rows = own.shape[0]
    both = dkv[...].reshape(4 * rows, dkv.shape[2])
    half = w_key.shape[1]
    value = dot(both[:, :half], w_key[...], NT) + dot(both[:, half:], w_value[...], NT)
    own[...] = value[:rows]
    for k, term in enumerate(terms, 1):
        term[...] = value[k * rows : (k + 1) * rows].astype(BF)


def latent_terms(dkv, w_key, w_value):
    rows, inner = dkv.shape[1:]
    features = w_key.shape[0]
    tile = features // 3
    weight = pl.BlockSpec((tile, w_key.shape[1]), lambda i: (i, 0))
    result = pl.BlockSpec((rows, tile), lambda i: (0, i))
    return pl.pallas_call(
        term_kernel,
        grid=(features // tile,),
        in_specs=[whole(dkv.shape), weight, weight],
        out_specs=[result] * 4,
        out_shape=[jax.ShapeDtypeStruct((rows, features), t) for t in (F32, BF, BF, BF)],
        compiler_params=params(),
        cost_estimate=pl.CostEstimate(
            flops=8 * rows * inner * features, bytes_accessed=8 << 20, transcendentals=0
        ),
    )(dkv, w_key, w_value)


def per_device(
    segment_inputs,
    cotangent,
    report_lengths,
    norm_gain,
    attn_gate,
    w_query,
    w_out,
    w_key,
    w_value,
    tiles,
    tile_counts,
    lat_query,
    request_source,
    request_slide,
    cross_pattern,
):
    z, y, core = (lax.axis_index(name) for name in DP)
    me_dp = (z * 4 + y) * 2 + core
    me_mp = lax.axis_index("mp")
    seg = lax.axis_index("segment")
    last = seg == 1
    reports = cross_pattern.shape[0]
    wanted = reports * SPR
    h = segment_inputs[0]
    tokens, width = h.shape
    half = 512

    slot = []
    for part in range(4):
        same_seg, same_mp = seg == part // 2, me_mp == part % 2
        slot.append(jnp.where(same_seg, jnp.where(same_mp, 0, 3), jnp.where(same_mp, 1, 2)))
    rows = lax.rem(places(z, y, core) * 32 - me_mp * half + 2 * half, 2 * half)
    info = [seg, me_mp * half, (1 - me_mp) * half]
    source = lax.dynamic_index_in_dim(
        request_source.reshape(32, wanted), me_dp, 0, keepdims=False
    )
    slide = lax.dynamic_index_in_dim(request_slide.reshape(32, wanted), me_dp, 0, keepdims=False)
    source_core = source % 2
    far_z = lax.rem(z - source // 8 + 4, 4)
    far_y = lax.rem(y - source // 2 % 4 + 4, 4)
    first = jnp.where(source_core == 0, far_y, far_z)
    second = jnp.where(source_core == 0, far_z, far_y)
    array = jnp.where(second < 2, second, jnp.where(second == 3, 2, jnp.where(first < 2, 3, 4)))
    array = array + jnp.where(source_core == core, 0, 5)
    block = jnp.where(second == 2, first % 2, first)
    meta = jnp.concatenate(
        [rows, jnp.stack(slot + info).astype(jnp.int32), report_lengths]
        + [cross_pattern.reshape(-1), array, block, slide]
    )

    h_all = lax.all_gather(h, "segment")

    wq_t = w_query[0].T
    block = jnp.concatenate([w_out[0], wq_t], axis=0)
    parts = [over_dp(block, 1, k) for k in (1, 2, 3)]
    kv_block = make_kv(tile_counts.reshape(4), tiles, lat_query, w_key[0], w_value[0])
    parts, kv_block = lax.optimization_barrier((parts, kv_block))
    bundle = jnp.stack([block, *parts])
    one, three = over_dp(bundle, 2, 1), over_dp(bundle, 2, 3)
    parts = [over_dp(kv_block, 1, k) for k in (1, 2, 3)]
    one, three, parts = lax.optimization_barrier((one, three, parts))
    two = [over_dp(one[:2], 2, 1), over_dp(three[2:], 2, 3)]
    kv_bundle = jnp.stack([kv_block, *parts])
    kv_one, kv_three = over_dp(kv_bundle, 2, 1), over_dp(kv_bundle, 2, 3)

    h32 = h.astype(F32)
    partial = jnp.sum(h32 * h32, axis=1)
    squares = partial + lax.ppermute(partial, "mp", [(0, 1), (1, 0)])
    rinv = lax.rsqrt(squares / MODEL_WIDTH + 1e-05)
    gain = norm_gain
    message = lax.ppermute(jnp.concatenate([rinv, gain[0]]), "segment", [(1, 0)])[None]
    rinv1, gain1 = message[:, :tokens], message[:, tokens:]
    normed = (h32 * rinv[:, None] * gain).astype(BF)
    position = jnp.arange(tokens)
    live = position % L < jnp.repeat(report_lengths, L)
    up1 = jnp.where(live[:, None], cotangent, jnp.zeros((), BF))
    rinv = rinv[None]
    gate = jnp.tanh(attn_gate)
    wq_t, _ = lax.optimization_barrier((wq_t, squares))
    wq1 = lax.ppermute(wq_t, "segment", [(1, 0)])
    others = over_core([bundle, one, three])
    two, others, normed, up1, rinv1, gain1, meta, wq1 = lax.optimization_barrier(
        (two, others, normed, up1, rinv1, gain1, meta, wq1)
    )
    wq1 = lax.all_gather(wq1, DP, axis=0, tiled=True)
    blocks = [bundle, one, three, *two, *others, *over_core(two)]

    q_send, wq_got = project(1, 1, BF, meta, normed, blocks)
    q_got = lax.ppermute(q_send, X, SWAP_MP)
    up1, q_send = lax.optimization_barrier((up1, q_send))
    o_send, wo_got = project(0, 1, BF, meta, up1, blocks)
    o_got = lax.ppermute(o_send, X, LAST_SWAP)
    kv_one, kv_three, o_send = lax.optimization_barrier((kv_one, kv_three, o_send))
    kv_two = [over_dp(kv_one[:2], 2, 1), over_dp(kv_three[2:], 2, 3)]
    kv_blocks = [kv_bundle, kv_one, kv_three, *kv_two]
    kv_blocks += over_core(kv_blocks)
    q_own, wq_own = project(1, 0, F32, meta, normed, blocks)
    up1, q_got, q_own = lax.optimization_barrier((up1, q_got, q_own))
    o_own, wo_own = project(0, 0, BF, meta, up1, blocks)
    kv_blocks, q_own, o_own = lax.optimization_barrier((kv_blocks, q_own, o_own))
    kv = select(wanted, meta, kv_blocks)
    probs = forward(meta, q_own, q_got, kv)
    dq1, dkv1 = backward(meta, gate, q_own, q_got, o_own, o_got, kv, probs)
    dqs = [lax.ppermute(dq1, X, LAST_TO_SAME), lax.ppermute(dq1, X, LAST_TO_CROSS)]
    own1, *terms = latent_terms(dkv1, w_key[0], w_value[0])
    dqs, terms = lax.optimization_barrier((dqs, terms))
    up, o_send = back(meta, rinv1, gain1, dqs, cotangent, h_all, [wq1], wo_got)
    o_got = lax.ppermute(o_send, X, FIRST_SWAP)
    o_own = dot(up, wo_own, NT).astype(BF)
    dq1, terms, _ = lax.optimization_barrier((dq1, terms, o_send))
    got1 = lax.ppermute(dq1, X, LAST_SWAP)
    moves = (LAST_TO_SAME, LAST_TO_CROSS, LAST_SWAP)
    got = [lax.ppermute(t, X, p) for t, p in zip(terms, moves)]

    dq0, dkv0 = backward(meta, gate, q_own, q_got, o_own, o_got, kv, probs)
    own0, *terms = latent_terms(dkv0, w_key[0], w_value[0])
    got0 = lax.ppermute(dq0, X, FIRST_SWAP)
    terms, got = lax.optimization_barrier((terms, got))
    moves = (FIRST_TO_SAME, FIRST_TO_CROSS, FIRST_SWAP)
    late = [lax.ppermute(t, X, p) for t, p in zip(terms, moves)]
    got, got0 = lax.optimization_barrier((got, got0))
    received = jnp.where(last, own1, own0)
    for term in got:
        received = received + term.astype(F32)
    (grads,) = back(meta, rinv, gain, [dq1, dq0, got1, got0], up, h, [wq_own, wq_got])
    latent_grad, late = lax.optimization_barrier((received, late))
    for term in late:
        latent_grad = latent_grad + term.astype(F32)
    return grads[None], latent_grad.reshape(reports, 48, E)


def solution(mesh):
    fine = Mesh(mesh.devices.reshape(2, 4, 4, 2, 2), ("segment", "z", "y", "core", "mp"))
    return jax.shard_map(
        per_device,
        mesh=fine,
        in_specs=(
            P("segment", DP, "mp"),
            P(DP, "mp"),
            P(DP),
            P("segment", "mp"),
            P("segment"),
            P("segment", "mp", DP),
            P("segment", DP, "mp"),
            P("segment", None, "mp"),
            P("segment", None, "mp"),
            P(DP, None, None),
            P(DP, None),
            P(),
            P(),
            P(),
            P(DP, None, None),
        ),
        out_specs=(P("segment", DP, "mp"), P(DP, X, None)),
        check_vma=False,
    )
```

```python
import functools

import jax
import jax.numpy as jnp
from jax import lax
from jax.experimental import pallas as pl
from jax.experimental.pallas import tpu as pltpu
from jax.sharding import Mesh
from jax.sharding import PartitionSpec as P

MODEL_WIDTH = 4096
E = 1536
HEAD = 128
LAT = 32
SPR = 6
L = 128
QBLK = 32
MAXT = 64
SCALE = HEAD ** (-0.5)
DP = ("z", "y", "core")
X = ("segment", "mp")
BF = jnp.bfloat16
F32 = jnp.float32
LIMIT = 64 * 1024 * 1024
NT = (((1,), (1,)), ((), ()))
NN = (((1,), (0,)), ((), ()))
TN = (((0,), (0,)), ((), ()))

SWAP_MP = [(0, 1), (1, 0), (2, 3), (3, 2)]
LAST_TO_SAME = [(2, 0), (3, 1)]
LAST_TO_CROSS = [(2, 1), (3, 0)]
LAST_SWAP = [(2, 3), (3, 2)]
FIRST_TO_SAME = [(0, 2), (1, 3)]
FIRST_TO_CROSS = [(0, 3), (1, 2)]
FIRST_SWAP = [(0, 1), (1, 0)]


def yz_perm(stage, k):
    pairs = []
    for z in range(4):
        for y in range(4):
            for core in range(2):
                along_y = (core == 0) == (stage == 1)
                to_z = z if along_y else (z + k) % 4
                to_y = (y + k) % 4 if along_y else y
                pairs.append(((z * 4 + y) * 2 + core, (to_z * 4 + to_y) * 2 + core))
    return pairs


def dot(a, b, dims):
    return lax.dot_general(a, b, dims, preferred_element_type=F32)


def params(**kwargs):
    return pltpu.CompilerParams(vmem_limit_bytes=LIMIT, **kwargs)


def whole(shape):
    return pl.BlockSpec(shape, lambda *_: (0,) * len(shape))


SMEM = pl.BlockSpec(memory_space=pltpu.SMEM)
ANY = pl.BlockSpec(memory_space=pl.ANY)
VMEM = pl.BlockSpec(memory_space=pltpu.VMEM)
TILE = 512
SMALL = pl.CostEstimate(flops=1, bytes_accessed=1, transcendentals=0)
ROWS, SLOT, INFO, LENGTHS, PATTERN, PICKS = 0, 32, 36, 39, 43, 139


def block_kernel(counts, tiles, queries, w_out, w_query, w_key, w_value, out, w_v, latents, sems):
    loads = [
        pltpu.make_async_copy(w, w_v.at[i], sems.at[i]) for i, w in enumerate((w_key, w_value))
    ]
    for load in loads:
        load.start()
    out[:32] = w_out[...]
    out[32:64] = w_query[...]
    heads = [slice(head * HEAD, (head + 1) * HEAD) for head in range(E // HEAD)]
    slot = lax.broadcasted_iota(jnp.int32, (LAT, MAXT), 1)
    for slide in range(tiles.shape[0]):
        tile = [tiles[slide, :, cols] for cols in heads]
        query = [queries[:, cols] for cols in heads]
        scores = [dot(q, t, NT) * SCALE for q, t in zip(query, tile)]
        scores = [jnp.where(slot < counts[slide], x, -1e30) for x in scores]
        exps = [jnp.exp(s - jnp.max(s, axis=1, keepdims=True)) for s in scores]
        weights = [(e / jnp.sum(e, axis=1, keepdims=True)).astype(BF) for e in exps]
        pooled = [dot(w, t, NN) for w, t in zip(weights, tile)]
        for cols, q, p in zip(heads, query, pooled):
            latents[slide * LAT : (slide + 1) * LAT, cols] = (q.astype(F32) + p).astype(BF)
    for i, load in enumerate(loads):
        load.wait()
        value = dot(latents[...], w_v[i], NN).astype(BF)
        half = value.shape[1]
        for slide in range(tiles.shape[0]):
            at = 64 + slide // 2 * LAT
            col = (slide % 2 * 2 + i) * half
            out[at : at + LAT, col : col + half] = value[slide * LAT : (slide + 1) * LAT]


def make_block(counts, tiles, queries, w_out, w_query, w_key, w_value):
    slides = tiles.shape[0]
    return pl.pallas_call(
        block_kernel,
        in_specs=[SMEM] + [VMEM] * 4 + [ANY] * 2,
        out_specs=VMEM,
        out_shape=jax.ShapeDtypeStruct((64 + slides // 2 * LAT, w_out.shape[1]), BF),
        scratch_shapes=[
            pltpu.VMEM((2,) + w_key.shape, BF),
            pltpu.VMEM((slides * LAT, E), BF),
            pltpu.SemaphoreType.DMA((2,)),
        ],
        compiler_params=params(),
        cost_estimate=SMALL,
    )(counts, tiles, queries, w_out, w_query, w_key, w_value)


def over_dp(array, stage, k):
    return lax.ppermute(array, DP, yz_perm(stage, k))


def over_core(arrays):
    return [lax.ppermute(a, "core", [(0, 1), (1, 0)]) for a in arrays]


def places(z, y, core):
    table = []
    for a in range(8):
        c = core if a < 4 else 1 - core
        for k in range(4):
            j = a % 4
            at_z = lax.rem(z - jnp.where(c == 0, j, k) + 4, 4)
            at_y = lax.rem(y - jnp.where(c == 0, k, j) + 4, 4)
            table.append((at_z * 4 + at_y) * 2 + c)
    return jnp.stack(table).astype(jnp.int32)


def column(row):
    return jnp.broadcast_to(row, (HEAD, row.shape[1])).T[:, :1]


def live_tokens(meta, tokens):
    index = lax.broadcasted_iota(jnp.int32, (tokens, 1), 0)
    parts = [index[r * L : (r + 1) * L] < r * L + meta[LENGTHS + r] for r in range(tokens // L)]
    return jnp.concatenate([p.astype(F32) for p in parts], axis=0) > 0


def project_kernel(part, meta, normed, upstream, *refs):
    ins, outs, weights, (w_v, x_v, sems) = refs[:16], refs[16:18], refs[18:20], refs[20:]
    half = w_v.shape[1]

    def load(i, x):
        pltpu.make_async_copy(x, x_v.at[i], sems.at[2 * i]).start()
        for a in range(16):
            for k in range(2):
                at = pl.multiple_of(meta[ROWS + a * 2 + k] - part * half, 32)

                @pl.when((at >= 0) & (at < half))
                def _():
                    pltpu.make_async_copy(
                        ins[a].at[k, pl.ds((1 - i) * 32, 32)],
                        w_v.at[i, pl.ds(at, 32)],
                        sems.at[2 * i + 1],
                    ).start()

    load(0, normed)
    stores = []
    for i in range(2):
        pltpu.make_async_copy(x_v.at[i], x_v.at[i], sems.at[2 * i]).wait()
        pltpu.make_async_copy(w_v.at[i], w_v.at[i], sems.at[2 * i + 1]).wait()
        if i == 0:
            load(1, upstream)
        stores.append(pltpu.make_async_copy(w_v.at[i], weights[i], sems.at[2 * i + 1]))
        stores[i].start()
        outs[i][...] = dot(x_v[i], w_v[i], NT).astype(outs[i].dtype)
    for store in stores:
        store.wait()


def project(part, dtype, meta, normed, upstream, blocks):
    tokens, width = normed.shape
    half = 512
    return pl.pallas_call(
        functools.partial(project_kernel, part),
        in_specs=[SMEM] + [ANY] * 18,
        out_specs=[VMEM, VMEM, ANY, ANY],
        out_shape=[
            jax.ShapeDtypeStruct((tokens, half), dtype),
            jax.ShapeDtypeStruct((tokens, half), BF),
            jax.ShapeDtypeStruct((half, width), BF),
            jax.ShapeDtypeStruct((half, width), BF),
        ],
        scratch_shapes=[
            pltpu.VMEM((2, half, width), BF),
            pltpu.VMEM((2, tokens, width), BF),
            pltpu.SemaphoreType.DMA((4,)),
        ],
        compiler_params=params(),
        cost_estimate=SMALL,
    )(meta, normed, upstream, *blocks)


def select_kernel(wanted, meta, *refs):
    ins, out, sems = refs[:16], refs[16], refs[17]
    width = out.shape[1]
    for i in range(wanted):
        array = meta[PICKS + i]
        block = meta[PICKS + wanted + i]
        slide = meta[PICKS + 2 * wanted + i]
        rows = pl.ds(pl.multiple_of(64 + slide // 2 * LAT, LAT), LAT)
        cols = pl.ds(pl.multiple_of(slide % 2 * width, width), width)
        for group in range(4):

            @pl.when(array // 4 == group)
            def _():
                for a in range(group * 4, group * 4 + 4):

                    @pl.when(array == a)
                    def _():
                        pltpu.make_async_copy(
                            ins[a].at[block, rows, cols], out.at[pl.ds(i * LAT, LAT)], sems.at[0]
                        ).start()

    pltpu.make_async_copy(out, out, sems.at[0]).wait()


def select(wanted, meta, blocks):
    return pl.pallas_call(
        functools.partial(select_kernel, wanted),
        in_specs=[SMEM] + [ANY] * 16,
        out_specs=VMEM,
        out_shape=jax.ShapeDtypeStruct((wanted * LAT, 1024), BF),
        scratch_shapes=[pltpu.SemaphoreType.DMA((1,))],
        compiler_params=params(),
        cost_estimate=SMALL,
    )(meta, *blocks)


def forward_kernel(meta, q_own, q_got, kv, probs):
    report = pl.program_id(0)
    span = kv.shape[0]
    slide = lax.broadcasted_iota(jnp.int32, (QBLK, span), 1) // LAT
    masks = []
    for block in range(L // QBLK):
        seen = jnp.zeros((QBLK, span), jnp.int32)
        for j in range(SPR):
            at = PATTERN + (report * (L // QBLK) + block) * SPR + j
            seen = jnp.where(slide == j, meta[at], seen)
        masks.append(seen)
    mask = jnp.concatenate(masks, axis=0) == 1
    heads = [slice(head * HEAD, (head + 1) * HEAD) for head in range(probs.shape[0])]
    qb = [(q_own[:, c] + q_got[:, c].astype(F32)).astype(BF) for c in heads]
    scores = [dot(q, kv[:, c], NT) * SCALE for q, c in zip(qb, heads)]
    scores = [jnp.where(mask, s, -1e30) for s in scores]
    exps = [jnp.exp(s - jnp.max(s, axis=1, keepdims=True)) for s in scores]
    totals = [jnp.sum(e, axis=1, keepdims=True) for e in exps]
    for head, (e, total) in enumerate(zip(exps, totals)):
        probs[head] = e / total


def forward(meta, q_own, q_got, kv):
    tokens, local = q_own.shape
    reports = tokens // L
    span = kv.shape[0] // reports
    heads = local // HEAD
    token = pl.BlockSpec((L, local), lambda i: (i, 0))
    return pl.pallas_call(
        forward_kernel,
        grid=(reports,),
        in_specs=[SMEM, token, token, pl.BlockSpec((span, local), lambda i: (i, 0))],
        out_specs=pl.BlockSpec((heads, L, span), lambda i: (0, i, 0)),
        out_shape=jax.ShapeDtypeStruct((heads, tokens, span), F32),
        compiler_params=params(),
        cost_estimate=SMALL,
    )(meta, q_own, q_got, kv)


def backward_kernel(meta, gate, q_own, q_got, o_own, o_got, keys, vals, probs, dq_out, dkv_out):
    report = pl.program_id(0)
    rows = pl.ds(pl.multiple_of(report * L, L), L)
    local = q_own.shape[1]
    heads = [slice(head * HEAD, (head + 1) * HEAD) for head in range(local // HEAD)]
    og = [
        (gate[0] * (o_own[:, c].astype(F32) + o_got[:, c].astype(F32))).astype(BF) for c in heads
    ]
    dprob = [dot(g, vals[:, c], NT) for g, c in zip(og, heads)]
    prob = [probs[head] for head in range(len(heads))]
    rowdot = [jnp.sum(p * d, axis=1, keepdims=True) for p, d in zip(prob, dprob)]
    dscore = [(p * (d - r)).astype(BF) for p, d, r in zip(prob, dprob, rowdot)]
    dq = [(dot(d, keys[:, c], NN) * SCALE).astype(BF) for d, c in zip(dscore, heads)]
    q = [q_own[:, c] + q_got[:, c].astype(F32) for c in heads]
    dkey = [(dot(d, x.astype(BF), TN) * SCALE).astype(BF) for d, x in zip(dscore, q)]
    dval = [dot(p.astype(BF), g, TN).astype(BF) for p, g in zip(prob, og)]
    stat = jnp.zeros((L, HEAD), F32)
    for c, d, x in zip(heads, dq, q):
        dq_out[rows, c] = d
        stat += x * d.astype(F32)
    into = pl.ds(pl.multiple_of(report * 48, 16), 48)
    both = jnp.concatenate(dkey + dval, axis=1)
    for part in range(4):
        dkv_out[meta[SLOT + part], into, :] = both[part * 48 : (part + 1) * 48]
    total = jnp.sum(stat.T, axis=0, keepdims=True)
    high = total.astype(BF)
    rest = total - high.astype(F32)
    low = rest.astype(BF)
    lower = (rest - low.astype(F32)).astype(BF)
    zero = jnp.zeros((13, L), F32)
    extra = jnp.concatenate([high.astype(F32), low.astype(F32), lower.astype(F32), zero], axis=0)
    dq_out[4 * L : 4 * L + 16, rows] = extra.astype(BF)


def backward(meta, gate, q_own, q_got, o_own, o_got, kv, probs):
    tokens, local = q_own.shape
    reports = tokens // L
    heads, _, span = probs.shape
    token = pl.BlockSpec((L, local), lambda i: (i, 0))
    return pl.pallas_call(
        backward_kernel,
        grid=(reports,),
        in_specs=[SMEM, SMEM, token, token, token, token]
        + [
            pl.BlockSpec((span, local), lambda i: (i, 0)),
            pl.BlockSpec((span, local), lambda i: (i, 1)),
            pl.BlockSpec((heads, L, span), lambda i: (0, i, 0)),
        ],
        out_specs=[whole((tokens + 16, local)), whole((4, reports * 48, 2 * local))],
        out_shape=[
            jax.ShapeDtypeStruct((tokens + 16, local), BF),
            jax.ShapeDtypeStruct((4, reports * 48, 2 * local), BF),
        ],
        compiler_params=params(),
        cost_estimate=SMALL,
    )(meta, gate, q_own, q_got, o_own, o_got, kv, kv, probs)


def back_kernel(following, meta, rinv, gain, *refs):
    if following:
        dq_own, dq_got, up, h, wq, wo, grad, o_send, wq_v, up_v, h_v, wo_v, sems = refs
        left, right = dq_own[...], dq_got[...]
    else:
        dq1, dq0, got1, got0, up, h, wq_own, wq_got, grad, wq_v, up_v, h_v, sems = refs
        left = jnp.where(meta[INFO] == 1, dq1[...].astype(F32), dq0[...].astype(F32)).astype(BF)
        right = (got1[...].astype(F32) + got0[...].astype(F32)).astype(BF)
    if len(h.shape) == 3:
        h = h.at[1]
    inner, width = wq_v.shape
    half = inner // 2
    tokens = up_v.shape[0]
    tiles = width // TILE

    def copies(tile):
        cols = slice(tile * TILE, (tile + 1) * TILE)
        out = []
        for part in range(2):
            into = wq_v.at[part * half : (part + 1) * half, cols]
            if following:
                at = pl.multiple_of(meta[INFO + 1 + part], half)
                out.append((wq.at[pl.ds(at, half), cols], into))
            else:
                out.append(((wq_own, wq_got)[part].at[:, cols], into))
        out.append((up.at[:, cols], up_v.at[:, cols]))
        out.append((h.at[:, cols], h_v.at[:, cols]))
        return [
            pltpu.make_async_copy(a, b, sems.at[tile * 4 + i]) for i, (a, b) in enumerate(out)
        ]

    for tile in range(2):
        for copy in copies(tile):
            copy.start()
    if following:
        load = pltpu.make_async_copy(wo, wo_v, sems.at[tiles * 4])
    stat = column(
        jnp.sum(left[tokens:].astype(F32) + right[tokens:].astype(F32), axis=0, keepdims=True)
    )
    dq = jnp.concatenate([left[:tokens], right[:tokens]], axis=1)
    scale = column(rinv[...])
    share = scale * scale * stat / MODEL_WIDTH
    if following:
        live = live_tokens(meta, tokens)
    stores = []
    for tile in range(tiles):
        for copy in copies(tile):
            copy.wait()
        if tile + 2 < tiles:
            for copy in copies(tile + 2):
                copy.start()
        elif following and tile + 2 == tiles:
            load.start()
        cols = slice(tile * TILE, (tile + 1) * TILE)
        dnormed = dot(dq, wq_v[:, cols], NN)
        upstream = up_v[:, cols].astype(F32)
        if following:
            upstream = jnp.where(live, upstream, 0.0)
        value = upstream + (scale * (gain[:, cols] * dnormed) - h_v[:, cols].astype(F32) * share)
        if following:
            value = jnp.where(meta[INFO] == 1, upstream, value)
        up_v[:, cols] = value.astype(BF)
        store = pltpu.make_async_copy(up_v.at[:, cols], grad.at[:, cols], sems.at[tile * 4])
        store.start()
        stores.append(store)
    if following:
        load.wait()
        o_send[...] = dot(up_v[...], wo_v[...], NT).astype(BF)
    for store in stores:
        store.wait()


def back(meta, rinv, gain, dqs, up, h, weights, wo=None):
    tokens, width = up.shape
    half = dqs[0].shape[1]
    inner = 2 * half
    inputs = [meta, rinv, gain, *dqs, up, h, *weights]
    in_specs = [SMEM] + [VMEM] * (2 + len(dqs)) + [ANY] * (2 + len(weights))
    out_specs = [ANY]
    out_shape = [jax.ShapeDtypeStruct((tokens, width), BF)]
    scratch = [pltpu.VMEM((inner, width), BF)] + [pltpu.VMEM((tokens, width), BF)] * 2
    if wo is not None:
        inputs.append(wo)
        in_specs.append(ANY)
        out_specs.append(VMEM)
        out_shape.append(jax.ShapeDtypeStruct((tokens, half), BF))
        scratch.append(pltpu.VMEM((half, width), BF))
    return pl.pallas_call(
        functools.partial(back_kernel, wo is not None),
        in_specs=in_specs,
        out_specs=out_specs,
        out_shape=out_shape,
        scratch_shapes=scratch + [pltpu.SemaphoreType.DMA((width // TILE * 4 + 1,))],
        compiler_params=params(),
        cost_estimate=SMALL,
    )(*inputs)


def term_kernel(groups, dkv, w_key, w_value, added, own, *terms):
    rows = own.shape[0]
    both = dkv[...].reshape(4 * rows, dkv.shape[2])
    half = w_key.shape[1]
    value = dot(both[:, :half], w_key[...], NT) + dot(both[:, half:], w_value[...], NT)
    own[...] = value[:rows]
    for group, term in zip(groups, terms):
        for i, k in enumerate(group):
            part = value[k * rows : (k + 1) * rows]
            if k == 2:
                part += added[...].astype(F32)
            term[i * rows : (i + 1) * rows] = part.astype(BF)


def latent_terms(groups, dkv, w_key, w_value, added):
    rows, inner = dkv.shape[1:]
    features = w_key.shape[0]
    tile = features // 3
    weight = pl.BlockSpec((tile, w_key.shape[1]), lambda i: (i, 0))
    sizes = [rows] + [rows * len(group) for group in groups]
    return pl.pallas_call(
        functools.partial(term_kernel, groups),
        grid=(features // tile,),
        in_specs=[whole(dkv.shape), weight, weight, pl.BlockSpec((rows, tile), lambda i: (0, i))],
        out_specs=[pl.BlockSpec((n, tile), lambda i: (0, i)) for n in sizes],
        out_shape=[
            jax.ShapeDtypeStruct((n, features), BF if i else F32) for i, n in enumerate(sizes)
        ],
        compiler_params=params(),
        cost_estimate=SMALL,
    )(dkv, w_key, w_value, added)


def per_device(
    segment_inputs,
    cotangent,
    report_lengths,
    norm_gain,
    attn_gate,
    w_query,
    w_out,
    w_key,
    w_value,
    tiles,
    tile_counts,
    lat_query,
    request_source,
    request_slide,
    cross_pattern,
):
    z, y, core = (lax.axis_index(name) for name in DP)
    me_dp = (z * 4 + y) * 2 + core
    me_mp = lax.axis_index("mp")
    seg = lax.axis_index("segment")
    last = seg == 1
    reports = cross_pattern.shape[0]
    wanted = reports * SPR
    h = segment_inputs[0]
    tokens, width = h.shape
    half = 512

    slot = []
    for part in range(4):
        same_seg, same_mp = seg == part // 2, me_mp == part % 2
        slot.append(jnp.where(same_seg, jnp.where(same_mp, 0, 3), jnp.where(same_mp, 1, 2)))
    rows = lax.rem(places(z, y, core) * 32 - me_mp * half + 2 * half, 2 * half)
    info = [seg, me_mp * half, (1 - me_mp) * half]
    source = lax.dynamic_index_in_dim(
        request_source.reshape(32, wanted), me_dp, 0, keepdims=False
    )
    slide = lax.dynamic_index_in_dim(request_slide.reshape(32, wanted), me_dp, 0, keepdims=False)
    source_core = source % 2
    far_z = lax.rem(z - source // 8 + 4, 4)
    far_y = lax.rem(y - source // 2 % 4 + 4, 4)
    first = jnp.where(source_core == 0, far_y, far_z)
    second = jnp.where(source_core == 0, far_z, far_y)
    array = 2 * second + first // 2 + jnp.where(source_core == core, 0, 8)
    first = first % 2
    meta = jnp.concatenate(
        [rows, jnp.stack(slot + info).astype(jnp.int32), report_lengths]
        + [cross_pattern.reshape(-1), array, first, slide]
    )

    h_all = lax.all_gather(segment_inputs, "segment", axis=0, tiled=True)

    h32 = h.astype(F32)
    partial = jnp.sum(h32 * h32, axis=1)
    squares = partial + lax.ppermute(partial, "mp", [(0, 1), (1, 0)])
    rinv = lax.rsqrt(squares / MODEL_WIDTH + 1e-05)
    gain = norm_gain
    message = lax.ppermute(jnp.concatenate([rinv, gain[0]]), "segment", [(1, 0)])[None]
    rinv1, gain1 = message[:, :tokens], message[:, tokens:]
    normed = (h32 * rinv[:, None] * gain).astype(BF)
    position = jnp.arange(tokens)
    live = position % L < jnp.repeat(report_lengths, L)
    up1 = jnp.where(live[:, None], cotangent, jnp.zeros((), BF))
    rinv = rinv[None]
    gate = jnp.tanh(attn_gate)
    wq_t = w_query[0].T
    block = make_block(
        tile_counts.reshape(4), tiles, lat_query, w_out[0], wq_t, w_key[0], w_value[0]
    )
    parts = [over_dp(block, 1, k) for k in (1, 2, 3)]
    low, high = jnp.stack([block, parts[0]]), jnp.stack(parts[1:])
    low1, high3 = over_dp(low, 2, 1), over_dp(high, 2, 3)
    high1, low3 = over_dp(high, 2, 1), over_dp(low, 2, 3)
    low2, high2 = over_dp(low1, 2, 1), over_dp(high3, 2, 3)
    mine = [low, high, low1, high1, low3, high3]
    others = over_core(mine)
    last2, mine, others, normed, up1, rinv1, gain1, meta = lax.optimization_barrier(
        ([low2, high2], mine, others, normed, up1, rinv1, gain1, meta)
    )
    others = others[:4] + over_core(last2) + others[4:]
    blocks = mine[:4] + last2 + mine[4:] + others
    wq_t, _ = lax.optimization_barrier((wq_t, last2))
    wq1 = lax.ppermute(wq_t, "segment", [(1, 0)])

    q_send, o_send, wq_got, wo_got = project(1, BF, meta, normed, up1, blocks)
    q_got = lax.ppermute(q_send, X, SWAP_MP)
    o_got = lax.ppermute(o_send, X, LAST_SWAP)
    meta, wq1, o_send = lax.optimization_barrier((meta, wq1, o_send))
    wq1 = lax.all_gather(wq1, DP, axis=0, tiled=True)
    kv = select(wanted, meta, blocks)
    normed, kv = lax.optimization_barrier((normed, kv))
    q_own, o_own, wq_own, wo_own = project(0, F32, meta, normed, up1, blocks)
    probs = forward(meta, q_own, q_got, kv)
    dq1, dkv1 = backward(meta, gate, q_own, q_got, o_own, o_got, kv, probs)
    dqs = [lax.ppermute(dq1, X, LAST_TO_SAME), lax.ppermute(dq1, X, LAST_TO_CROSS)]
    own1, *terms = latent_terms(
        ((1, 3), (2,)), dkv1, w_key[0], w_value[0], jnp.zeros((192, E), BF)
    )
    dqs, terms = lax.optimization_barrier((dqs, terms))
    up, o_send = back(meta, rinv1, gain1, dqs, cotangent, h_all, [wq1], wo_got)
    o_got = lax.ppermute(o_send, X, FIRST_SWAP)
    o_own = dot(up, wo_own, NT).astype(BF)
    dq_cross, o_own = lax.optimization_barrier((dqs[1], o_own))
    got1 = lax.ppermute(dq_cross, X, FIRST_TO_SAME)
    pair = lax.ppermute(terms[0], X, LAST_TO_SAME)
    got = [pair[:192], lax.ppermute(terms[1], X, LAST_TO_CROSS)]
    relayed = pair[192:]
    o_got, got, relayed = lax.optimization_barrier((o_got, got, relayed))

    dq0, dkv0 = backward(meta, gate, q_own, q_got, o_own, o_got, kv, probs)
    dkv0, got1 = lax.optimization_barrier((dkv0, got1))
    own0, *terms = latent_terms(((1,), (2,), (3,)), dkv0, w_key[0], w_value[0], relayed)
    got0 = lax.ppermute(dq0, X, FIRST_SWAP)
    moves = (FIRST_TO_SAME, FIRST_TO_CROSS, FIRST_SWAP)
    late = [lax.ppermute(t, X, p) for t, p in zip(terms, moves)]
    got, got0 = lax.optimization_barrier((got, got0))
    received = jnp.where(last, own1, own0)
    for term in got:
        received = received + term.astype(F32)
    (grads,) = back(meta, rinv, gain, [dq1, dq0, got1, got0], up, h, [wq_own, wq_got])
    latent_grad, late = lax.optimization_barrier((received, late))
    for term in late:
        latent_grad = latent_grad + term.astype(F32)
    return grads[None], latent_grad.reshape(reports, 48, E)


def solution(mesh):
    fine = Mesh(mesh.devices.reshape(2, 4, 4, 2, 2), ("segment", "z", "y", "core", "mp"))
    return jax.shard_map(
        per_device,
        mesh=fine,
        in_specs=(
            P("segment", DP, "mp"),
            P(DP, "mp"),
            P(DP),
            P("segment", "mp"),
            P("segment"),
            P("segment", "mp", DP),
            P("segment", DP, "mp"),
            P("segment", None, "mp"),
            P("segment", None, "mp"),
            P(DP, None, None),
            P(DP, None),
            P(),
            P(),
            P(),
            P(DP, None, None),
        ),
        out_specs=(P("segment", DP, "mp"), P(DP, X, None)),
        check_vma=False,
    )
```

```python
import functools

import jax
import jax.numpy as jnp
from jax import lax
from jax.experimental import pallas as pl
from jax.experimental.pallas import tpu as pltpu
from jax.sharding import Mesh
from jax.sharding import PartitionSpec as P

MODEL_WIDTH = 4096
E = 1536
HEAD = 128
LAT = 32
SPR = 6
L = 128
QBLK = 32
MAXT = 64
SCALE = HEAD ** (-0.5)
DP = ("z", "y", "core")
X = ("segment", "mp")
BF = jnp.bfloat16
F32 = jnp.float32
LIMIT = 64 * 1024 * 1024
NT = (((1,), (1,)), ((), ()))
NN = (((1,), (0,)), ((), ()))
TN = (((0,), (0,)), ((), ()))

SWAP_MP = [(0, 1), (1, 0), (2, 3), (3, 2)]
LAST_TO_SAME = [(2, 0), (3, 1)]
LAST_TO_CROSS = [(2, 1), (3, 0)]
LAST_SWAP = [(2, 3), (3, 2)]
FIRST_TO_SAME = [(0, 2), (1, 3)]
FIRST_TO_CROSS = [(0, 3), (1, 2)]
FIRST_SWAP = [(0, 1), (1, 0)]


def yz_perm(stage, k):
    pairs = []
    for z in range(4):
        for y in range(4):
            for core in range(2):
                along_y = (core == 0) == (stage == 1)
                to_z = z if along_y else (z + k) % 4
                to_y = (y + k) % 4 if along_y else y
                pairs.append(((z * 4 + y) * 2 + core, (to_z * 4 + to_y) * 2 + core))
    return pairs


def dot(a, b, dims):
    return lax.dot_general(a, b, dims, preferred_element_type=F32)


def params(**kwargs):
    return pltpu.CompilerParams(vmem_limit_bytes=LIMIT, **kwargs)


def whole(shape):
    return pl.BlockSpec(shape, lambda *_: (0,) * len(shape))


SMEM = pl.BlockSpec(memory_space=pltpu.SMEM)
ANY = pl.BlockSpec(memory_space=pl.ANY)
VMEM = pl.BlockSpec(memory_space=pltpu.VMEM)
TILE = 512
SMALL = pl.CostEstimate(flops=1, bytes_accessed=1, transcendentals=0)
ROWS, SLOT, INFO, LENGTHS, PATTERN, PICKS = 0, 32, 36, 39, 43, 139


def block_kernel(counts, tiles, queries, w_out, w_query, w_key, w_value, out, w_v, latents, sems):
    loads = [
        pltpu.make_async_copy(w, w_v.at[i], sems.at[i]) for i, w in enumerate((w_key, w_value))
    ]
    for load in loads:
        load.start()
    out[:32] = w_out[...]
    out[32:64] = w_query[...]
    heads = [slice(head * HEAD, (head + 1) * HEAD) for head in range(E // HEAD)]
    slot = lax.broadcasted_iota(jnp.int32, (LAT, MAXT), 1)
    for slide in range(tiles.shape[0]):
        tile = [tiles[slide, :, cols] for cols in heads]
        query = [queries[:, cols] for cols in heads]
        scores = [dot(q, t, NT) * SCALE for q, t in zip(query, tile)]
        scores = [jnp.where(slot < counts[slide], x, -1e30) for x in scores]
        exps = [jnp.exp(s - jnp.max(s, axis=1, keepdims=True)) for s in scores]
        weights = [(e / jnp.sum(e, axis=1, keepdims=True)).astype(BF) for e in exps]
        pooled = [dot(w, t, NN) for w, t in zip(weights, tile)]
        for cols, q, p in zip(heads, query, pooled):
            latents[slide * LAT : (slide + 1) * LAT, cols] = (q.astype(F32) + p).astype(BF)
    for i, load in enumerate(loads):
        load.wait()
        value = dot(latents[...], w_v[i], NN).astype(BF)
        half = value.shape[1]
        for slide in range(tiles.shape[0]):
            at = 64 + slide // 2 * LAT
            col = (slide % 2 * 2 + i) * half
            out[at : at + LAT, col : col + half] = value[slide * LAT : (slide + 1) * LAT]


def make_block(counts, tiles, queries, w_out, w_query, w_key, w_value):
    slides = tiles.shape[0]
    return pl.pallas_call(
        block_kernel,
        in_specs=[SMEM] + [VMEM] * 4 + [ANY] * 2,
        out_specs=VMEM,
        out_shape=jax.ShapeDtypeStruct((64 + slides // 2 * LAT, w_out.shape[1]), BF),
        scratch_shapes=[
            pltpu.VMEM((2,) + w_key.shape, BF),
            pltpu.VMEM((slides * LAT, E), BF),
            pltpu.SemaphoreType.DMA((2,)),
        ],
        compiler_params=params(),
        cost_estimate=SMALL,
    )(counts, tiles, queries, w_out, w_query, w_key, w_value)


def over_dp(array, stage, k):
    return lax.ppermute(array, DP, yz_perm(stage, k))


def over_core(arrays):
    return [lax.ppermute(a, "core", [(0, 1), (1, 0)]) for a in arrays]


def places(z, y, core):
    table = []
    for a in range(8):
        c = core if a < 4 else 1 - core
        for k in range(4):
            j = a % 4
            at_z = lax.rem(z - jnp.where(c == 0, j, k) + 4, 4)
            at_y = lax.rem(y - jnp.where(c == 0, k, j) + 4, 4)
            table.append((at_z * 4 + at_y) * 2 + c)
    return jnp.stack(table).astype(jnp.int32)


def column(row):
    return jnp.broadcast_to(row, (HEAD, row.shape[1])).T[:, :1]


def live_tokens(meta, tokens):
    index = lax.broadcasted_iota(jnp.int32, (tokens, 1), 0)
    parts = [index[r * L : (r + 1) * L] < r * L + meta[LENGTHS + r] for r in range(tokens // L)]
    return jnp.concatenate([p.astype(F32) for p in parts], axis=0) > 0


def project_kernel(part, meta, normed, upstream, *refs):
    ins, outs, weights, (w_v, x_v, sems) = refs[:16], refs[16:18], refs[18:20], refs[20:]
    half = w_v.shape[1]

    def load(i, x):
        pltpu.make_async_copy(x, x_v.at[i], sems.at[2 * i]).start()
        for a in range(16):
            for k in range(2):
                at = pl.multiple_of(meta[ROWS + a * 2 + k] - part * half, 32)

                @pl.when((at >= 0) & (at < half))
                def _():
                    pltpu.make_async_copy(
                        ins[a].at[k, pl.ds((1 - i) * 32, 32)],
                        w_v.at[i, pl.ds(at, 32)],
                        sems.at[2 * i + 1],
                    ).start()

    load(0, normed)
    stores = []
    for i in range(2):
        pltpu.make_async_copy(x_v.at[i], x_v.at[i], sems.at[2 * i]).wait()
        pltpu.make_async_copy(w_v.at[i], w_v.at[i], sems.at[2 * i + 1]).wait()
        if i == 0:
            load(1, upstream)
        stores.append(pltpu.make_async_copy(w_v.at[i], weights[i], sems.at[2 * i + 1]))
        stores[i].start()
        outs[i][...] = dot(x_v[i], w_v[i], NT).astype(outs[i].dtype)
    for store in stores:
        store.wait()


def project(part, dtype, meta, normed, upstream, blocks):
    tokens, width = normed.shape
    half = 512
    return pl.pallas_call(
        functools.partial(project_kernel, part),
        in_specs=[SMEM] + [ANY] * 18,
        out_specs=[VMEM, VMEM, ANY, ANY],
        out_shape=[
            jax.ShapeDtypeStruct((tokens, half), dtype),
            jax.ShapeDtypeStruct((tokens, half), BF),
            jax.ShapeDtypeStruct((half, width), BF),
            jax.ShapeDtypeStruct((half, width), BF),
        ],
        scratch_shapes=[
            pltpu.VMEM((2, half, width), BF),
            pltpu.VMEM((2, tokens, width), BF),
            pltpu.SemaphoreType.DMA((4,)),
        ],
        compiler_params=params(),
        cost_estimate=SMALL,
    )(meta, normed, upstream, *blocks)


def select_kernel(wanted, meta, *refs):
    ins, out, sems = refs[:16], refs[16], refs[17]
    width = out.shape[1]
    for i in range(wanted):
        array = meta[PICKS + i]
        block = meta[PICKS + wanted + i]
        slide = meta[PICKS + 2 * wanted + i]
        rows = pl.ds(pl.multiple_of(64 + slide // 2 * LAT, LAT), LAT)
        cols = pl.ds(pl.multiple_of(slide % 2 * width, width), width)
        for group in range(4):

            @pl.when(array // 4 == group)
            def _():
                for a in range(group * 4, group * 4 + 4):

                    @pl.when(array == a)
                    def _():
                        pltpu.make_async_copy(
                            ins[a].at[block, rows, cols], out.at[pl.ds(i * LAT, LAT)], sems.at[0]
                        ).start()

    pltpu.make_async_copy(out, out, sems.at[0]).wait()


def select(wanted, meta, blocks):
    return pl.pallas_call(
        functools.partial(select_kernel, wanted),
        in_specs=[SMEM] + [ANY] * 16,
        out_specs=VMEM,
        out_shape=jax.ShapeDtypeStruct((wanted * LAT, 1024), BF),
        scratch_shapes=[pltpu.SemaphoreType.DMA((1,))],
        compiler_params=params(),
        cost_estimate=SMALL,
    )(meta, *blocks)


def forward_kernel(meta, q_own, q_got, kv, probs):
    report = pl.program_id(0)
    span = kv.shape[0]
    slide = lax.broadcasted_iota(jnp.int32, (QBLK, span), 1) // LAT
    masks = []
    for block in range(L // QBLK):
        seen = jnp.zeros((QBLK, span), jnp.int32)
        for j in range(SPR):
            at = PATTERN + (report * (L // QBLK) + block) * SPR + j
            seen = jnp.where(slide == j, meta[at], seen)
        masks.append(seen)
    mask = jnp.concatenate(masks, axis=0) == 1
    heads = [slice(head * HEAD, (head + 1) * HEAD) for head in range(probs.shape[0])]
    qb = [(q_own[:, c] + q_got[:, c].astype(F32)).astype(BF) for c in heads]
    scores = [dot(q, kv[:, c], NT) * SCALE for q, c in zip(qb, heads)]
    scores = [jnp.where(mask, s, -1e30) for s in scores]
    exps = [jnp.exp(s - jnp.max(s, axis=1, keepdims=True)) for s in scores]
    totals = [jnp.sum(e, axis=1, keepdims=True) for e in exps]
    for head, (e, total) in enumerate(zip(exps, totals)):
        probs[head] = e / total


def forward(meta, q_own, q_got, kv):
    tokens, local = q_own.shape
    reports = tokens // L
    span = kv.shape[0] // reports
    heads = local // HEAD
    token = pl.BlockSpec((L, local), lambda i: (i, 0))
    return pl.pallas_call(
        forward_kernel,
        grid=(reports,),
        in_specs=[SMEM, token, token, pl.BlockSpec((span, local), lambda i: (i, 0))],
        out_specs=pl.BlockSpec((heads, L, span), lambda i: (0, i, 0)),
        out_shape=jax.ShapeDtypeStruct((heads, tokens, span), F32),
        compiler_params=params(),
        cost_estimate=SMALL,
    )(meta, q_own, q_got, kv)


def backward_kernel(meta, gate, q_own, q_got, o_own, o_got, keys, vals, probs, dq_out, dkv_out):
    report = pl.program_id(0)
    rows = pl.ds(pl.multiple_of(report * L, L), L)
    local = q_own.shape[1]
    heads = [slice(head * HEAD, (head + 1) * HEAD) for head in range(local // HEAD)]
    og = [
        (gate[0] * (o_own[:, c].astype(F32) + o_got[:, c].astype(F32))).astype(BF) for c in heads
    ]
    dprob = [dot(g, vals[:, c], NT) for g, c in zip(og, heads)]
    prob = [probs[head] for head in range(len(heads))]
    rowdot = [jnp.sum(p * d, axis=1, keepdims=True) for p, d in zip(prob, dprob)]
    dscore = [(p * (d - r)).astype(BF) for p, d, r in zip(prob, dprob, rowdot)]
    dq = [(dot(d, keys[:, c], NN) * SCALE).astype(BF) for d, c in zip(dscore, heads)]
    q = [q_own[:, c] + q_got[:, c].astype(F32) for c in heads]
    dkey = [(dot(d, x.astype(BF), TN) * SCALE).astype(BF) for d, x in zip(dscore, q)]
    dval = [dot(p.astype(BF), g, TN).astype(BF) for p, g in zip(prob, og)]
    stat = jnp.zeros((L, HEAD), F32)
    for c, d, x in zip(heads, dq, q):
        dq_out[rows, c] = d
        stat += x * d.astype(F32)
    into = pl.ds(pl.multiple_of(report * 48, 16), 48)
    both = jnp.concatenate(dkey + dval, axis=1)
    for part in range(4):
        dkv_out[meta[SLOT + part], into, :] = both[part * 48 : (part + 1) * 48]
    total = jnp.sum(stat.T, axis=0, keepdims=True)
    high = total.astype(BF)
    rest = total - high.astype(F32)
    low = rest.astype(BF)
    lower = (rest - low.astype(F32)).astype(BF)
    zero = jnp.zeros((13, L), F32)
    extra = jnp.concatenate([high.astype(F32), low.astype(F32), lower.astype(F32), zero], axis=0)
    dq_out[4 * L : 4 * L + 16, rows] = extra.astype(BF)


def backward(meta, gate, q_own, q_got, o_own, o_got, kv, probs):
    tokens, local = q_own.shape
    reports = tokens // L
    heads, _, span = probs.shape
    token = pl.BlockSpec((L, local), lambda i: (i, 0))
    return pl.pallas_call(
        backward_kernel,
        grid=(reports,),
        in_specs=[SMEM, SMEM, token, token, token, token]
        + [
            pl.BlockSpec((span, local), lambda i: (i, 0)),
            pl.BlockSpec((span, local), lambda i: (i, 1)),
            pl.BlockSpec((heads, L, span), lambda i: (0, i, 0)),
        ],
        out_specs=[whole((tokens + 16, local)), whole((4, reports * 48, 2 * local))],
        out_shape=[
            jax.ShapeDtypeStruct((tokens + 16, local), BF),
            jax.ShapeDtypeStruct((4, reports * 48, 2 * local), BF),
        ],
        compiler_params=params(),
        cost_estimate=SMALL,
    )(meta, gate, q_own, q_got, o_own, o_got, kv, kv, probs)


def back_kernel(following, meta, rinv, gain, *refs):
    if following:
        dq_own, dq_got, up, h, wq, wo, grad, o_send, wq_v, up_v, h_v, wo_v, sems = refs
        left, right = dq_own[...], dq_got[...]
    else:
        dq1, dq0, got1, got0, up, h, wq_own, wq_got, grad, wq_v, up_v, h_v, sems = refs
        left = jnp.where(meta[INFO] == 1, dq1[...].astype(F32), dq0[...].astype(F32)).astype(BF)
        right = (got1[...].astype(F32) + got0[...].astype(F32)).astype(BF)
    if len(h.shape) == 3:
        h = h.at[1]
    inner, width = wq_v.shape
    half = inner // 2
    tokens = up_v.shape[0]
    tiles = width // TILE

    def copies(tile):
        cols = slice(tile * TILE, (tile + 1) * TILE)
        out = []
        for part in range(2):
            into = wq_v.at[part * half : (part + 1) * half, cols]
            if following:
                at = pl.multiple_of(meta[INFO + 1 + part], half)
                out.append((wq.at[pl.ds(at, half), cols], into))
            else:
                out.append(((wq_own, wq_got)[part].at[:, cols], into))
        out.append((up.at[:, cols], up_v.at[:, cols]))
        out.append((h.at[:, cols], h_v.at[:, cols]))
        return [
            pltpu.make_async_copy(a, b, sems.at[tile * 4 + i]) for i, (a, b) in enumerate(out)
        ]

    for tile in range(2):
        for copy in copies(tile):
            copy.start()
    if following:
        load = pltpu.make_async_copy(wo, wo_v, sems.at[tiles * 4])
    stat = column(
        jnp.sum(left[tokens:].astype(F32) + right[tokens:].astype(F32), axis=0, keepdims=True)
    )
    dq = jnp.concatenate([left[:tokens], right[:tokens]], axis=1)
    scale = column(rinv[...])
    share = scale * scale * stat / MODEL_WIDTH
    if following:
        live = live_tokens(meta, tokens)
    stores = []
    for tile in range(tiles):
        for copy in copies(tile):
            copy.wait()
        if tile + 2 < tiles:
            for copy in copies(tile + 2):
                copy.start()
        elif following and tile + 2 == tiles:
            load.start()
        cols = slice(tile * TILE, (tile + 1) * TILE)
        dnormed = dot(dq, wq_v[:, cols], NN)
        upstream = up_v[:, cols].astype(F32)
        if following:
            upstream = jnp.where(live, upstream, 0.0)
        value = upstream + (scale * (gain[:, cols] * dnormed) - h_v[:, cols].astype(F32) * share)
        if following:
            value = jnp.where(meta[INFO] == 1, upstream, value)
        up_v[:, cols] = value.astype(BF)
        store = pltpu.make_async_copy(up_v.at[:, cols], grad.at[:, cols], sems.at[tile * 4])
        store.start()
        stores.append(store)
    if following:
        load.wait()
        o_send[...] = dot(up_v[...], wo_v[...], NT).astype(BF)
    for store in stores:
        store.wait()


def back(meta, rinv, gain, dqs, up, h, weights, wo=None):
    tokens, width = up.shape
    half = dqs[0].shape[1]
    inner = 2 * half
    inputs = [meta, rinv, gain, *dqs, up, h, *weights]
    in_specs = [SMEM] + [VMEM] * (2 + len(dqs)) + [ANY] * (2 + len(weights))
    out_specs = [ANY]
    out_shape = [jax.ShapeDtypeStruct((tokens, width), BF)]
    scratch = [pltpu.VMEM((inner, width), BF)] + [pltpu.VMEM((tokens, width), BF)] * 2
    if wo is not None:
        inputs.append(wo)
        in_specs.append(ANY)
        out_specs.append(VMEM)
        out_shape.append(jax.ShapeDtypeStruct((tokens, half), BF))
        scratch.append(pltpu.VMEM((half, width), BF))
    return pl.pallas_call(
        functools.partial(back_kernel, wo is not None),
        in_specs=in_specs,
        out_specs=out_specs,
        out_shape=out_shape,
        scratch_shapes=scratch + [pltpu.SemaphoreType.DMA((width // TILE * 4 + 1,))],
        compiler_params=params(),
        cost_estimate=SMALL,
    )(*inputs)


def term_kernel(dkv, w_key, w_value, own, *terms):
    rows = own.shape[0]
    both = dkv[...].reshape(4 * rows, dkv.shape[2])
    half = w_key.shape[1]
    value = dot(both[:, :half], w_key[...], NT) + dot(both[:, half:], w_value[...], NT)
    own[...] = value[:rows]
    for k, term in enumerate(terms, 1):
        term[...] = value[k * rows : (k + 1) * rows].astype(BF)


def latent_terms(dkv, w_key, w_value):
    rows, inner = dkv.shape[1:]
    features = w_key.shape[0]
    tile = features // 3
    weight = pl.BlockSpec((tile, w_key.shape[1]), lambda i: (i, 0))
    result = pl.BlockSpec((rows, tile), lambda i: (0, i))
    return pl.pallas_call(
        term_kernel,
        grid=(features // tile,),
        in_specs=[whole(dkv.shape), weight, weight],
        out_specs=[result] * 4,
        out_shape=[jax.ShapeDtypeStruct((rows, features), t) for t in (F32, BF, BF, BF)],
        compiler_params=params(),
        cost_estimate=SMALL,
    )(dkv, w_key, w_value)


def per_device(
    segment_inputs,
    cotangent,
    report_lengths,
    norm_gain,
    attn_gate,
    w_query,
    w_out,
    w_key,
    w_value,
    tiles,
    tile_counts,
    lat_query,
    request_source,
    request_slide,
    cross_pattern,
):
    z, y, core = (lax.axis_index(name) for name in DP)
    me_dp = (z * 4 + y) * 2 + core
    me_mp = lax.axis_index("mp")
    seg = lax.axis_index("segment")
    last = seg == 1
    reports = cross_pattern.shape[0]
    wanted = reports * SPR
    h = segment_inputs[0]
    tokens, width = h.shape
    half = 512

    slot = []
    for part in range(4):
        same_seg, same_mp = seg == part // 2, me_mp == part % 2
        slot.append(jnp.where(same_seg, jnp.where(same_mp, 0, 3), jnp.where(same_mp, 1, 2)))
    rows = lax.rem(places(z, y, core) * 32 - me_mp * half + 2 * half, 2 * half)
    info = [seg, me_mp * half, (1 - me_mp) * half]
    source = lax.dynamic_index_in_dim(
        request_source.reshape(32, wanted), me_dp, 0, keepdims=False
    )
    slide = lax.dynamic_index_in_dim(request_slide.reshape(32, wanted), me_dp, 0, keepdims=False)
    source_core = source % 2
    far_z = lax.rem(z - source // 8 + 4, 4)
    far_y = lax.rem(y - source // 2 % 4 + 4, 4)
    first = jnp.where(source_core == 0, far_y, far_z)
    second = jnp.where(source_core == 0, far_z, far_y)
    array = 2 * second + first // 2 + jnp.where(source_core == core, 0, 8)
    first = first % 2
    meta = jnp.concatenate(
        [rows, jnp.stack(slot + info).astype(jnp.int32), report_lengths]
        + [cross_pattern.reshape(-1), array, first, slide]
    )

    h_all = lax.all_gather(segment_inputs, "segment", axis=0, tiled=True)

    h32 = h.astype(F32)
    partial = jnp.sum(h32 * h32, axis=1)
    squares = partial + lax.ppermute(partial, "mp", [(0, 1), (1, 0)])
    rinv = lax.rsqrt(squares / MODEL_WIDTH + 1e-05)
    gain = norm_gain
    message = lax.ppermute(jnp.concatenate([rinv, gain[0]]), "segment", [(1, 0)])[None]
    rinv1, gain1 = message[:, :tokens], message[:, tokens:]
    normed = (h32 * rinv[:, None] * gain).astype(BF)
    position = jnp.arange(tokens)
    live = position % L < jnp.repeat(report_lengths, L)
    up1 = jnp.where(live[:, None], cotangent, jnp.zeros((), BF))
    rinv = rinv[None]
    gate = jnp.tanh(attn_gate)
    wq_t = w_query[0].T
    block = make_block(
        tile_counts.reshape(4), tiles, lat_query, w_out[0], wq_t, w_key[0], w_value[0]
    )
    parts = [over_dp(block, 1, k) for k in (1, 2, 3)]
    wq1 = lax.ppermute(wq_t, "segment", [(1, 0)])
    parts, wq1, rinv, rinv1, gain1 = lax.optimization_barrier((parts, wq1, rinv, rinv1, gain1))
    low, high = jnp.stack([block, parts[0]]), jnp.stack(parts[1:])
    low1, high3 = over_dp(low, 2, 1), over_dp(high, 2, 3)
    high1, low3 = over_dp(high, 2, 1), over_dp(low, 2, 3)
    others = over_core([low, high])
    low1, high3, others = lax.optimization_barrier((low1, high3, others))
    low2, high2 = over_dp(low1, 2, 1), over_dp(high3, 2, 3)
    mine = [low, high, low1, high1, low3, high3]
    others += over_core(mine[2:])
    last2, mine, others, normed, up1, meta = lax.optimization_barrier(
        ([low2, high2], mine, others, normed, up1, meta)
    )
    others = others[:4] + over_core(last2) + others[4:]
    blocks = mine[:4] + last2 + mine[4:] + others
    wq1, _ = lax.optimization_barrier((wq1, last2))
    wq1 = lax.all_gather(wq1, DP, axis=0, tiled=True)

    q_send, o_send, wq_got, wo_got = project(1, BF, meta, normed, up1, blocks)
    q_got = lax.ppermute(q_send, X, SWAP_MP)
    o_got = lax.ppermute(o_send, X, LAST_SWAP)
    meta, o_send = lax.optimization_barrier((meta, o_send))
    kv = select(wanted, meta, blocks)
    normed, kv = lax.optimization_barrier((normed, kv))
    q_own, o_own, wq_own, wo_own = project(0, F32, meta, normed, up1, blocks)
    probs = forward(meta, q_own, q_got, kv)
    dq1, dkv1 = backward(meta, gate, q_own, q_got, o_own, o_got, kv, probs)
    dqs = [lax.ppermute(dq1, X, LAST_TO_SAME), lax.ppermute(dq1, X, LAST_TO_CROSS)]
    own1, *terms = latent_terms(dkv1, w_key[0], w_value[0])
    got1 = lax.ppermute(dq1, X, LAST_SWAP)
    moves = (LAST_SWAP, LAST_TO_CROSS, LAST_TO_SAME)
    got = [lax.ppermute(t, X, p) for t, p in zip(terms[::-1], moves)]
    dqs, own1 = lax.optimization_barrier((dqs, own1))
    up, o_send = back(meta, rinv1, gain1, dqs, cotangent, h_all, [wq1], wo_got)
    o_send, got1 = lax.optimization_barrier((o_send, got1))
    o_got = lax.ppermute(o_send, X, FIRST_SWAP)
    o_own = dot(up, wo_own, NT).astype(BF)
    o_got, got[:2] = lax.optimization_barrier((o_got, got[:2]))

    dq0, dkv0 = backward(meta, gate, q_own, q_got, o_own, o_got, kv, probs)
    own0, *terms = latent_terms(dkv0, w_key[0], w_value[0])
    got0 = lax.ppermute(dq0, X, FIRST_SWAP)
    terms, got = lax.optimization_barrier((terms, got))
    moves = (FIRST_SWAP, FIRST_TO_CROSS, FIRST_TO_SAME)
    late = [lax.ppermute(t, X, p) for t, p in zip(terms[::-1], moves)]
    got, got0 = lax.optimization_barrier((got, got0))
    received = jnp.where(last, own1, own0)
    for term in got:
        received = received + term.astype(F32)
    (grads,) = back(meta, rinv, gain, [dq1, dq0, got1, got0], up, h, [wq_own, wq_got])
    latent_grad, late = lax.optimization_barrier((received, late))
    for term in late:
        latent_grad = latent_grad + term.astype(F32)
    return grads[None], latent_grad.reshape(reports, 48, E)


def solution(mesh):
    fine = Mesh(mesh.devices.reshape(2, 4, 4, 2, 2), ("segment", "z", "y", "core", "mp"))
    return jax.shard_map(
        per_device,
        mesh=fine,
        in_specs=(
            P("segment", DP, "mp"),
            P(DP, "mp"),
            P(DP),
            P("segment", "mp"),
            P("segment"),
            P("segment", "mp", DP),
            P("segment", DP, "mp"),
            P("segment", None, "mp"),
            P("segment", None, "mp"),
            P(DP, None, None),
            P(DP, None),
            P(),
            P(),
            P(),
            P(DP, None, None),
        ),
        out_specs=(P("segment", DP, "mp"), P(DP, X, None)),
        check_vma=False,
    )
```

```python
import functools

import jax
import jax.numpy as jnp
from jax import lax
from jax.experimental import pallas as pl
from jax.experimental.pallas import tpu as pltpu
from jax.sharding import Mesh
from jax.sharding import PartitionSpec as P

MODEL_WIDTH = 4096
E = 1536
HEAD = 128
LAT = 32
SPR = 6
L = 128
QBLK = 32
MAXT = 64
SCALE = HEAD ** (-0.5)
DP = ("z", "y", "core")
X = ("segment", "mp")
BF = jnp.bfloat16
F32 = jnp.float32
LIMIT = 64 * 1024 * 1024
NT = (((1,), (1,)), ((), ()))
NN = (((1,), (0,)), ((), ()))
TN = (((0,), (0,)), ((), ()))

SWAP_MP = [(0, 1), (1, 0), (2, 3), (3, 2)]
LAST_TO_SAME = [(2, 0), (3, 1)]
LAST_TO_CROSS = [(2, 1), (3, 0)]
LAST_SWAP = [(2, 3), (3, 2)]
FIRST_TO_SAME = [(0, 2), (1, 3)]
FIRST_TO_CROSS = [(0, 3), (1, 2)]
FIRST_SWAP = [(0, 1), (1, 0)]


def yz_perm(stage, k):
    pairs = []
    for z in range(4):
        for y in range(4):
            for core in range(2):
                along_y = (core == 0) == (stage == 1)
                to_z = z if along_y else (z + k) % 4
                to_y = (y + k) % 4 if along_y else y
                pairs.append(((z * 4 + y) * 2 + core, (to_z * 4 + to_y) * 2 + core))
    return pairs


def dot(a, b, dims):
    return lax.dot_general(a, b, dims, preferred_element_type=F32)


def params(**kwargs):
    return pltpu.CompilerParams(vmem_limit_bytes=LIMIT, **kwargs)


def whole(shape):
    return pl.BlockSpec(shape, lambda *_: (0,) * len(shape))


SMEM = pl.BlockSpec(memory_space=pltpu.SMEM)
ANY = pl.BlockSpec(memory_space=pl.ANY)
VMEM = pl.BlockSpec(memory_space=pltpu.VMEM)
TILE = 512
SMALL = pl.CostEstimate(flops=1, bytes_accessed=1, transcendentals=0)
ROWS, SLOT, INFO, LENGTHS, PATTERN, PICKS = 0, 32, 36, 39, 43, 139


def block_kernel(counts, tiles, queries, w_out, w_query, w_key, w_value, out, w_v, latents, sems):
    loads = [
        pltpu.make_async_copy(w, w_v.at[i], sems.at[i]) for i, w in enumerate((w_key, w_value))
    ]
    for load in loads:
        load.start()
    out[:32] = w_out[...]
    out[32:64] = w_query[...]
    heads = [slice(head * HEAD, (head + 1) * HEAD) for head in range(E // HEAD)]
    slot = lax.broadcasted_iota(jnp.int32, (LAT, MAXT), 1)
    for slide in range(tiles.shape[0]):
        tile = [tiles[slide, :, cols] for cols in heads]
        query = [queries[:, cols] for cols in heads]
        scores = [dot(q, t, NT) * SCALE for q, t in zip(query, tile)]
        scores = [jnp.where(slot < counts[slide], x, -1e30) for x in scores]
        exps = [jnp.exp(s - jnp.max(s, axis=1, keepdims=True)) for s in scores]
        weights = [(e / jnp.sum(e, axis=1, keepdims=True)).astype(BF) for e in exps]
        pooled = [dot(w, t, NN) for w, t in zip(weights, tile)]
        for cols, q, p in zip(heads, query, pooled):
            latents[slide * LAT : (slide + 1) * LAT, cols] = (q.astype(F32) + p).astype(BF)
    for i, load in enumerate(loads):
        load.wait()
        value = dot(latents[...], w_v[i], NN).astype(BF)
        half = value.shape[1]
        for slide in range(tiles.shape[0]):
            at = 64 + slide // 2 * LAT
            col = (slide % 2 * 2 + i) * half
            out[at : at + LAT, col : col + half] = value[slide * LAT : (slide + 1) * LAT]


def make_block(counts, tiles, queries, w_out, w_query, w_key, w_value):
    slides = tiles.shape[0]
    return pl.pallas_call(
        block_kernel,
        in_specs=[SMEM] + [VMEM] * 4 + [ANY] * 2,
        out_specs=VMEM,
        out_shape=jax.ShapeDtypeStruct((64 + slides // 2 * LAT, w_out.shape[1]), BF),
        scratch_shapes=[
            pltpu.VMEM((2,) + w_key.shape, BF),
            pltpu.VMEM((slides * LAT, E), BF),
            pltpu.SemaphoreType.DMA((2,)),
        ],
        compiler_params=params(),
        cost_estimate=SMALL,
    )(counts, tiles, queries, w_out, w_query, w_key, w_value)


def over_dp(array, stage, k):
    return lax.ppermute(array, DP, yz_perm(stage, k))


def over_core(arrays):
    return [lax.ppermute(a, "core", [(0, 1), (1, 0)]) for a in arrays]


def places(z, y, core):
    table = []
    for a in range(8):
        c = core if a < 4 else 1 - core
        for k in range(4):
            j = a % 4
            at_z = lax.rem(z - jnp.where(c == 0, j, k) + 4, 4)
            at_y = lax.rem(y - jnp.where(c == 0, k, j) + 4, 4)
            table.append((at_z * 4 + at_y) * 2 + c)
    return jnp.stack(table).astype(jnp.int32)


def column(row):
    return jnp.broadcast_to(row, (HEAD, row.shape[1])).T[:, :1]


def live_tokens(meta, tokens):
    index = lax.broadcasted_iota(jnp.int32, (tokens, 1), 0)
    parts = [index[r * L : (r + 1) * L] < r * L + meta[LENGTHS + r] for r in range(tokens // L)]
    return jnp.concatenate([p.astype(F32) for p in parts], axis=0) > 0


def project_kernel(part, meta, normed, upstream, *refs):
    ins, outs, weights, (w_v, x_v, sems) = refs[:16], refs[16:18], refs[18:20], refs[20:]
    half = w_v.shape[1]

    def load(i, x):
        pltpu.make_async_copy(x, x_v.at[i], sems.at[2 * i]).start()
        for a in range(16):
            for k in range(2):
                at = pl.multiple_of(meta[ROWS + a * 2 + k] - part * half, 32)

                @pl.when((at >= 0) & (at < half))
                def _():
                    pltpu.make_async_copy(
                        ins[a].at[k, pl.ds((1 - i) * 32, 32)],
                        w_v.at[i, pl.ds(at, 32)],
                        sems.at[2 * i + 1],
                    ).start()

    load(0, normed)
    stores = []
    for i in range(2):
        pltpu.make_async_copy(x_v.at[i], x_v.at[i], sems.at[2 * i]).wait()
        pltpu.make_async_copy(w_v.at[i], w_v.at[i], sems.at[2 * i + 1]).wait()
        if i == 0:
            load(1, upstream)
        stores.append(pltpu.make_async_copy(w_v.at[i], weights[i], sems.at[2 * i + 1]))
        stores[i].start()
        outs[i][...] = dot(x_v[i], w_v[i], NT).astype(outs[i].dtype)
    for store in stores:
        store.wait()


def project(part, dtype, meta, normed, upstream, blocks):
    tokens, width = normed.shape
    half = 512
    return pl.pallas_call(
        functools.partial(project_kernel, part),
        in_specs=[SMEM] + [ANY] * 18,
        out_specs=[VMEM, VMEM, ANY, ANY],
        out_shape=[
            jax.ShapeDtypeStruct((tokens, half), dtype),
            jax.ShapeDtypeStruct((tokens, half), BF),
            jax.ShapeDtypeStruct((half, width), BF),
            jax.ShapeDtypeStruct((half, width), BF),
        ],
        scratch_shapes=[
            pltpu.VMEM((2, half, width), BF),
            pltpu.VMEM((2, tokens, width), BF),
            pltpu.SemaphoreType.DMA((4,)),
        ],
        compiler_params=params(),
        cost_estimate=SMALL,
    )(meta, normed, upstream, *blocks)


def select_kernel(wanted, meta, *refs):
    ins, out, sems = refs[:16], refs[16], refs[17]
    width = out.shape[1]
    for i in range(wanted):
        array = meta[PICKS + i]
        block = meta[PICKS + wanted + i]
        slide = meta[PICKS + 2 * wanted + i]
        rows = pl.ds(pl.multiple_of(64 + slide // 2 * LAT, LAT), LAT)
        cols = pl.ds(pl.multiple_of(slide % 2 * width, width), width)
        for group in range(4):

            @pl.when(array // 4 == group)
            def _():
                for a in range(group * 4, group * 4 + 4):

                    @pl.when(array == a)
                    def _():
                        pltpu.make_async_copy(
                            ins[a].at[block, rows, cols], out.at[pl.ds(i * LAT, LAT)], sems.at[0]
                        ).start()

    pltpu.make_async_copy(out, out, sems.at[0]).wait()


def select(wanted, meta, blocks):
    return pl.pallas_call(
        functools.partial(select_kernel, wanted),
        in_specs=[SMEM] + [ANY] * 16,
        out_specs=VMEM,
        out_shape=jax.ShapeDtypeStruct((wanted * LAT, 1024), BF),
        scratch_shapes=[pltpu.SemaphoreType.DMA((1,))],
        compiler_params=params(),
        cost_estimate=SMALL,
    )(meta, *blocks)


def forward_kernel(meta, q_own, q_got, kv, probs):
    report = pl.program_id(0)
    span = kv.shape[0]
    slide = lax.broadcasted_iota(jnp.int32, (QBLK, span), 1) // LAT
    masks = []
    for block in range(L // QBLK):
        seen = jnp.zeros((QBLK, span), jnp.int32)
        for j in range(SPR):
            at = PATTERN + (report * (L // QBLK) + block) * SPR + j
            seen = jnp.where(slide == j, meta[at], seen)
        masks.append(seen)
    mask = jnp.concatenate(masks, axis=0) == 1
    heads = [slice(head * HEAD, (head + 1) * HEAD) for head in range(probs.shape[0])]
    qb = [(q_own[:, c] + q_got[:, c].astype(F32)).astype(BF) for c in heads]
    scores = [dot(q, kv[:, c], NT) * SCALE for q, c in zip(qb, heads)]
    scores = [jnp.where(mask, s, -1e30) for s in scores]
    exps = [jnp.exp(s - jnp.max(s, axis=1, keepdims=True)) for s in scores]
    totals = [jnp.sum(e, axis=1, keepdims=True) for e in exps]
    for head, (e, total) in enumerate(zip(exps, totals)):
        probs[head] = e / total


def forward(meta, q_own, q_got, kv):
    tokens, local = q_own.shape
    reports = tokens // L
    span = kv.shape[0] // reports
    heads = local // HEAD
    token = pl.BlockSpec((L, local), lambda i: (i, 0))
    return pl.pallas_call(
        forward_kernel,
        grid=(reports,),
        in_specs=[SMEM, token, token, pl.BlockSpec((span, local), lambda i: (i, 0))],
        out_specs=pl.BlockSpec((heads, L, span), lambda i: (0, i, 0)),
        out_shape=jax.ShapeDtypeStruct((heads, tokens, span), F32),
        compiler_params=params(),
        cost_estimate=SMALL,
    )(meta, q_own, q_got, kv)


def backward_kernel(meta, gate, q_own, q_got, o_own, o_got, keys, vals, probs, dq_out, dkv_out):
    report = pl.program_id(0)
    rows = pl.ds(pl.multiple_of(report * L, L), L)
    local = q_own.shape[1]
    heads = [slice(head * HEAD, (head + 1) * HEAD) for head in range(local // HEAD)]
    og = [
        (gate[0] * (o_own[:, c].astype(F32) + o_got[:, c].astype(F32))).astype(BF) for c in heads
    ]
    dprob = [dot(g, vals[:, c], NT) for g, c in zip(og, heads)]
    prob = [probs[head] for head in range(len(heads))]
    rowdot = [jnp.sum(p * d, axis=1, keepdims=True) for p, d in zip(prob, dprob)]
    dscore = [(p * (d - r)).astype(BF) for p, d, r in zip(prob, dprob, rowdot)]
    dq = [(dot(d, keys[:, c], NN) * SCALE).astype(BF) for d, c in zip(dscore, heads)]
    q = [q_own[:, c] + q_got[:, c].astype(F32) for c in heads]
    dkey = [(dot(d, x.astype(BF), TN) * SCALE).astype(BF) for d, x in zip(dscore, q)]
    dval = [dot(p.astype(BF), g, TN).astype(BF) for p, g in zip(prob, og)]
    stat = jnp.zeros((L, HEAD), F32)
    for c, d, x in zip(heads, dq, q):
        dq_out[rows, c] = d
        stat += x * d.astype(F32)
    into = pl.ds(pl.multiple_of(report * 48, 16), 48)
    both = jnp.concatenate(dkey + dval, axis=1)
    for part in range(4):
        dkv_out[meta[SLOT + part], into, :] = both[part * 48 : (part + 1) * 48]
    total = jnp.sum(stat.T, axis=0, keepdims=True)
    high = total.astype(BF)
    rest = total - high.astype(F32)
    low = rest.astype(BF)
    lower = (rest - low.astype(F32)).astype(BF)
    zero = jnp.zeros((13, L), F32)
    extra = jnp.concatenate([high.astype(F32), low.astype(F32), lower.astype(F32), zero], axis=0)
    dq_out[4 * L : 4 * L + 16, rows] = extra.astype(BF)


def backward(meta, gate, q_own, q_got, o_own, o_got, kv, probs):
    tokens, local = q_own.shape
    reports = tokens // L
    heads, _, span = probs.shape
    token = pl.BlockSpec((L, local), lambda i: (i, 0))
    return pl.pallas_call(
        backward_kernel,
        grid=(reports,),
        in_specs=[SMEM, SMEM, token, token, token, token]
        + [
            pl.BlockSpec((span, local), lambda i: (i, 0)),
            pl.BlockSpec((span, local), lambda i: (i, 1)),
            pl.BlockSpec((heads, L, span), lambda i: (0, i, 0)),
        ],
        out_specs=[whole((tokens + 16, local)), whole((4, reports * 48, 2 * local))],
        out_shape=[
            jax.ShapeDtypeStruct((tokens + 16, local), BF),
            jax.ShapeDtypeStruct((4, reports * 48, 2 * local), BF),
        ],
        compiler_params=params(),
        cost_estimate=SMALL,
    )(meta, gate, q_own, q_got, o_own, o_got, kv, kv, probs)


def back_kernel(following, meta, rinv, gain, *refs):
    if following:
        dq_own, dq_got, up, h, wq, wo, grad, o_send, wq_v, up_v, h_v, wo_v, sems = refs
        left, right = dq_own[...], dq_got[...]
    else:
        dq1, dq0, got1, got0, up, h, wq_own, wq_got, grad, wq_v, up_v, h_v, sems = refs
        left = jnp.where(meta[INFO] == 1, dq1[...].astype(F32), dq0[...].astype(F32)).astype(BF)
        right = (got1[...].astype(F32) + got0[...].astype(F32)).astype(BF)
    if len(h.shape) == 3:
        h = h.at[1]
    inner, width = wq_v.shape
    half = inner // 2
    tokens = up_v.shape[0]
    tiles = width // TILE

    def copies(tile):
        cols = slice(tile * TILE, (tile + 1) * TILE)
        out = []
        for part in range(2):
            into = wq_v.at[part * half : (part + 1) * half, cols]
            if following:
                at = pl.multiple_of(meta[INFO + 1 + part], half)
                out.append((wq.at[pl.ds(at, half), cols], into))
            else:
                out.append(((wq_own, wq_got)[part].at[:, cols], into))
        out.append((up.at[:, cols], up_v.at[:, cols]))
        out.append((h.at[:, cols], h_v.at[:, cols]))
        return [
            pltpu.make_async_copy(a, b, sems.at[tile * 4 + i]) for i, (a, b) in enumerate(out)
        ]

    for tile in range(2):
        for copy in copies(tile):
            copy.start()
    if following:
        load = pltpu.make_async_copy(wo, wo_v, sems.at[tiles * 4])
    stat = column(
        jnp.sum(left[tokens:].astype(F32) + right[tokens:].astype(F32), axis=0, keepdims=True)
    )
    dq = jnp.concatenate([left[:tokens], right[:tokens]], axis=1)
    scale = column(rinv[...])
    share = scale * scale * stat / MODEL_WIDTH
    if following:
        live = live_tokens(meta, tokens)
    stores = []
    for tile in range(tiles):
        for copy in copies(tile):
            copy.wait()
        if tile + 2 < tiles:
            for copy in copies(tile + 2):
                copy.start()
        elif following and tile + 2 == tiles:
            load.start()
        cols = slice(tile * TILE, (tile + 1) * TILE)
        dnormed = dot(dq, wq_v[:, cols], NN)
        upstream = up_v[:, cols].astype(F32)
        if following:
            upstream = jnp.where(live, upstream, 0.0)
        value = upstream + (scale * (gain[:, cols] * dnormed) - h_v[:, cols].astype(F32) * share)
        if following:
            value = jnp.where(meta[INFO] == 1, upstream, value)
        up_v[:, cols] = value.astype(BF)
        store = pltpu.make_async_copy(up_v.at[:, cols], grad.at[:, cols], sems.at[tile * 4])
        store.start()
        stores.append(store)
    if following:
        load.wait()
        o_send[...] = dot(up_v[...], wo_v[...], NT).astype(BF)
    for store in stores:
        store.wait()


def back(meta, rinv, gain, dqs, up, h, weights, wo=None):
    tokens, width = up.shape
    half = dqs[0].shape[1]
    inner = 2 * half
    inputs = [meta, rinv, gain, *dqs, up, h, *weights]
    in_specs = [SMEM] + [VMEM] * (2 + len(dqs)) + [ANY] * (2 + len(weights))
    out_specs = [ANY]
    out_shape = [jax.ShapeDtypeStruct((tokens, width), BF)]
    scratch = [pltpu.VMEM((inner, width), BF)] + [pltpu.VMEM((tokens, width), BF)] * 2
    if wo is not None:
        inputs.append(wo)
        in_specs.append(ANY)
        out_specs.append(VMEM)
        out_shape.append(jax.ShapeDtypeStruct((tokens, half), BF))
        scratch.append(pltpu.VMEM((half, width), BF))
    return pl.pallas_call(
        functools.partial(back_kernel, wo is not None),
        in_specs=in_specs,
        out_specs=out_specs,
        out_shape=out_shape,
        scratch_shapes=scratch + [pltpu.SemaphoreType.DMA((width // TILE * 4 + 1,))],
        compiler_params=params(),
        cost_estimate=SMALL,
    )(*inputs)


def term_kernel(dkv, w_key, w_value, own, *terms):
    rows = own.shape[0]
    both = dkv[...].reshape(4 * rows, dkv.shape[2])
    half = w_key.shape[1]
    value = dot(both[:, :half], w_key[...], NT) + dot(both[:, half:], w_value[...], NT)
    own[...] = value[:rows]
    for k, term in enumerate(terms, 1):
        term[...] = value[k * rows : (k + 1) * rows].astype(BF)


def latent_terms(dkv, w_key, w_value):
    rows, inner = dkv.shape[1:]
    features = w_key.shape[0]
    tile = features // 3
    weight = pl.BlockSpec((tile, w_key.shape[1]), lambda i: (i, 0))
    result = pl.BlockSpec((rows, tile), lambda i: (0, i))
    return pl.pallas_call(
        term_kernel,
        grid=(features // tile,),
        in_specs=[whole(dkv.shape), weight, weight],
        out_specs=[result] * 4,
        out_shape=[jax.ShapeDtypeStruct((rows, features), t) for t in (F32, BF, BF, BF)],
        compiler_params=params(),
        cost_estimate=SMALL,
    )(dkv, w_key, w_value)


def per_device(
    segment_inputs,
    cotangent,
    report_lengths,
    norm_gain,
    attn_gate,
    w_query,
    w_out,
    w_key,
    w_value,
    tiles,
    tile_counts,
    lat_query,
    request_source,
    request_slide,
    cross_pattern,
):
    z, y, core = (lax.axis_index(name) for name in DP)
    me_dp = (z * 4 + y) * 2 + core
    me_mp = lax.axis_index("mp")
    seg = lax.axis_index("segment")
    last = seg == 1
    reports = cross_pattern.shape[0]
    wanted = reports * SPR
    h = segment_inputs[0]
    tokens, width = h.shape
    half = 512

    slot = []
    for part in range(4):
        same_seg, same_mp = seg == part // 2, me_mp == part % 2
        slot.append(jnp.where(same_seg, jnp.where(same_mp, 0, 3), jnp.where(same_mp, 1, 2)))
    rows = lax.rem(places(z, y, core) * 32 - me_mp * half + 2 * half, 2 * half)
    info = [seg, me_mp * half, (1 - me_mp) * half]
    source = lax.dynamic_index_in_dim(
        request_source.reshape(32, wanted), me_dp, 0, keepdims=False
    )
    slide = lax.dynamic_index_in_dim(request_slide.reshape(32, wanted), me_dp, 0, keepdims=False)
    source_core = source % 2
    far_z = lax.rem(z - source // 8 + 4, 4)
    far_y = lax.rem(y - source // 2 % 4 + 4, 4)
    first = jnp.where(source_core == 0, far_y, far_z)
    second = jnp.where(source_core == 0, far_z, far_y)
    array = 2 * second + first // 2 + jnp.where(source_core == core, 0, 8)
    first = first % 2
    meta = jnp.concatenate(
        [rows, jnp.stack(slot + info).astype(jnp.int32), report_lengths]
        + [cross_pattern.reshape(-1), array, first, slide]
    )

    h_all = lax.all_gather(segment_inputs, "segment", axis=0, tiled=True)

    h32 = h.astype(F32)
    partial = jnp.sum(h32 * h32, axis=1)
    squares = partial + lax.ppermute(partial, "mp", [(0, 1), (1, 0)])
    rinv = lax.rsqrt(squares / MODEL_WIDTH + 1e-05)
    gain = norm_gain
    message = lax.ppermute(jnp.concatenate([rinv, gain[0]]), "segment", [(1, 0)])[None]
    rinv1, gain1 = message[:, :tokens], message[:, tokens:]
    normed = (h32 * rinv[:, None] * gain).astype(BF)
    position = jnp.arange(tokens)
    live = position % L < jnp.repeat(report_lengths, L)
    up1 = jnp.where(live[:, None], cotangent, jnp.zeros((), BF))
    rinv = rinv[None]
    gate = jnp.tanh(attn_gate)
    wq_t = w_query[0].T
    block = make_block(
        tile_counts.reshape(4), tiles, lat_query, w_out[0], wq_t, w_key[0], w_value[0]
    )
    parts = [over_dp(block, 1, k) for k in (1, 2, 3)]
    wq1 = lax.ppermute(wq_t, "segment", [(1, 0)])
    low = jnp.stack([block, parts[0]])
    parts[1:], wq1, rinv, rinv1, gain1 = lax.optimization_barrier(
        (parts[1:], wq1, rinv, rinv1, gain1)
    )
    high = jnp.stack(parts[1:])
    low1, high3 = over_dp(low, 2, 1), over_dp(high, 2, 3)
    high1, low3 = over_dp(high, 2, 1), over_dp(low, 2, 3)
    others = over_core([low, high])
    low1, high3, others = lax.optimization_barrier((low1, high3, others))
    low2, high2 = over_dp(low1, 2, 1), over_dp(high3, 2, 3)
    mine = [low, high, low1, high1, low3, high3]
    others += over_core(mine[2:])
    last2, mine, others, normed, up1, meta = lax.optimization_barrier(
        ([low2, high2], mine, others, normed, up1, meta)
    )
    others = others[:4] + over_core(last2) + others[4:]
    blocks = mine[:4] + last2 + mine[4:] + others
    wq1, _ = lax.optimization_barrier((wq1, last2))
    wq1 = lax.all_gather(wq1, DP, axis=0, tiled=True)

    q_send, o_send, wq_got, wo_got = project(1, BF, meta, normed, up1, blocks)
    q_got = lax.ppermute(q_send, X, SWAP_MP)
    o_got = lax.ppermute(o_send, X, LAST_SWAP)
    meta, o_send = lax.optimization_barrier((meta, o_send))
    kv = select(wanted, meta, blocks)
    normed, kv = lax.optimization_barrier((normed, kv))
    q_own, o_own, wq_own, wo_own = project(0, F32, meta, normed, up1, blocks)
    probs = forward(meta, q_own, q_got, kv)
    dq1, dkv1 = backward(meta, gate, q_own, q_got, o_own, o_got, kv, probs)
    dqs = [lax.ppermute(dq1, X, LAST_TO_SAME), lax.ppermute(dq1, X, LAST_TO_CROSS)]
    own1, *terms = latent_terms(dkv1, w_key[0], w_value[0])
    got1 = lax.ppermute(dq1, X, LAST_SWAP)
    moves = (LAST_TO_SAME, LAST_TO_CROSS, LAST_SWAP)
    got = [lax.ppermute(t, X, p) for t, p in zip(terms, moves)]
    dqs, own1 = lax.optimization_barrier((dqs, own1))
    up, o_send = back(meta, rinv1, gain1, dqs, cotangent, h_all, [wq1], wo_got)
    o_send, got1 = lax.optimization_barrier((o_send, got1))
    o_got = lax.ppermute(o_send, X, FIRST_SWAP)
    o_own = dot(up, wo_own, NT).astype(BF)
    o_got, got[:2] = lax.optimization_barrier((o_got, got[:2]))

    dq0, dkv0 = backward(meta, gate, q_own, q_got, o_own, o_got, kv, probs)
    own0, *terms = latent_terms(dkv0, w_key[0], w_value[0])
    got0 = lax.ppermute(dq0, X, FIRST_SWAP)
    terms, got = lax.optimization_barrier((terms, got))
    moves = (FIRST_SWAP, FIRST_TO_CROSS, FIRST_TO_SAME)
    late = [lax.ppermute(t, X, p) for t, p in zip(terms[::-1], moves)]
    got, got0 = lax.optimization_barrier((got, got0))
    received = jnp.where(last, own1, own0)
    for term in got:
        received = received + term.astype(F32)
    (grads,) = back(meta, rinv, gain, [dq1, dq0, got1, got0], up, h, [wq_own, wq_got])
    latent_grad, late = lax.optimization_barrier((received, late))
    for term in late:
        latent_grad = latent_grad + term.astype(F32)
    return grads[None], latent_grad.reshape(reports, 48, E)


def solution(mesh):
    fine = Mesh(mesh.devices.reshape(2, 4, 4, 2, 2), ("segment", "z", "y", "core", "mp"))
    return jax.shard_map(
        per_device,
        mesh=fine,
        in_specs=(
            P("segment", DP, "mp"),
            P(DP, "mp"),
            P(DP),
            P("segment", "mp"),
            P("segment"),
            P("segment", "mp", DP),
            P("segment", DP, "mp"),
            P("segment", None, "mp"),
            P("segment", None, "mp"),
            P(DP, None, None),
            P(DP, None),
            P(),
            P(),
            P(),
            P(DP, None, None),
        ),
        out_specs=(P("segment", DP, "mp"), P(DP, X, None)),
        check_vma=False,
    )
```

```python
import functools

import jax
import jax.numpy as jnp
from jax import lax
from jax.experimental import pallas as pl
from jax.experimental.pallas import tpu as pltpu
from jax.sharding import Mesh
from jax.sharding import PartitionSpec as P

MODEL_WIDTH = 4096
E = 1536
HEAD = 128
LAT = 32
SPR = 6
L = 128
QBLK = 32
MAXT = 64
SCALE = HEAD ** (-0.5)
DP = ("z", "y", "core")
X = ("segment", "mp")
BF = jnp.bfloat16
F32 = jnp.float32
LIMIT = 64 * 1024 * 1024
NT = (((1,), (1,)), ((), ()))
NN = (((1,), (0,)), ((), ()))
TN = (((0,), (0,)), ((), ()))

SWAP_MP = [(0, 1), (1, 0), (2, 3), (3, 2)]
LAST_TO_SAME = [(2, 0), (3, 1)]
LAST_TO_CROSS = [(2, 1), (3, 0)]
LAST_SWAP = [(2, 3), (3, 2)]
FIRST_TO_SAME = [(0, 2), (1, 3)]
FIRST_TO_CROSS = [(0, 3), (1, 2)]
FIRST_SWAP = [(0, 1), (1, 0)]


def yz_perm(stage, k):
    pairs = []
    for z in range(4):
        for y in range(4):
            for core in range(2):
                along_y = (core == 0) == (stage == 1)
                to_z = z if along_y else (z + k) % 4
                to_y = (y + k) % 4 if along_y else y
                pairs.append(((z * 4 + y) * 2 + core, (to_z * 4 + to_y) * 2 + core))
    return pairs


def dot(a, b, dims):
    return lax.dot_general(a, b, dims, preferred_element_type=F32)


def params(**kwargs):
    return pltpu.CompilerParams(vmem_limit_bytes=LIMIT, **kwargs)


def whole(shape):
    return pl.BlockSpec(shape, lambda *_: (0,) * len(shape))


SMEM = pl.BlockSpec(memory_space=pltpu.SMEM)
ANY = pl.BlockSpec(memory_space=pl.ANY)
VMEM = pl.BlockSpec(memory_space=pltpu.VMEM)
TILE = 512
SMALL = pl.CostEstimate(flops=1, bytes_accessed=1, transcendentals=0)
ROWS, SLOT, INFO, LENGTHS, PATTERN, PICKS = 0, 32, 36, 39, 43, 139


def block_kernel(counts, tiles, queries, w_out, w_query, w_key, w_value, out, w_v, latents, sems):
    loads = [
        pltpu.make_async_copy(w, w_v.at[i], sems.at[i]) for i, w in enumerate((w_key, w_value))
    ]
    for load in loads:
        load.start()
    out[:32] = w_out[...]
    out[32:64] = w_query[...]
    heads = [slice(head * HEAD, (head + 1) * HEAD) for head in range(E // HEAD)]
    slot = lax.broadcasted_iota(jnp.int32, (LAT, MAXT), 1)
    for slide in range(tiles.shape[0]):
        tile = [tiles[slide, :, cols] for cols in heads]
        query = [queries[:, cols] for cols in heads]
        scores = [dot(q, t, NT) * SCALE for q, t in zip(query, tile)]
        scores = [jnp.where(slot < counts[slide], x, -1e30) for x in scores]
        exps = [jnp.exp(s - jnp.max(s, axis=1, keepdims=True)) for s in scores]
        weights = [(e / jnp.sum(e, axis=1, keepdims=True)).astype(BF) for e in exps]
        pooled = [dot(w, t, NN) for w, t in zip(weights, tile)]
        for cols, q, p in zip(heads, query, pooled):
            latents[slide * LAT : (slide + 1) * LAT, cols] = (q.astype(F32) + p).astype(BF)
    for i, load in enumerate(loads):
        load.wait()
        value = dot(latents[...], w_v[i], NN).astype(BF)
        half = value.shape[1]
        for slide in range(tiles.shape[0]):
            at = 64 + slide // 2 * LAT
            col = (slide % 2 * 2 + i) * half
            out[at : at + LAT, col : col + half] = value[slide * LAT : (slide + 1) * LAT]


def make_block(counts, tiles, queries, w_out, w_query, w_key, w_value):
    slides = tiles.shape[0]
    return pl.pallas_call(
        block_kernel,
        in_specs=[SMEM] + [VMEM] * 4 + [ANY] * 2,
        out_specs=VMEM,
        out_shape=jax.ShapeDtypeStruct((64 + slides // 2 * LAT, w_out.shape[1]), BF),
        scratch_shapes=[
            pltpu.VMEM((2,) + w_key.shape, BF),
            pltpu.VMEM((slides * LAT, E), BF),
            pltpu.SemaphoreType.DMA((2,)),
        ],
        compiler_params=params(),
        cost_estimate=SMALL,
    )(counts, tiles, queries, w_out, w_query, w_key, w_value)


def over_dp(array, stage, k):
    return lax.ppermute(array, DP, yz_perm(stage, k))


def over_core(arrays):
    return [lax.ppermute(a, "core", [(0, 1), (1, 0)]) for a in arrays]


def places(z, y, core):
    table = []
    for a in range(8):
        c = core if a < 4 else 1 - core
        for k in range(4):
            j = a % 4
            at_z = lax.rem(z - jnp.where(c == 0, j, k) + 4, 4)
            at_y = lax.rem(y - jnp.where(c == 0, k, j) + 4, 4)
            table.append((at_z * 4 + at_y) * 2 + c)
    return jnp.stack(table).astype(jnp.int32)


def column(row):
    return jnp.broadcast_to(row, (HEAD, row.shape[1])).T[:, :1]


def live_tokens(meta, tokens):
    index = lax.broadcasted_iota(jnp.int32, (tokens, 1), 0)
    parts = [index[r * L : (r + 1) * L] < r * L + meta[LENGTHS + r] for r in range(tokens // L)]
    return jnp.concatenate([p.astype(F32) for p in parts], axis=0) > 0


def project_kernel(part, meta, normed, upstream, *refs):
    ins, outs, weights, (w_v, x_v, sems) = refs[:16], refs[16:18], refs[18:20], refs[20:]
    half = w_v.shape[1]

    def load(i, x):
        pltpu.make_async_copy(x, x_v.at[i], sems.at[2 * i]).start()
        for a in range(16):
            for k in range(2):
                at = pl.multiple_of(meta[ROWS + a * 2 + k] - part * half, 32)

                @pl.when((at >= 0) & (at < half))
                def _():
                    pltpu.make_async_copy(
                        ins[a].at[k, pl.ds((1 - i) * 32, 32)],
                        w_v.at[i, pl.ds(at, 32)],
                        sems.at[2 * i + 1],
                    ).start()

    load(0, normed)
    stores = []
    for i in range(2):
        pltpu.make_async_copy(x_v.at[i], x_v.at[i], sems.at[2 * i]).wait()
        pltpu.make_async_copy(w_v.at[i], w_v.at[i], sems.at[2 * i + 1]).wait()
        if i == 0:
            load(1, upstream)
        stores.append(pltpu.make_async_copy(w_v.at[i], weights[i], sems.at[2 * i + 1]))
        stores[i].start()
        outs[i][...] = dot(x_v[i], w_v[i], NT).astype(outs[i].dtype)
    for store in stores:
        store.wait()


def project(part, dtype, meta, normed, upstream, blocks):
    tokens, width = normed.shape
    half = 512
    return pl.pallas_call(
        functools.partial(project_kernel, part),
        in_specs=[SMEM] + [ANY] * 18,
        out_specs=[VMEM, VMEM, ANY, ANY],
        out_shape=[
            jax.ShapeDtypeStruct((tokens, half), dtype),
            jax.ShapeDtypeStruct((tokens, half), BF),
            jax.ShapeDtypeStruct((half, width), BF),
            jax.ShapeDtypeStruct((half, width), BF),
        ],
        scratch_shapes=[
            pltpu.VMEM((2, half, width), BF),
            pltpu.VMEM((2, tokens, width), BF),
            pltpu.SemaphoreType.DMA((4,)),
        ],
        compiler_params=params(),
        cost_estimate=SMALL,
    )(meta, normed, upstream, *blocks)


def select_kernel(wanted, meta, *refs):
    ins, out, sems = refs[:16], refs[16], refs[17]
    width = out.shape[1]
    for i in range(wanted):
        array = meta[PICKS + i]
        block = meta[PICKS + wanted + i]
        slide = meta[PICKS + 2 * wanted + i]
        rows = pl.ds(pl.multiple_of(64 + slide // 2 * LAT, LAT), LAT)
        cols = pl.ds(pl.multiple_of(slide % 2 * width, width), width)
        for group in range(4):

            @pl.when(array // 4 == group)
            def _():
                for a in range(group * 4, group * 4 + 4):

                    @pl.when(array == a)
                    def _():
                        pltpu.make_async_copy(
                            ins[a].at[block, rows, cols], out.at[pl.ds(i * LAT, LAT)], sems.at[0]
                        ).start()

    pltpu.make_async_copy(out, out, sems.at[0]).wait()


def select(wanted, meta, blocks):
    return pl.pallas_call(
        functools.partial(select_kernel, wanted),
        in_specs=[SMEM] + [ANY] * 16,
        out_specs=VMEM,
        out_shape=jax.ShapeDtypeStruct((wanted * LAT, 1024), BF),
        scratch_shapes=[pltpu.SemaphoreType.DMA((1,))],
        compiler_params=params(),
        cost_estimate=SMALL,
    )(meta, *blocks)


def forward_kernel(meta, q_own, q_got, kv, probs):
    report = pl.program_id(0)
    span = kv.shape[0]
    slide = lax.broadcasted_iota(jnp.int32, (QBLK, span), 1) // LAT
    masks = []
    for block in range(L // QBLK):
        seen = jnp.zeros((QBLK, span), jnp.int32)
        for j in range(SPR):
            at = PATTERN + (report * (L // QBLK) + block) * SPR + j
            seen = jnp.where(slide == j, meta[at], seen)
        masks.append(seen)
    mask = jnp.concatenate(masks, axis=0) == 1
    heads = [slice(head * HEAD, (head + 1) * HEAD) for head in range(probs.shape[0])]
    qb = [(q_own[:, c] + q_got[:, c].astype(F32)).astype(BF) for c in heads]
    scores = [dot(q, kv[:, c], NT) * SCALE for q, c in zip(qb, heads)]
    scores = [jnp.where(mask, s, -1e30) for s in scores]
    exps = [jnp.exp(s - jnp.max(s, axis=1, keepdims=True)) for s in scores]
    totals = [jnp.sum(e, axis=1, keepdims=True) for e in exps]
    for head, (e, total) in enumerate(zip(exps, totals)):
        probs[head] = e / total


def forward(meta, q_own, q_got, kv):
    tokens, local = q_own.shape
    reports = tokens // L
    span = kv.shape[0] // reports
    heads = local // HEAD
    token = pl.BlockSpec((L, local), lambda i: (i, 0))
    return pl.pallas_call(
        forward_kernel,
        grid=(reports,),
        in_specs=[SMEM, token, token, pl.BlockSpec((span, local), lambda i: (i, 0))],
        out_specs=pl.BlockSpec((heads, L, span), lambda i: (0, i, 0)),
        out_shape=jax.ShapeDtypeStruct((heads, tokens, span), F32),
        compiler_params=params(),
        cost_estimate=SMALL,
    )(meta, q_own, q_got, kv)


def backward_kernel(meta, gate, q_own, q_got, o_own, o_got, keys, vals, probs, dq_out, dkv_out):
    report = pl.program_id(0)
    rows = pl.ds(pl.multiple_of(report * L, L), L)
    local = q_own.shape[1]
    heads = [slice(head * HEAD, (head + 1) * HEAD) for head in range(local // HEAD)]
    og = [
        (gate[0] * (o_own[:, c].astype(F32) + o_got[:, c].astype(F32))).astype(BF) for c in heads
    ]
    dprob = [dot(g, vals[:, c], NT) for g, c in zip(og, heads)]
    prob = [probs[head] for head in range(len(heads))]
    rowdot = [jnp.sum(p * d, axis=1, keepdims=True) for p, d in zip(prob, dprob)]
    dscore = [(p * (d - r)).astype(BF) for p, d, r in zip(prob, dprob, rowdot)]
    dq = [(dot(d, keys[:, c], NN) * SCALE).astype(BF) for d, c in zip(dscore, heads)]
    q = [q_own[:, c] + q_got[:, c].astype(F32) for c in heads]
    dkey = [(dot(d, x.astype(BF), TN) * SCALE).astype(BF) for d, x in zip(dscore, q)]
    dval = [dot(p.astype(BF), g, TN).astype(BF) for p, g in zip(prob, og)]
    stat = jnp.zeros((L, HEAD), F32)
    for c, d, x in zip(heads, dq, q):
        dq_out[rows, c] = d
        stat += x * d.astype(F32)
    into = pl.ds(pl.multiple_of(report * 48, 16), 48)
    both = jnp.concatenate(dkey + dval, axis=1)
    for part in range(4):
        dkv_out[meta[SLOT + part], into, :] = both[part * 48 : (part + 1) * 48]
    total = jnp.sum(stat.T, axis=0, keepdims=True)
    high = total.astype(BF)
    rest = total - high.astype(F32)
    low = rest.astype(BF)
    lower = (rest - low.astype(F32)).astype(BF)
    zero = jnp.zeros((13, L), F32)
    extra = jnp.concatenate([high.astype(F32), low.astype(F32), lower.astype(F32), zero], axis=0)
    dq_out[4 * L : 4 * L + 16, rows] = extra.astype(BF)


def backward(meta, gate, q_own, q_got, o_own, o_got, kv, probs):
    tokens, local = q_own.shape
    reports = tokens // L
    heads, _, span = probs.shape
    token = pl.BlockSpec((L, local), lambda i: (i, 0))
    return pl.pallas_call(
        backward_kernel,
        grid=(reports,),
        in_specs=[SMEM, SMEM, token, token, token, token]
        + [
            pl.BlockSpec((span, local), lambda i: (i, 0)),
            pl.BlockSpec((span, local), lambda i: (i, 1)),
            pl.BlockSpec((heads, L, span), lambda i: (0, i, 0)),
        ],
        out_specs=[whole((tokens + 16, local)), whole((4, reports * 48, 2 * local))],
        out_shape=[
            jax.ShapeDtypeStruct((tokens + 16, local), BF),
            jax.ShapeDtypeStruct((4, reports * 48, 2 * local), BF),
        ],
        compiler_params=params(),
        cost_estimate=SMALL,
    )(meta, gate, q_own, q_got, o_own, o_got, kv, kv, probs)


def back_kernel(following, meta, rinv, gain, *refs):
    if following:
        dq_own, dq_got, up, h, wq, wo, grad, o_send, wq_v, up_v, h_v, wo_v, sems = refs
        left, right = dq_own[...], dq_got[...]
    else:
        dq1, dq0, got1, got0, up, h, wq_own, wq_got, grad, wq_v, up_v, h_v, sems = refs
        left = jnp.where(meta[INFO] == 1, dq1[...].astype(F32), dq0[...].astype(F32)).astype(BF)
        right = (got1[...].astype(F32) + got0[...].astype(F32)).astype(BF)
    if len(h.shape) == 3:
        h = h.at[1]
    inner, width = wq_v.shape
    half = inner // 2
    tokens = up_v.shape[0]
    tiles = width // TILE

    def copies(tile):
        cols = slice(tile * TILE, (tile + 1) * TILE)
        out = []
        for part in range(2):
            into = wq_v.at[part * half : (part + 1) * half, cols]
            if following:
                at = pl.multiple_of(meta[INFO + 1 + part], half)
                out.append((wq.at[pl.ds(at, half), cols], into))
            else:
                out.append(((wq_own, wq_got)[part].at[:, cols], into))
        out.append((up.at[:, cols], up_v.at[:, cols]))
        out.append((h.at[:, cols], h_v.at[:, cols]))
        return [
            pltpu.make_async_copy(a, b, sems.at[tile * 4 + i]) for i, (a, b) in enumerate(out)
        ]

    for tile in range(2):
        for copy in copies(tile):
            copy.start()
    if following:
        load = pltpu.make_async_copy(wo, wo_v, sems.at[tiles * 4])
    stat = column(
        jnp.sum(left[tokens:].astype(F32) + right[tokens:].astype(F32), axis=0, keepdims=True)
    )
    dq = jnp.concatenate([left[:tokens], right[:tokens]], axis=1)
    scale = column(rinv[...])
    share = scale * scale * stat / MODEL_WIDTH
    if following:
        live = live_tokens(meta, tokens)
    stores = []
    for tile in range(tiles):
        for copy in copies(tile):
            copy.wait()
        if tile + 2 < tiles:
            for copy in copies(tile + 2):
                copy.start()
        elif following and tile + 2 == tiles:
            load.start()
        cols = slice(tile * TILE, (tile + 1) * TILE)
        dnormed = dot(dq, wq_v[:, cols], NN)
        upstream = up_v[:, cols].astype(F32)
        if following:
            upstream = jnp.where(live, upstream, 0.0)
        value = upstream + (scale * (gain[:, cols] * dnormed) - h_v[:, cols].astype(F32) * share)
        if following:
            value = jnp.where(meta[INFO] == 1, upstream, value)
        up_v[:, cols] = value.astype(BF)
        store = pltpu.make_async_copy(up_v.at[:, cols], grad.at[:, cols], sems.at[tile * 4])
        store.start()
        stores.append(store)
    if following:
        load.wait()
        o_send[...] = dot(up_v[...], wo_v[...], NT).astype(BF)
    for store in stores:
        store.wait()


def back(meta, rinv, gain, dqs, up, h, weights, wo=None):
    tokens, width = up.shape
    half = dqs[0].shape[1]
    inner = 2 * half
    inputs = [meta, rinv, gain, *dqs, up, h, *weights]
    in_specs = [SMEM] + [VMEM] * (2 + len(dqs)) + [ANY] * (2 + len(weights))
    out_specs = [ANY]
    out_shape = [jax.ShapeDtypeStruct((tokens, width), BF)]
    scratch = [pltpu.VMEM((inner, width), BF)] + [pltpu.VMEM((tokens, width), BF)] * 2
    if wo is not None:
        inputs.append(wo)
        in_specs.append(ANY)
        out_specs.append(VMEM)
        out_shape.append(jax.ShapeDtypeStruct((tokens, half), BF))
        scratch.append(pltpu.VMEM((half, width), BF))
    return pl.pallas_call(
        functools.partial(back_kernel, wo is not None),
        in_specs=in_specs,
        out_specs=out_specs,
        out_shape=out_shape,
        scratch_shapes=scratch + [pltpu.SemaphoreType.DMA((width // TILE * 4 + 1,))],
        compiler_params=params(),
        cost_estimate=SMALL,
    )(*inputs)


def term_kernel(dkv, w_key, w_value, own, *terms):
    rows = own.shape[0]
    both = dkv[...].reshape(4 * rows, dkv.shape[2])
    half = w_key.shape[1]
    value = dot(both[:, :half], w_key[...], NT) + dot(both[:, half:], w_value[...], NT)
    own[...] = value[:rows]
    for k, term in enumerate(terms, 1):
        term[...] = value[k * rows : (k + 1) * rows].astype(BF)


def latent_terms(dkv, w_key, w_value):
    rows, inner = dkv.shape[1:]
    features = w_key.shape[0]
    tile = features // 3
    weight = pl.BlockSpec((tile, w_key.shape[1]), lambda i: (i, 0))
    result = pl.BlockSpec((rows, tile), lambda i: (0, i))
    return pl.pallas_call(
        term_kernel,
        grid=(features // tile,),
        in_specs=[whole(dkv.shape), weight, weight],
        out_specs=[result] * 4,
        out_shape=[jax.ShapeDtypeStruct((rows, features), t) for t in (F32, BF, BF, BF)],
        compiler_params=params(),
        cost_estimate=SMALL,
    )(dkv, w_key, w_value)


def per_device(
    segment_inputs,
    cotangent,
    report_lengths,
    norm_gain,
    attn_gate,
    w_query,
    w_out,
    w_key,
    w_value,
    tiles,
    tile_counts,
    lat_query,
    request_source,
    request_slide,
    cross_pattern,
):
    z, y, core = (lax.axis_index(name) for name in DP)
    me_dp = (z * 4 + y) * 2 + core
    me_mp = lax.axis_index("mp")
    seg = lax.axis_index("segment")
    last = seg == 1
    reports = cross_pattern.shape[0]
    wanted = reports * SPR
    h = segment_inputs[0]
    tokens, width = h.shape
    half = 512

    slot = []
    for part in range(4):
        same_seg, same_mp = seg == part // 2, me_mp == part % 2
        slot.append(jnp.where(same_seg, jnp.where(same_mp, 0, 3), jnp.where(same_mp, 1, 2)))
    rows = lax.rem(places(z, y, core) * 32 - me_mp * half + 2 * half, 2 * half)
    info = [seg, me_mp * half, (1 - me_mp) * half]
    source = lax.dynamic_index_in_dim(
        request_source.reshape(32, wanted), me_dp, 0, keepdims=False
    )
    slide = lax.dynamic_index_in_dim(request_slide.reshape(32, wanted), me_dp, 0, keepdims=False)
    source_core = source % 2
    far_z = lax.rem(z - source // 8 + 4, 4)
    far_y = lax.rem(y - source // 2 % 4 + 4, 4)
    first = jnp.where(source_core == 0, far_y, far_z)
    second = jnp.where(source_core == 0, far_z, far_y)
    array = 2 * second + first // 2 + jnp.where(source_core == core, 0, 8)
    first = first % 2
    meta = jnp.concatenate(
        [rows, jnp.stack(slot + info).astype(jnp.int32), report_lengths]
        + [cross_pattern.reshape(-1), array, first, slide]
    )

    h_all = lax.all_gather(segment_inputs, "segment", axis=0, tiled=True)

    h32 = h.astype(F32)
    partial = jnp.sum(h32 * h32, axis=1)
    squares = partial + lax.ppermute(partial, "mp", [(0, 1), (1, 0)])
    rinv = lax.rsqrt(squares / MODEL_WIDTH + 1e-05)
    gain = norm_gain
    message = lax.ppermute(jnp.concatenate([rinv, gain[0]]), "segment", [(1, 0)])[None]
    rinv1, gain1 = message[:, :tokens], message[:, tokens:]
    normed = (h32 * rinv[:, None] * gain).astype(BF)
    position = jnp.arange(tokens)
    live = position % L < jnp.repeat(report_lengths, L)
    up1 = jnp.where(live[:, None], cotangent, jnp.zeros((), BF))
    rinv = rinv[None]
    gate = jnp.tanh(attn_gate)
    wq_t = w_query[0].T
    block = make_block(
        tile_counts.reshape(4), tiles, lat_query, w_out[0], wq_t, w_key[0], w_value[0]
    )
    parts = [over_dp(block, 1, k) for k in (1, 2, 3)]
    wq1 = lax.ppermute(wq_t, "segment", [(1, 0)])
    low = jnp.stack([block, parts[0]])
    parts[1:], wq1, rinv, rinv1, gain1 = lax.optimization_barrier(
        (parts[1:], wq1, rinv, rinv1, gain1)
    )
    high = jnp.stack(parts[1:])
    low1, high3 = over_dp(low, 2, 1), over_dp(high, 2, 3)
    high1, low3 = over_dp(high, 2, 1), over_dp(low, 2, 3)
    others = over_core([low, high])
    low1, high3, others = lax.optimization_barrier((low1, high3, others))
    low2, high2 = over_dp(low1, 2, 1), over_dp(high3, 2, 3)
    mine = [low, high, low1, high1, low3, high3]
    others += over_core(mine[2:])
    last2, mine, others, normed, up1, meta = lax.optimization_barrier(
        ([low2, high2], mine, others, normed, up1, meta)
    )
    others = others[:4] + over_core(last2) + others[4:]
    blocks = mine[:4] + last2 + mine[4:] + others
    wq1, _ = lax.optimization_barrier((wq1, last2))
    wq1 = lax.all_gather(wq1, DP, axis=0, tiled=True)

    q_send, o_send, wq_got, wo_got = project(1, BF, meta, normed, up1, blocks)
    q_got = lax.ppermute(q_send, X, SWAP_MP)
    o_got = lax.ppermute(o_send, X, LAST_SWAP)
    meta, o_send = lax.optimization_barrier((meta, o_send))
    kv = select(wanted, meta, blocks)
    normed, kv = lax.optimization_barrier((normed, kv))
    q_own, o_own, wq_own, wo_own = project(0, F32, meta, normed, up1, blocks)
    probs = forward(meta, q_own, q_got, kv)
    dq1, dkv1 = backward(meta, gate, q_own, q_got, o_own, o_got, kv, probs)
    dqs = [lax.ppermute(dq1, X, LAST_TO_SAME), lax.ppermute(dq1, X, LAST_TO_CROSS)]
    own1, *terms = latent_terms(dkv1, w_key[0], w_value[0])
    moves = (LAST_TO_SAME, LAST_TO_CROSS, LAST_SWAP)
    got = [lax.ppermute(t, X, p) for t, p in zip(terms, moves)]
    dqs, own1 = lax.optimization_barrier((dqs, own1))
    up, o_send = back(meta, rinv1, gain1, dqs, cotangent, h_all, [wq1], wo_got)
    o_got = lax.ppermute(o_send, X, FIRST_SWAP)
    o_own = dot(up, wo_own, NT).astype(BF)
    dq1, o_own = lax.optimization_barrier((dq1, o_own))
    got1 = lax.ppermute(dq1, X, LAST_SWAP)
    o_got, got[:2] = lax.optimization_barrier((o_got, got[:2]))

    dq0, dkv0 = backward(meta, gate, q_own, q_got, o_own, o_got, kv, probs)
    dkv0, got1 = lax.optimization_barrier((dkv0, got1))
    own0, *terms = latent_terms(dkv0, w_key[0], w_value[0])
    got0 = lax.ppermute(dq0, X, FIRST_SWAP)
    terms, got = lax.optimization_barrier((terms, got))
    moves = (FIRST_SWAP, FIRST_TO_CROSS, FIRST_TO_SAME)
    late = [lax.ppermute(t, X, p) for t, p in zip(terms[::-1], moves)]
    got, got0 = lax.optimization_barrier((got, got0))
    received = jnp.where(last, own1, own0)
    for term in got:
        received = received + term.astype(F32)
    (grads,) = back(meta, rinv, gain, [dq1, dq0, got1, got0], up, h, [wq_own, wq_got])
    latent_grad, late = lax.optimization_barrier((received, late))
    for term in late:
        latent_grad = latent_grad + term.astype(F32)
    return grads[None], latent_grad.reshape(reports, 48, E)


def solution(mesh):
    fine = Mesh(mesh.devices.reshape(2, 4, 4, 2, 2), ("segment", "z", "y", "core", "mp"))
    return jax.shard_map(
        per_device,
        mesh=fine,
        in_specs=(
            P("segment", DP, "mp"),
            P(DP, "mp"),
            P(DP),
            P("segment", "mp"),
            P("segment"),
            P("segment", "mp", DP),
            P("segment", DP, "mp"),
            P("segment", None, "mp"),
            P("segment", None, "mp"),
            P(DP, None, None),
            P(DP, None),
            P(),
            P(),
            P(),
            P(DP, None, None),
        ),
        out_specs=(P("segment", DP, "mp"), P(DP, X, None)),
        check_vma=False,
    )
```
